32 devices in a mesh: wide: 8 (over y, x, core), section: 4 (over z).
Axes of the slice: x: 2, y: 2, z: 4, core: 2. Of those that a mesh axis runs over, the one named last changes fastest.
Arguments:
- inputs: float32 [16, 64, 64, 512], P('wide', 'section'), may hold values from -6 to 6
- norm_gain: float32 [2, 2, 512], replicated, may hold values from 0.5 to 1.5
- norm_bias: float32 [2, 2, 512], replicated, may hold values from -2 to 2
- mix_weight: float32 [2, 2, 2, 4, 128, 128], replicated, may hold values from -0.375 to 0.375
- mix_bias: float32 [2, 2, 2, 4, 128], replicated, may hold values from -2 to 2
- up_weight: float32 [2, 512, 512], replicated, may hold values from -0.25 to 0.25
- up_bias: float32 [2, 512], replicated, may hold values from -2 to 2
- down_weight: float32 [2, 512, 512], replicated, may hold values from -0.25 to 0.25
- down_bias: float32 [2, 512], replicated, may hold values from -2 to 2
- out_grad: float32 [16, 64, 64, 512], P('wide', 'section'), may hold values from -6 to 6
Outputs:
- outputs: float32 [16, 64, 64, 512], P('wide', 'section')
- input_grad: float32 [16, 64, 64, 512], P('wide', 'section')
- gain_grad: float32 [2, 2, 512], replicated
- bias_grad: float32 [2, 2, 512], replicated
- mix_weight_grad: float32 [2, 2, 2, 4, 128, 128], replicated
- mix_bias_grad: float32 [2, 2, 2, 4, 128], replicated
- up_weight_grad: float32 [2, 512, 512], replicated
- up_bias_grad: float32 [2, 512], replicated
- down_weight_grad: float32 [2, 512, 512], replicated
- down_bias_grad: float32 [2, 512], replicated
The draws below stay inside these ranges and needn't reach their ends.
All inputs are finite; a program needn't handle non-finite values.
Results may differ from the reference program's by a relative error of at most 0.0002.
Values sent between devices are 32-bit elements; how exact they have to be, the bound alone decides.
No kernel may reach another device: no remote copies, remote signals or barrier semaphores. Data moves between devices by JAX's collectives and lax.ppermute only.
A program may use at most 320 MiB of HBM per device.

```python
import jax
import jax.numpy as jnp
from jax import lax

D = 512
FF = 512
BLOCKS = 4
GRID = 64
MODES = 32
BLOCK = 128
ITEMS = 16


def steps_of(rng, extent, shards, least, high):
    factor_of = 1.0
    for dim, shards_of in shards:
        heights = jax.random.uniform(jax.random.fold_in(jax.random.fold_in(rng, 6), dim), (shards_of,), jnp.float32, least / len(shards), high / len(shards))
        factor_of = factor_of * jnp.repeat(jnp.exp(heights), extent[dim] // shards_of).reshape((-1,) + (1,) * (len(extent) - 1 - dim))
    return factor_of


def bell_draw(stream_key, extent, spread, most, cuts=(), kind=jnp.bfloat16):
    gain = steps_of(stream_key, extent, cuts, -0.22, 0.18) if cuts else 1.0
    drawn = jax.random.normal(stream_key, extent, jnp.float32) * spread * gain
    return jnp.minimum(jnp.maximum(drawn, -most), most).astype(kind)


def setup_inputs(seed: int = 0) -> dict:
    splits = jax.random.split(jax.random.key(seed), 11)
    inputs = bell_draw(splits[0], (ITEMS, GRID, GRID, D), 1.0, 6.0, ((0, 8), (1, 4)), jnp.float32)
    norm_gain = jnp.clip(1.0 + 0.1 * jax.random.normal(splits[1], (2, 2, D), jnp.float32), 0.5, 1.5)
    norm_bias = bell_draw(splits[2], (2, 2, D), 0.3, 2.0, (), jnp.float32)
    mix_weight = bell_draw(splits[3], (2, 2, 2, BLOCKS, BLOCK, BLOCK), (2 * BLOCK) ** -0.5, 0.375, (), jnp.float32)
    mix_bias = bell_draw(splits[4], (2, 2, 2, BLOCKS, BLOCK), 0.3, 2.0, (), jnp.float32)
    up_weight = bell_draw(splits[5], (2, D, FF), D ** -0.5, 0.25, (), jnp.float32)
    up_bias = bell_draw(splits[6], (2, FF), 0.3, 2.0, (), jnp.float32)
    down_weight = bell_draw(splits[7], (2, FF, D), FF ** -0.5, 0.25, (), jnp.float32)
    down_bias = bell_draw(splits[8], (2, D), 0.3, 2.0, (), jnp.float32)
    out_grad = bell_draw(splits[9], (ITEMS, GRID, GRID, D), 1.0, 6.0, ((0, 8), (1, 4)), jnp.float32)
    return dict(inputs=inputs, norm_gain=norm_gain, norm_bias=norm_bias, mix_weight=mix_weight, mix_bias=mix_bias, up_weight=up_weight, up_bias=up_bias, down_weight=down_weight, down_bias=down_bias, out_grad=out_grad)


EPSILON = 1e-05
THRESHOLD = 0.05
PRECISE = lax.Precision.HIGHEST

def layer_norm(values, gains, biases):
    average = lax.optimization_barrier(jnp.mean(values, axis=-1, keepdims=True))
    centered = values - average
    variance = lax.optimization_barrier(jnp.mean(centered * centered, axis=-1, keepdims=True))
    return centered * lax.rsqrt(variance + EPSILON) * gains + biases

def complex_mix(real_in, imag_in, weights, offsets):
    real_out = jnp.einsum('jkbi,bio->jkbo', real_in, weights[0], precision=PRECISE) - jnp.einsum('jkbi,bio->jkbo', imag_in, weights[1], precision=PRECISE) + offsets[0]
    imag_out = jnp.einsum('jkbi,bio->jkbo', real_in, weights[1], precision=PRECISE) + jnp.einsum('jkbi,bio->jkbo', imag_in, weights[0], precision=PRECISE) + offsets[1]
    return (real_out, imag_out)

def shrink(values):
    return values - THRESHOLD * jnp.tanh(values / THRESHOLD)

def spectral(normed, mix_weights, mix_offsets):
    half_modes = MODES // 2
    spectrum = jnp.fft.rfft2(normed, axes=(0, 1), norm='ortho')
    retained = jnp.concatenate([spectrum[:half_modes, :MODES], spectrum[GRID - half_modes:, :MODES]], axis=0)
    block_shape = (MODES, MODES, BLOCKS, BLOCK)
    real_in = jnp.real(retained).reshape(block_shape)
    imag_in = jnp.imag(retained).reshape(block_shape)
    hidden_real, hidden_imag = complex_mix(real_in, imag_in, mix_weights[0], mix_offsets[0])
    hidden_real = jax.nn.gelu(hidden_real, approximate=False)
    hidden_imag = jax.nn.gelu(hidden_imag, approximate=False)
    out_real, out_imag = complex_mix(hidden_real, hidden_imag, mix_weights[1], mix_offsets[1])
    modes_out = lax.complex(shrink(out_real).reshape(MODES, MODES, D), shrink(out_imag).reshape(MODES, MODES, D))
    placed = jnp.zeros_like(spectrum)
    placed = placed.at[:half_modes, :MODES].set(modes_out[:half_modes])
    placed = placed.at[GRID - half_modes:, :MODES].set(modes_out[half_modes:])
    return jnp.fft.irfft2(placed, s=(GRID, GRID), axes=(0, 1), norm='ortho')

def layer_apply(one_item, parameters):
    gains, biases, mix_weights, mix_offsets, up_matrix, up_offset, down_matrix, down_offset = parameters
    normed = layer_norm(one_item, gains[0], biases[0])
    mixed = one_item + spectral(normed, mix_weights, mix_offsets)
    second = layer_norm(mixed, gains[1], biases[1]).reshape(GRID * GRID, D)
    hidden = jax.nn.gelu(jnp.dot(second, up_matrix, precision=PRECISE) + up_offset, approximate=False)
    branch = jnp.dot(hidden, down_matrix, precision=PRECISE) + down_offset
    return mixed + branch.reshape(GRID, GRID, D)

def whole_item(layer_params, one_item):
    for layer_index in range(2):
        one_item = layer_apply(one_item, tuple((weight[layer_index] for weight in layer_params)))
    return one_item

def reference(inputs, norm_gain, norm_bias, mix_weight, mix_bias, up_weight, up_bias, down_weight, down_bias, out_grad):
    parameters = (norm_gain, norm_bias, mix_weight, mix_bias, up_weight, up_bias, down_weight, down_bias)
    checked = jax.checkpoint(whole_item)

    def forward(layer_params, item_batch):

        def apply_one(one_item):
            return checked(layer_params, one_item)
        return lax.map(apply_one, item_batch)
    outputs, pullback = jax.vjp(forward, parameters, inputs)
    grad_layers, grad_inputs = pullback(out_grad)
    return (outputs, grad_inputs, grad_layers[0], grad_layers[1], grad_layers[2], grad_layers[3], grad_layers[4], grad_layers[5], grad_layers[6], grad_layers[7])
```

```python
import functools
import math

import jax
import jax.numpy as jnp
import numpy as np
from jax import lax
from jax.experimental import pallas as pl
from jax.experimental.pallas import tpu as pltpu
from jax.sharding import PartitionSpec as P

BLOCKS = 4
GRID = 64
MODES = 32
EPSILON = 1e-05
THRESHOLD = 0.05
ROWS = 4
F32 = jnp.float32
BF16 = jnp.bfloat16
BOTH = ("wide", "section")


def split_table(table):
    table = table.astype(np.float32)
    high = table.astype(jnp.bfloat16)
    low = (table - high.astype(np.float32)).astype(jnp.bfloat16)
    return np.concatenate([high, high, low, low], axis=1)


def column_tables():
    columns = np.arange(MODES)
    angles = 2.0 * math.pi * (columns[:, None] * np.arange(GRID)[None, :] % GRID) / GRID
    plain = np.concatenate([np.cos(angles), np.sin(angles)], axis=0) / GRID
    factor = np.where(columns == 0, 1.0, 2.0)
    weighted = plain * np.concatenate([factor, factor])[:, None]
    return plain, weighted


def twiddle(index, length):
    angle = 2.0 * math.pi * index / length
    return math.cos(angle), math.sin(angle)


def half_spectrum(planes, pruned=False):
    length = len(planes)
    if length == 2:
        return [(planes[0] + planes[1], None), (planes[0] - planes[1], None)]
    even = half_spectrum(planes[0::2])
    odd = half_spectrum(planes[1::2])
    quarter = length // 4
    first, second = [], []
    for k in range(quarter + 1):
        (er, ei), (dr, di) = even[k], odd[k]
        if k == 0:
            first.append((er + dr, None))
            second.append((er - dr, None))
            continue
        if k == quarter:
            first.append((er, -dr))
            continue
        c, s = twiddle(k, length)
        if 2 * k == quarter:
            tr, ti = (dr + di) * c, (di - dr) * c
        else:
            tr, ti = dr * c + di * s, di * c - dr * s
        first.append((er + tr, ei + ti))
        second.append((er - tr, ti - ei))
    if pruned:
        return first
    return first + second[::-1]


def half_synthesis(spectrum, length, pruned=False):
    if length == 2:
        (a, _), (b, _) = spectrum
        return [a + b, a - b]
    quarter = length // 4
    even, odd = [], []
    for k in range(quarter + 1):
        ar, ai = spectrum[k]
        if k == quarter:
            even.append((ar, None))
            odd.append((-ai, None))
            continue
        if k == 0:
            if pruned:
                even.append((ar, None))
                odd.append((ar, None))
            else:
                br = spectrum[length // 2][0]
                even.append((ar + br, None))
                odd.append((ar - br, None))
            continue
        if pruned:
            sr, si, tr, ti = ar, ai, ar, ai
        else:
            br, bi = spectrum[length // 2 - k]
            sr, si, tr, ti = ar + br, ai - bi, ar - br, ai + bi
        even.append((sr, si))
        c, s = twiddle(k, length)
        if 2 * k == quarter:
            odd.append(((tr - ti) * c, (ti + tr) * c))
        else:
            odd.append((tr * c - ti * s, ti * c + tr * s))
    even_planes = half_synthesis(even, length // 2)
    odd_planes = half_synthesis(odd, length // 2)
    planes = []
    for e, o in zip(even_planes, odd_planes):
        planes += [e, o]
    return planes


def exact_dot(left, right, left_dim, right_dim):
    return lax.dot_general(
        left,
        right,
        (((left_dim,), (right_dim,)), ((), ())),
        precision=lax.Precision.HIGH,
        preferred_element_type=F32,
    )


def split(values):
    high = values.astype(BF16)
    low = (values - high.astype(F32)).astype(BF16)
    return high, low


def table_dot(table, values):
    high, low = split(values)
    stacked = jnp.concatenate([high, low, high, low], axis=0)
    return jnp.dot(table, stacked, preferred_element_type=F32)


def gelu(values):
    return 0.5 * values * (1.0 + lax.erf(values * math.sqrt(0.5)))


def gelu_and_slope(values):
    cumulative = 0.5 * (1.0 + lax.erf(values * math.sqrt(0.5)))
    density = jnp.exp(-0.5 * values * values) * (1.0 / math.sqrt(2.0 * math.pi))
    return values * cumulative, cumulative + values * density


def normalise(values):
    average = jnp.mean(values, axis=-1, keepdims=True)
    centered = values - average
    variance = jnp.mean(centered * centered, axis=-1, keepdims=True)
    scale = lax.rsqrt(variance + EPSILON)
    return centered * scale, scale


def norm_backward(grad, unit, scale, gains):
    inner = grad * gains
    mean_inner = jnp.mean(inner, axis=-1, keepdims=True)
    mean_unit = jnp.mean(inner * unit, axis=-1, keepdims=True)
    return scale * (inner - mean_inner - unit * mean_unit)


def column_sum(values):
    return jnp.sum(values, axis=0, keepdims=True)


def joined(core, kept, other):
    shape = (kept.shape[0] * kept.shape[1], kept.shape[2])
    kept, other = kept[...].reshape(shape), other[...].reshape(shape)
    first = jnp.where(core == 0, kept, other)
    second = jnp.where(core == 0, other, kept)
    return jnp.concatenate([first, second], axis=1)


def parted(core, values, kept, other):
    half = values.shape[1] // 2
    first, second = values[:, :half], values[:, half:]
    kept[...] = jnp.where(core == 0, first, second).reshape(kept.shape)
    other[...] = jnp.where(core == 0, second, first).reshape(other.shape)


def flat(ref):
    return ref[...].reshape(-1, ref.shape[-1])


def picked(step, steps, refs):
    if len(refs) == 1:
        return flat(refs[0])
    return jnp.where(step < steps // 2, flat(refs[0]), flat(refs[1]))


def put_pieces(step, steps, refs, values):
    if len(refs) == 1:
        refs[0][...] = values.reshape(refs[0].shape)
        return

    @pl.when(step < steps // 2)
    def _():
        refs[0][...] = values.reshape(refs[0].shape)

    @pl.when(step >= steps // 2)
    def _():
        refs[1][...] = values.reshape(refs[1].shape)


def analyse(own, recv, table, sign, planes, modes):
    def rows(index, _):
        at = pl.ds(pl.multiple_of(index * 8, 8), 8)
        loaded = [own[p, at, :] for p in range(GRID // 2)] + [recv[p, at, :] for p in range(GRID // 2)]
        for k, (re, im) in enumerate(half_spectrum(loaded, pruned=True)):
            im = jnp.zeros_like(re) if im is None else im
            if k % 2:
                re, im = re * sign, im * sign
            planes[k, at, :] = jnp.concatenate([re, im], axis=1)
        return 0

    lax.fori_loop(0, GRID // 8, rows, 0)
    for k in range(MODES // 2 + 1):
        found = table_dot(table[...], planes[k])
        lanes = found.shape[1] // 2
        cr, ci = found[:MODES, :lanes], found[:MODES, lanes:]
        sr, si = found[MODES:, :lanes], found[MODES:, lanes:]
        if k < MODES // 2:
            modes[k * MODES : (k + 1) * MODES, :] = jnp.concatenate([cr + si, ci - sr], axis=1)
        if k > 0:
            place = MODES - k
            modes[place * MODES : (place + 1) * MODES, :] = jnp.concatenate([cr - si, -ci - sr], axis=1)


def synthesise(modes, table, sign, planes, keep, send):
    lanes = modes.shape[1] // 2
    for k in range(MODES // 2 + 1):
        place = MODES - k
        if k == 0:
            above, below = modes[0:MODES, :], None
            total, apart = above, above
        elif k == MODES // 2:
            below = modes[place * MODES : (place + 1) * MODES, :]
            total, apart = below, -below
        else:
            above = modes[k * MODES : (k + 1) * MODES, :]
            below = modes[place * MODES : (place + 1) * MODES, :]
            total, apart = above + below, above - below
        upper = jnp.concatenate([total[:, :lanes], apart[:, lanes:]], axis=1)
        lower = jnp.concatenate([-total[:, lanes:], apart[:, :lanes]], axis=1)
        planes[k] = table_dot(table[...], jnp.concatenate([upper, lower], axis=0))

    def rows(index, _):
        at = pl.ds(pl.multiple_of(index * 8, 8), 8)
        spectrum = []
        for k in range(MODES // 2 + 1):
            both = planes[k, at, :]
            if k % 2:
                both = both * sign
            spectrum.append((both[:, :lanes], both[:, lanes:]))
        cells = half_synthesis(spectrum, GRID, pruned=True)
        for p in range(GRID // 2):
            keep[p, at, :] = cells[p]
            send[p, at, :] = cells[GRID // 2 + p]
        return 0

    lax.fori_loop(0, GRID // 8, rows, 0)


def place_weights(weight, stacked):
    lanes = weight.shape[-1]
    for j in range(2):
        real, imag = weight[j, 0], weight[j, 1]
        stacked[j, :lanes, :lanes] = real
        stacked[j, :lanes, lanes:] = imag
        stacked[j, lanes:, :lanes] = -imag
        stacked[j, lanes:, lanes:] = real


MIX_ROWS = 256


def mix_offsets(offset, block):
    at = pl.ds(block, 1)
    return [jnp.concatenate([offset[j, 0, at, :], offset[j, 1, at, :]], axis=1) for j in range(2)]


def spectral_forward_kernel(
    info, own, recv, weight, offset, table_in, table_out, keep, send, modes, before, after, planes, shrunk, stacked
):
    core = info[0]
    sign = jnp.where(core == 1, -1.0, 1.0).astype(F32)
    place_weights(weight, stacked)
    first_offset, second_offset = mix_offsets(offset, 2 * core + pl.program_id(0))
    analyse(own, recv, table_in, sign, planes, modes)

    def mix(index, _):
        at = pl.ds(pl.multiple_of(index * MIX_ROWS, MIX_ROWS), MIX_ROWS)
        first = exact_dot(modes[at, :], stacked[0], 1, 0) + first_offset
        before[at, :] = first
        second = exact_dot(gelu(first), stacked[1], 1, 0) + second_offset
        after[at, :] = second
        shrunk[at, :] = second - THRESHOLD * jnp.tanh(second * (1.0 / THRESHOLD))
        return 0

    lax.fori_loop(0, MODES * MODES // MIX_ROWS, mix, 0)
    synthesise(shrunk, table_out, sign, planes, keep, send)


def spectral_backward_kernel(
    info, own, recv, weight, modes, before, after, table_in, table_out, keep, send, weight_grad, offset_grad, planes, flowing, stacked, summed
):
    core = info[0]
    sign = jnp.where(core == 1, -1.0, 1.0).astype(F32)
    place_weights(weight, stacked)
    analyse(own, recv, table_in, sign, planes, flowing)
    summed[...] = jnp.zeros_like(summed)

    def mix(index, totals):
        at = pl.ds(pl.multiple_of(index * MIX_ROWS, MIX_ROWS), MIX_ROWS)
        ratio = jnp.tanh(after[at, :] * (1.0 / THRESHOLD))
        grad_second = flowing[at, :] * ratio * ratio
        hidden, slope = gelu_and_slope(before[at, :])
        summed[1] += exact_dot(hidden, grad_second, 0, 0)
        grad_first = exact_dot(grad_second, stacked[1], 1, 1) * slope
        summed[0] += exact_dot(modes[at, :], grad_first, 0, 0)
        flowing[at, :] = exact_dot(grad_first, stacked[0], 1, 1)
        return totals[0] + column_sum(grad_first), totals[1] + column_sum(grad_second)

    empty = jnp.zeros((1, flowing.shape[1]), F32)
    totals = lax.fori_loop(0, MODES * MODES // MIX_ROWS, mix, (empty, empty))
    lanes = flowing.shape[1] // 2
    for j in range(2):
        offset_grad[j, 0] = totals[j][:, :lanes]
        offset_grad[j, 1] = totals[j][:, lanes:]
        weight_grad[j, 0] = summed[j, :lanes, :lanes] + summed[j, lanes:, lanes:]
        weight_grad[j, 1] = summed[j, :lanes, lanes:] - summed[j, lanes:, :lanes]
    synthesise(flowing, table_out, sign, planes, keep, send)


def first_norm_kernel(steps, info, a, b, gains, biases, keep, send):
    unit, _ = normalise(picked(pl.program_id(0), steps, (a, b)))
    parted(info[0], unit * gains[0:1] + biases[0:1], keep, send)


def ffn_forward_kernel(steps, layer, pieces, more, info, *refs):
    step = pl.program_id(0)
    refs = list(refs)
    x_refs, refs = refs[:pieces], refs[pieces:]
    kept, taken, gains, biases, up, up_offset, down, down_offset = refs[:8]
    refs = refs[8:]
    core = info[0]
    mixed = picked(step, steps, x_refs) + joined(core, kept, taken)
    unit, _ = normalise(mixed)
    normed = unit * gains[1:2] + biases[1:2]
    before = exact_dot(normed, up[...], 1, 0) + up_offset[layer : layer + 1]
    result = mixed + exact_dot(gelu(before), down[...], 1, 0) + down_offset[layer : layer + 1]
    if more:
        next_gains, next_biases, mixed_out, before_out, result_out, keep, send = refs
        put_pieces(step, steps, (result_out,), result)
        unit, _ = normalise(result)
        parted(core, unit * next_gains[0:1] + next_biases[0:1], keep, send)
    else:
        mixed_out, before_out, first_out, second_out = refs
        put_pieces(step, steps, (first_out, second_out), result)
    mixed_out[...] = mixed.reshape(mixed_out.shape)
    before_out[...] = before.reshape(before_out.shape)


def first_norm_backward(core, x, du_kept, du_sent, dh_kept, dh_taken, gains):
    grad = joined(core, dh_kept, dh_taken)
    unit, scale = normalise(x)
    result = joined(core, du_kept, du_sent) + norm_backward(grad, unit, scale, gains[0:1])
    return result, column_sum(grad * unit), column_sum(grad)


def ffn_backward_kernel(steps, fused, info, *refs):
    step = pl.program_id(0)
    core = info[0]
    refs = list(refs)
    mixed, before, gains, biases, up, down = refs[:6]
    if fused:
        x, du_kept, du_sent, dh_kept, dh_taken, next_gains = refs[6:12]
        grad, late_gain, late_bias = first_norm_backward(core, flat(x), du_kept, du_sent, dh_kept, dh_taken, next_gains)
        refs = refs[12:]
    else:
        grad = picked(step, steps, refs[6:8])
        refs = refs[8:]
    keep, send, up_grad, down_grad, small = refs

    @pl.when(step == 0)
    def _():
        up_grad[...] = jnp.zeros_like(up_grad)
        down_grad[...] = jnp.zeros_like(down_grad)
        small[...] = jnp.zeros_like(small)

    unit, scale = normalise(flat(mixed))
    normed = unit * gains[1:2] + biases[1:2]
    hidden, slope = gelu_and_slope(flat(before))
    down_grad[...] += exact_dot(hidden, grad, 0, 0)
    inner = exact_dot(grad, down[...], 1, 1) * slope
    up_grad[...] += exact_dot(normed, inner, 0, 0)
    outer = exact_dot(inner, up[...], 1, 1)
    small[0:1] += column_sum(outer * unit)
    small[1:2] += column_sum(outer)
    small[2:3] += column_sum(inner)
    small[3:4] += column_sum(grad)
    if fused:
        small[4:5] += late_gain
        small[5:6] += late_bias
    parted(core, grad + norm_backward(outer, unit, scale, gains[1:2]), keep, send)


def input_grad_kernel(steps, info, a, b, du_kept, du_sent, dh_kept, dh_taken, gains, first_out, second_out, small):
    step = pl.program_id(0)
    x = picked(step, steps, (a, b))
    result, gain_sum, bias_sum = first_norm_backward(info[0], x, du_kept, du_sent, dh_kept, dh_taken, gains)

    @pl.when(step == 0)
    def _():
        small[...] = jnp.zeros_like(small)

    small[0:1] += gain_sum
    small[1:2] += bias_sum
    put_pieces(step, steps, (first_out, second_out), result)


def call(kernel, grid, in_specs, out_specs, out_shapes, scratch, flops, moved, name):
    return pl.pallas_call(
        kernel,
        grid_spec=pltpu.PrefetchScalarGridSpec(
            num_scalar_prefetch=1,
            grid=(grid,),
            in_specs=in_specs,
            out_specs=out_specs,
            scratch_shapes=scratch,
        ),
        out_shape=out_shapes,
        compiler_params=pltpu.CompilerParams(vmem_limit_bytes=56 * 2**20),
        cost_estimate=pl.CostEstimate(flops=int(flops), bytes_accessed=int(moved), transcendentals=0),
        name=name,
    )


class Plan:
    def __init__(self, quarter, width, hidden):
        self.quarter, self.width, self.hidden = quarter, width, hidden
        self.steps = 2 * quarter // ROWS
        per_piece = quarter // ROWS
        half = width // 2

        def local(j, s):
            return (j, 0, 0)

        def canonical(j, s):
            return (((j // per_piece) ^ s[1]) * per_piece + j % per_piece, 0, 0)

        self.row = pl.BlockSpec((ROWS, GRID, width), local)
        self.wide_row = pl.BlockSpec((ROWS, GRID, hidden), local)
        self.half_row = pl.BlockSpec((ROWS, GRID, half), canonical)
        self.first = pl.BlockSpec((ROWS, GRID, width), lambda j, s: (jnp.minimum(j, per_piece - 1), 0, 0))
        self.second = pl.BlockSpec((ROWS, GRID, width), lambda j, s: (jnp.maximum(j - per_piece, 0), 0, 0))
        self.half_shape = jax.ShapeDtypeStruct((2 * quarter, GRID, half), F32)
        self.row_shape = jax.ShapeDtypeStruct((2 * quarter, GRID, width), F32)
        self.wide_shape = jax.ShapeDtypeStruct((2 * quarter, GRID, hidden), F32)
        self.piece_shape = jax.ShapeDtypeStruct((quarter, GRID, width), F32)

    def norm(self, layer):
        return pl.BlockSpec((None, 2, self.width), lambda j, s: (layer, 0, 0))

    def matrix(self, layer, rows, columns):
        return pl.BlockSpec((None, rows, columns), lambda j, s: (layer, 0, 0))

    def whole(self, shape):
        return pl.BlockSpec(shape, lambda j, s: (0,) * len(shape))


def first_norm(plan, info, a, b, gains, biases):
    return call(
        functools.partial(first_norm_kernel, plan.steps),
        plan.steps,
        [plan.first, plan.second, plan.norm(0), plan.norm(0)],
        [plan.half_row, plan.half_row],
        [plan.half_shape, plan.half_shape],
        [],
        0,
        4 * 2**20 * 2,
        "first_norm",
    )(info, a, b, gains, biases)


def spectral_specs(layer, width):
    block = width // BLOCKS
    cells = pl.BlockSpec((GRID // 2, GRID, block), lambda b, s: (0, 0, b))
    weight = pl.BlockSpec((None, 2, 2, None, block, block), lambda b, s: (layer, 0, 0, 2 * s[0] + b, 0, 0))
    offset = pl.BlockSpec((None, 2, 2, BLOCKS, block), lambda b, s: (layer, 0, 0, 0, 0))
    table = pl.BlockSpec((GRID, 4 * GRID), lambda b, s: (0, 0))
    modes = pl.BlockSpec((None, MODES * MODES, 2 * block), lambda b, s: (b, 0, 0))
    modes_shape = jax.ShapeDtypeStruct((2, MODES * MODES, 2 * block), F32)
    planes = pltpu.VMEM((MODES // 2 + 1, GRID, 2 * block), F32)
    flowing = pltpu.VMEM((MODES * MODES, 2 * block), F32)
    stacked = pltpu.VMEM((2, 2 * block, 2 * block), F32)
    return block, cells, weight, offset, table, modes, modes_shape, planes, flowing, stacked


def spectral_forward(plan, layer, info, own, recv, weight_all, offset_all, tables):
    block, cells, weight, offset, table, modes, modes_shape, planes, flowing, stacked = spectral_specs(layer, plan.width)
    return call(
        spectral_forward_kernel,
        2,
        [cells, cells, weight, offset, table, table],
        [cells, cells, modes, modes, modes],
        [plan.half_shape, plan.half_shape, modes_shape, modes_shape, modes_shape],
        [planes, flowing, stacked],
        3 * 2e9,
        14 * 2**20,
        f"spectral_forward_{layer}",
    )(info, own, recv, weight_all, offset_all, tables[0], tables[3])


def spectral_backward(plan, layer, info, own, recv, weight_all, saved, tables):
    block, cells, weight, offset, table, modes, modes_shape, planes, flowing, stacked = spectral_specs(layer, plan.width)
    return call(
        spectral_backward_kernel,
        2,
        [cells, cells, weight, modes, modes, modes, table, table],
        [
            cells,
            cells,
            pl.BlockSpec((2, 2, None, block, block), lambda b, s: (0, 0, b, 0, 0)),
            pl.BlockSpec((2, 2, None, 1, block), lambda b, s: (0, 0, b, 0, 0)),
        ],
        [
            plan.half_shape,
            plan.half_shape,
            jax.ShapeDtypeStruct((2, 2, 2, block, block), F32),
            jax.ShapeDtypeStruct((2, 2, 2, 1, block), F32),
        ],
        [planes, flowing, stacked, pltpu.VMEM((2, 2 * block, 2 * block), F32)],
        3 * 4e9,
        14 * 2**20,
        f"spectral_backward_{layer}",
    )(info, own, recv, weight_all, *saved, tables[1], tables[2])


def ffn_forward(plan, layer, more, info, x, kept, taken, gains, biases, up, up_offset, down, down_offset):
    width, hidden = plan.width, plan.hidden
    specs = [plan.first, plan.second] if len(x) == 2 else [plan.row]
    specs += [plan.half_row, plan.half_row, plan.norm(layer), plan.norm(layer)]
    specs += [plan.matrix(layer, width, hidden), plan.whole(up_offset.shape)]
    specs += [plan.matrix(layer, hidden, width), plan.whole(down_offset.shape)]
    args = [*x, kept, taken, gains, biases, up, up_offset, down, down_offset]
    out_specs = [plan.row, plan.wide_row]
    out_shapes = [plan.row_shape, plan.wide_shape]
    if more:
        specs += [plan.norm(layer + 1), plan.norm(layer + 1)]
        args += [gains, biases]
        out_specs += [plan.row, plan.half_row, plan.half_row]
        out_shapes += [plan.row_shape, plan.half_shape, plan.half_shape]
    else:
        out_specs += [plan.first, plan.second]
        out_shapes += [plan.piece_shape, plan.piece_shape]
    return call(
        functools.partial(ffn_forward_kernel, plan.steps, layer, len(x), more),
        plan.steps,
        specs,
        out_specs,
        out_shapes,
        [],
        3 * 4 * 2048 * width * hidden,
        24 * 2**20,
        f"ffn_forward_{layer}",
    )(info, *args)


def ffn_backward(plan, layer, info, mixed, before, gains, biases, up, down, grads):
    width, hidden = plan.width, plan.hidden
    fused = len(grads) == 5
    specs = [plan.row, plan.wide_row, plan.norm(layer), plan.norm(layer)]
    specs += [plan.matrix(layer, width, hidden), plan.matrix(layer, hidden, width)]
    args = [mixed, before, gains, biases, up, down, *grads]
    if fused:
        specs += [plan.row] + [plan.half_row] * 4 + [plan.norm(layer + 1)]
        args += [gains]
    else:
        specs += [plan.first, plan.second]
    return call(
        functools.partial(ffn_backward_kernel, plan.steps, fused),
        plan.steps,
        specs,
        [
            plan.half_row,
            plan.half_row,
            plan.whole((width, hidden)),
            plan.whole((hidden, width)),
            plan.whole((8, width)),
        ],
        [
            plan.half_shape,
            plan.half_shape,
            jax.ShapeDtypeStruct((width, hidden), F32),
            jax.ShapeDtypeStruct((hidden, width), F32),
            jax.ShapeDtypeStruct((8, width), F32),
        ],
        [],
        3 * 8 * 2048 * width * hidden,
        24 * 2**20,
        f"ffn_backward_{layer}",
    )(info, *args)


def input_gradient(plan, info, a, b, du, dh, gains):
    return call(
        functools.partial(input_grad_kernel, plan.steps),
        plan.steps,
        [plan.first, plan.second] + [plan.half_row] * 4 + [plan.norm(0)],
        [plan.first, plan.second, plan.whole((8, plan.width))],
        [plan.piece_shape, plan.piece_shape, jax.ShapeDtypeStruct((8, plan.width), F32)],
        [],
        0,
        16 * 2**20,
        "input_gradient",
    )(info, a, b, *du, *dh, gains)


def item_routes(wide, section):
    routes = []
    for flip in range(2):
        pairs = []
        for w in range(wide):
            c = w % 2
            for z in range(section):
                pairs.append((w * section + z, (w - c + z // 2) * section + 2 * c + (z % 2 ^ flip)))
        routes.append(pairs)
    return routes


def gather_pieces(shard, parity, routes):
    first = lax.dynamic_index_in_dim(shard, parity, 0, keepdims=False)
    second = lax.dynamic_index_in_dim(shard, 1 - parity, 0, keepdims=False)
    return lax.ppermute(first, BOTH, routes[0]), lax.ppermute(second, BOTH, routes[1])


def scatter_pieces(first, second, parity, routes):
    first = lax.ppermute(first, BOTH, [(b, a) for a, b in routes[0]])
    second = lax.ppermute(second, BOTH, [(b, a) for a, b in routes[1]])
    low = jnp.where(parity == 0, first, second)
    high = jnp.where(parity == 0, second, first)
    return jnp.stack([low, high])


def swap(values):
    return lax.ppermute(values, "wide", [(i, i ^ 1) for i in range(lax.axis_size("wide"))])


def on_device(
    inputs,
    norm_gain,
    norm_bias,
    mix_weight,
    mix_bias,
    up_weight,
    up_bias,
    down_weight,
    down_bias,
    out_grad,
):
    width, hidden = up_weight.shape[1:]
    plan = Plan(inputs.shape[1], width, hidden)
    routes = item_routes(lax.axis_size("wide"), lax.axis_size("section"))
    core = lax.axis_index("wide") % 2
    parity = lax.axis_index("section") % 2
    info = jnp.stack([core, parity]).astype(jnp.int32)
    plain, weighted = column_tables()
    tables = [jnp.asarray(split_table(t)) for t in (plain, weighted, plain.T, weighted.T)]

    xa, xb = gather_pieces(inputs, parity, routes)
    out_grad, xa, xb = lax.optimization_barrier((out_grad, xa, xb))
    ga, gb = gather_pieces(out_grad, parity, routes)

    ffn_args = (norm_gain, norm_bias, up_weight, up_bias, down_weight, down_bias)
    keep, send = first_norm(plan, info, xa, xb, norm_gain, norm_bias)
    keep, send, *saved0 = spectral_forward(plan, 0, info, keep, swap(send), mix_weight, mix_bias, tables)
    u0, a0, x1, keep, send = ffn_forward(plan, 0, True, info, (xa, xb), keep, swap(send), *ffn_args)
    keep, send, *saved1 = spectral_forward(plan, 1, info, keep, swap(send), mix_weight, mix_bias, tables)
    u1, a1, va, vb = ffn_forward(plan, 1, False, info, (x1,), keep, swap(send), *ffn_args)

    va, vb, ga, gb = lax.optimization_barrier((va, vb, ga, gb))
    outputs = scatter_pieces(va, vb, parity, routes)

    back_args = (norm_gain, norm_bias, up_weight, down_weight)
    du1 = ffn_backward(plan, 1, info, u1, a1, *back_args, (ga, gb))
    dh1 = spectral_backward(plan, 1, info, du1[0], swap(du1[1]), mix_weight, saved1, tables)
    late = (x1, du1[0], du1[1], dh1[0], swap(dh1[1]))
    du0 = ffn_backward(plan, 0, info, u0, a0, *back_args, late)
    dh0 = spectral_backward(plan, 0, info, du0[0], swap(du0[1]), mix_weight, saved0, tables)
    dxa, dxb, small = input_gradient(plan, info, xa, xb, du0[:2], (dh0[0], swap(dh0[1])), norm_gain)
    input_grad = scatter_pieces(dxa, dxb, parity, routes)

    def placed(part):
        empty = jnp.zeros_like(part)
        return jnp.where(core == 0, jnp.concatenate([part, empty], 2), jnp.concatenate([empty, part], 2))

    mix_grads = jnp.stack([placed(dh0[2]), placed(dh1[2])])
    offset_grads = jnp.stack([placed(dh0[3]), placed(dh1[3])])[:, :, :, :, 0]
    gain_grads = jnp.stack([jnp.stack([small[0], du0[4][0]]), jnp.stack([du0[4][4], du1[4][0]])])
    bias_grads = jnp.stack([jnp.stack([small[1], du0[4][1]]), jnp.stack([du0[4][5], du1[4][1]])])
    up_grads = jnp.stack([du0[2], du1[2]])
    down_grads = jnp.stack([du0[3], du1[3]])
    up_offset_grads = jnp.stack([du0[4][2], du1[4][2]])
    down_offset_grads = jnp.stack([du0[4][3], du1[4][3]])
    summed = lax.psum(
        (gain_grads, bias_grads, mix_grads, offset_grads, up_grads, up_offset_grads, down_grads, down_offset_grads), BOTH
    )
    return (outputs, input_grad, *summed)


def solution(mesh):
    cells = P("wide", "section", None, None)
    return jax.shard_map(
        on_device,
        mesh=mesh,
        in_specs=(cells, P(), P(), P(), P(), P(), P(), P(), P(), cells),
        out_specs=(cells, cells, P(), P(), P(), P(), P(), P(), P(), P()),
        check_vma=False,
    )
```

```python
import functools
import math

import jax
import jax.numpy as jnp
import numpy as np
from jax import lax
from jax.experimental import pallas as pl
from jax.experimental.pallas import tpu as pltpu
from jax.sharding import PartitionSpec as P

BLOCKS = 4
GRID = 64
MODES = 32
EPSILON = 1e-05
THRESHOLD = 0.05
ROWS = 4
F32 = jnp.float32
BF16 = jnp.bfloat16
BOTH = ("wide", "section")


def split_table(table):
    table = table.astype(np.float32)
    high = table.astype(jnp.bfloat16)
    low = (table - high.astype(np.float32)).astype(jnp.bfloat16)
    return np.concatenate([high, high, low, low], axis=1)


def column_tables():
    columns = np.arange(MODES)
    angles = 2.0 * math.pi * (columns[:, None] * np.arange(GRID)[None, :] % GRID) / GRID
    plain = np.concatenate([np.cos(angles), np.sin(angles)], axis=0) / GRID
    factor = np.where(columns == 0, 1.0, 2.0)
    weighted = plain * np.concatenate([factor, factor])[:, None]
    return plain, weighted


def twiddle(index, length):
    angle = 2.0 * math.pi * index / length
    return math.cos(angle), math.sin(angle)


def half_spectrum(planes, pruned=False):
    length = len(planes)
    if length == 2:
        return [(planes[0] + planes[1], None), (planes[0] - planes[1], None)]
    even = half_spectrum(planes[0::2])
    odd = half_spectrum(planes[1::2])
    quarter = length // 4
    first, second = [], []
    for k in range(quarter + 1):
        (er, ei), (dr, di) = even[k], odd[k]
        if k == 0:
            first.append((er + dr, None))
            second.append((er - dr, None))
            continue
        if k == quarter:
            first.append((er, -dr))
            continue
        c, s = twiddle(k, length)
        if 2 * k == quarter:
            tr, ti = (dr + di) * c, (di - dr) * c
        else:
            tr, ti = dr * c + di * s, di * c - dr * s
        first.append((er + tr, ei + ti))
        second.append((er - tr, ti - ei))
    if pruned:
        return first
    return first + second[::-1]


def half_synthesis(spectrum, length, pruned=False):
    if length == 2:
        (a, _), (b, _) = spectrum
        return [a + b, a - b]
    quarter = length // 4
    even, odd = [], []
    for k in range(quarter + 1):
        ar, ai = spectrum[k]
        if k == quarter:
            even.append((ar, None))
            odd.append((-ai, None))
            continue
        if k == 0:
            if pruned:
                even.append((ar, None))
                odd.append((ar, None))
            else:
                br = spectrum[length // 2][0]
                even.append((ar + br, None))
                odd.append((ar - br, None))
            continue
        if pruned:
            sr, si, tr, ti = ar, ai, ar, ai
        else:
            br, bi = spectrum[length // 2 - k]
            sr, si, tr, ti = ar + br, ai - bi, ar - br, ai + bi
        even.append((sr, si))
        c, s = twiddle(k, length)
        if 2 * k == quarter:
            odd.append(((tr - ti) * c, (ti + tr) * c))
        else:
            odd.append((tr * c - ti * s, ti * c + tr * s))
    even_planes = half_synthesis(even, length // 2)
    odd_planes = half_synthesis(odd, length // 2)
    planes = []
    for e, o in zip(even_planes, odd_planes):
        planes += [e, o]
    return planes


def exact_dot(left, right, left_dim, right_dim):
    return lax.dot_general(
        left,
        right,
        (((left_dim,), (right_dim,)), ((), ())),
        precision=lax.Precision.HIGH,
        preferred_element_type=F32,
    )


def split(values):
    high = values.astype(BF16)
    low = (values - high.astype(F32)).astype(BF16)
    return high, low


def table_dot(table, values):
    high, low = split(values)
    stacked = jnp.concatenate([high, low, high, low], axis=0)
    return jnp.dot(table, stacked, preferred_element_type=F32)


def gelu(values):
    return 0.5 * values * (1.0 + lax.erf(values * math.sqrt(0.5)))


def gelu_and_slope(values):
    cumulative = 0.5 * (1.0 + lax.erf(values * math.sqrt(0.5)))
    density = jnp.exp(-0.5 * values * values) * (1.0 / math.sqrt(2.0 * math.pi))
    return values * cumulative, cumulative + values * density


def normalise(values):
    average = jnp.mean(values, axis=-1, keepdims=True)
    centered = values - average
    variance = jnp.mean(centered * centered, axis=-1, keepdims=True)
    scale = lax.rsqrt(variance + EPSILON)
    return centered * scale, scale


def norm_backward(grad, unit, scale, gains):
    inner = grad * gains
    mean_inner = jnp.mean(inner, axis=-1, keepdims=True)
    mean_unit = jnp.mean(inner * unit, axis=-1, keepdims=True)
    return scale * (inner - mean_inner - unit * mean_unit)


def column_sum(values):
    return jnp.sum(values, axis=0, keepdims=True)


def joined(core, kept, other):
    shape = (kept.shape[0] * kept.shape[1], kept.shape[2])
    kept, other = kept[...].reshape(shape), other[...].reshape(shape)
    first = jnp.where(core == 0, kept, other)
    second = jnp.where(core == 0, other, kept)
    return jnp.concatenate([first, second], axis=1)


def parted(core, values, kept, other):
    half = values.shape[1] // 2
    first, second = values[:, :half], values[:, half:]
    kept[...] = jnp.where(core == 0, first, second).reshape(kept.shape)
    other[...] = jnp.where(core == 0, second, first).reshape(other.shape)


def flat(ref):
    return ref[...].reshape(-1, ref.shape[-1])


def picked(step, steps, refs):
    if len(refs) == 1:
        return flat(refs[0])
    return jnp.where(step < steps // 2, flat(refs[0]), flat(refs[1]))


def put_pieces(step, steps, refs, values):
    if len(refs) == 1:
        refs[0][...] = values.reshape(refs[0].shape)
        return

    @pl.when(step < steps // 2)
    def _():
        refs[0][...] = values.reshape(refs[0].shape)

    @pl.when(step >= steps // 2)
    def _():
        refs[1][...] = values.reshape(refs[1].shape)


def analyse(own, recv, table, sign, planes, modes):
    def rows(index, _):
        at = pl.ds(pl.multiple_of(index * 8, 8), 8)
        loaded = [own[p, at, :] for p in range(GRID // 2)] + [recv[p, at, :] for p in range(GRID // 2)]
        for k, (re, im) in enumerate(half_spectrum(loaded, pruned=True)):
            im = jnp.zeros_like(re) if im is None else im
            if k % 2:
                re, im = re * sign, im * sign
            planes[k, at, :] = jnp.concatenate([re, im], axis=1)
        return 0

    lax.fori_loop(0, GRID // 8, rows, 0)
    for k in range(MODES // 2 + 1):
        found = table_dot(table[...], planes[k])
        lanes = found.shape[1] // 2
        cr, ci = found[:MODES, :lanes], found[:MODES, lanes:]
        sr, si = found[MODES:, :lanes], found[MODES:, lanes:]
        if k < MODES // 2:
            modes[k * MODES : (k + 1) * MODES, :] = jnp.concatenate([cr + si, ci - sr], axis=1)
        if k > 0:
            place = MODES - k
            modes[place * MODES : (place + 1) * MODES, :] = jnp.concatenate([cr - si, -ci - sr], axis=1)


def synthesise(modes, table, sign, planes, keep, send):
    lanes = modes.shape[1] // 2
    for k in range(MODES // 2 + 1):
        place = MODES - k
        if k == 0:
            above, below = modes[0:MODES, :], None
            total, apart = above, above
        elif k == MODES // 2:
            below = modes[place * MODES : (place + 1) * MODES, :]
            total, apart = below, -below
        else:
            above = modes[k * MODES : (k + 1) * MODES, :]
            below = modes[place * MODES : (place + 1) * MODES, :]
            total, apart = above + below, above - below
        upper = jnp.concatenate([total[:, :lanes], apart[:, lanes:]], axis=1)
        lower = jnp.concatenate([-total[:, lanes:], apart[:, :lanes]], axis=1)
        planes[k] = table_dot(table[...], jnp.concatenate([upper, lower], axis=0))

    def rows(index, _):
        at = pl.ds(pl.multiple_of(index * 8, 8), 8)
        spectrum = []
        for k in range(MODES // 2 + 1):
            both = planes[k, at, :]
            if k % 2:
                both = both * sign
            spectrum.append((both[:, :lanes], both[:, lanes:]))
        cells = half_synthesis(spectrum, GRID, pruned=True)
        for p in range(GRID // 2):
            keep[p, at, :] = cells[p]
            send[p, at, :] = cells[GRID // 2 + p]
        return 0

    lax.fori_loop(0, GRID // 8, rows, 0)


def place_weights(weight, stacked):
    lanes = weight.shape[-1]
    for j in range(2):
        real, imag = weight[j, 0], weight[j, 1]
        stacked[j, :lanes, :lanes] = real
        stacked[j, :lanes, lanes:] = imag
        stacked[j, lanes:, :lanes] = -imag
        stacked[j, lanes:, lanes:] = real


MIX_ROWS = 256


def mix_offsets(offset, block):
    at = pl.ds(block, 1)
    return [jnp.concatenate([offset[j, 0, at, :], offset[j, 1, at, :]], axis=1) for j in range(2)]


def spectral_forward_kernel(
    info, own, recv, weight, offset, table_in, table_out, keep, send, modes, before, after, planes, shrunk, stacked
):
    core = info[0]
    sign = jnp.where(core == 1, -1.0, 1.0).astype(F32)
    place_weights(weight, stacked)
    first_offset, second_offset = mix_offsets(offset, 2 * core + pl.program_id(0))
    analyse(own, recv, table_in, sign, planes, modes)

    def mix(index, _):
        at = pl.ds(pl.multiple_of(index * MIX_ROWS, MIX_ROWS), MIX_ROWS)
        first = exact_dot(modes[at, :], stacked[0], 1, 0) + first_offset
        before[at, :] = first
        second = exact_dot(gelu(first), stacked[1], 1, 0) + second_offset
        after[at, :] = second
        shrunk[at, :] = second - THRESHOLD * jnp.tanh(second * (1.0 / THRESHOLD))
        return 0

    lax.fori_loop(0, MODES * MODES // MIX_ROWS, mix, 0)
    synthesise(shrunk, table_out, sign, planes, keep, send)


def spectral_backward_kernel(
    info, own, recv, weight, modes, before, after, table_in, table_out, keep, send, weight_grad, offset_grad, planes, flowing, stacked, summed
):
    core = info[0]
    sign = jnp.where(core == 1, -1.0, 1.0).astype(F32)
    place_weights(weight, stacked)
    analyse(own, recv, table_in, sign, planes, flowing)
    summed[...] = jnp.zeros_like(summed)

    def mix(index, totals):
        at = pl.ds(pl.multiple_of(index * MIX_ROWS, MIX_ROWS), MIX_ROWS)
        ratio = jnp.tanh(after[at, :] * (1.0 / THRESHOLD))
        grad_second = flowing[at, :] * ratio * ratio
        hidden, slope = gelu_and_slope(before[at, :])
        summed[1] += exact_dot(hidden, grad_second, 0, 0)
        grad_first = exact_dot(grad_second, stacked[1], 1, 1) * slope
        summed[0] += exact_dot(modes[at, :], grad_first, 0, 0)
        flowing[at, :] = exact_dot(grad_first, stacked[0], 1, 1)
        return totals[0] + column_sum(grad_first), totals[1] + column_sum(grad_second)

    empty = jnp.zeros((1, flowing.shape[1]), F32)
    totals = lax.fori_loop(0, MODES * MODES // MIX_ROWS, mix, (empty, empty))
    lanes = flowing.shape[1] // 2
    for j in range(2):
        offset_grad[j, 0] = totals[j][:, :lanes]
        offset_grad[j, 1] = totals[j][:, lanes:]
        weight_grad[j, 0] = summed[j, :lanes, :lanes] + summed[j, lanes:, lanes:]
        weight_grad[j, 1] = summed[j, :lanes, lanes:] - summed[j, lanes:, :lanes]
    synthesise(flowing, table_out, sign, planes, keep, send)


def first_norm_kernel(steps, info, a, b, gains, biases, keep, send):
    unit, _ = normalise(picked(pl.program_id(0), steps, (a, b)))
    parted(info[0], unit * gains[0:1] + biases[0:1], keep, send)


def ffn_forward_kernel(steps, layer, pieces, more, info, *refs):
    step = pl.program_id(0)
    refs = list(refs)
    x_refs, refs = refs[:pieces], refs[pieces:]
    kept, taken, gains, biases, up, up_offset, down, down_offset = refs[:8]
    refs = refs[8:]
    core = info[0]
    mixed = picked(step, steps, x_refs) + joined(core, kept, taken)
    unit, _ = normalise(mixed)
    normed = unit * gains[1:2] + biases[1:2]
    before = exact_dot(normed, up[...], 1, 0) + up_offset[layer : layer + 1]
    result = mixed + exact_dot(gelu(before), down[...], 1, 0) + down_offset[layer : layer + 1]
    if more:
        next_gains, next_biases, mixed_out, before_out, result_out, keep, send = refs
        put_pieces(step, steps, (result_out,), result)
        unit, _ = normalise(result)
        parted(core, unit * next_gains[0:1] + next_biases[0:1], keep, send)
    else:
        mixed_out, before_out, first_out, second_out = refs
        put_pieces(step, steps, (first_out, second_out), result)
    mixed_out[...] = mixed.reshape(mixed_out.shape)
    before_out[...] = before.reshape(before_out.shape)


def first_norm_backward(core, x, du_kept, du_sent, dh_kept, dh_taken, gains):
    grad = joined(core, dh_kept, dh_taken)
    unit, scale = normalise(x)
    result = joined(core, du_kept, du_sent) + norm_backward(grad, unit, scale, gains[0:1])
    return result, column_sum(grad * unit), column_sum(grad)


def lanes_first(values):
    return [values[:, at : at + 128] for at in range(0, values.shape[1], 128)]


def ffn_backward_kernel(steps, fused, by_member, info, *refs):
    step = pl.program_id(0)
    core = info[0]
    refs = list(refs)
    mixed, before, gains, biases, up, down = refs[:6]
    if fused:
        x, du_kept, du_sent, dh_kept, dh_taken, next_gains = refs[6:12]
        grad, late_gain, late_bias = first_norm_backward(core, flat(x), du_kept, du_sent, dh_kept, dh_taken, next_gains)
        refs = refs[12:]
    else:
        grad = picked(step, steps, refs[6:8])
        refs = refs[8:]
    keep, send, *packed, up_grad, down_grad, small = refs
    kept_grads, sent_grads = packed if by_member else (packed[0].at[0], packed[0].at[1])

    @pl.when(step == 0)
    def _():
        up_grad[...] = jnp.zeros_like(up_grad)
        down_grad[...] = jnp.zeros_like(down_grad)
        small[...] = jnp.zeros_like(small)

    unit, scale = normalise(flat(mixed))
    normed = unit * gains[1:2] + biases[1:2]
    hidden, slope = gelu_and_slope(flat(before))
    down_grad[...] += exact_dot(hidden, grad, 0, 0)
    inner = exact_dot(grad, down[...], 1, 1) * slope
    up_grad[...] += exact_dot(normed, inner, 0, 0)
    outer = exact_dot(inner, up[...], 1, 1)
    small[0:1] += column_sum(outer * unit)
    small[1:2] += column_sum(outer)
    small[2:3] += column_sum(inner)
    small[3:4] += column_sum(grad)
    if fused:
        small[4:5] += late_gain
        small[5:6] += late_bias
    parted(core, grad + norm_backward(outer, unit, scale, gains[1:2]), keep, send)

    @pl.when(step == steps - 1)
    def _():
        width = up_grad.shape[0]
        parts = zip(lanes_first(up_grad[...]), lanes_first(down_grad[...]), lanes_first(small[...]))
        for index, (a, b, c) in enumerate(parts):
            kept_grads[index, :width] = jnp.where(core == 0, a, b) if by_member else a
            sent_grads[index, :width] = jnp.where(core == 0, b, a) if by_member else b
            kept_grads[index, width:] = c
            sent_grads[index, width:] = c


def input_grad_kernel(steps, info, a, b, du_kept, du_sent, dh_kept, dh_taken, gains, first_out, second_out, small):
    step = pl.program_id(0)
    x = picked(step, steps, (a, b))
    result, gain_sum, bias_sum = first_norm_backward(info[0], x, du_kept, du_sent, dh_kept, dh_taken, gains)

    @pl.when(step == 0)
    def _():
        small[...] = jnp.zeros_like(small)

    small[0:1] += gain_sum
    small[1:2] += bias_sum
    put_pieces(step, steps, (first_out, second_out), result)


def call(kernel, grid, in_specs, out_specs, out_shapes, scratch, flops, moved, name, vmem=56):
    return pl.pallas_call(
        kernel,
        grid_spec=pltpu.PrefetchScalarGridSpec(
            num_scalar_prefetch=1,
            grid=(grid,),
            in_specs=in_specs,
            out_specs=out_specs,
            scratch_shapes=scratch,
        ),
        out_shape=out_shapes,
        compiler_params=pltpu.CompilerParams(vmem_limit_bytes=vmem * 2**20),
        cost_estimate=pl.CostEstimate(flops=int(flops), bytes_accessed=int(moved), transcendentals=0),
        name=name,
    )


class Plan:
    def __init__(self, quarter, width, hidden):
        self.quarter, self.width, self.hidden = quarter, width, hidden
        self.steps = 2 * quarter // ROWS
        per_piece = quarter // ROWS
        half = width // 2

        def local(j, s):
            return (j, 0, 0)

        def canonical(j, s):
            return (((j // per_piece) ^ s[1]) * per_piece + j % per_piece, 0, 0)

        self.row = pl.BlockSpec((ROWS, GRID, width), local)
        self.wide_row = pl.BlockSpec((ROWS, GRID, hidden), local)
        self.half_row = pl.BlockSpec((ROWS, GRID, half), canonical)
        self.first = pl.BlockSpec((ROWS, GRID, width), lambda j, s: (jnp.minimum(j, per_piece - 1), 0, 0))
        self.second = pl.BlockSpec((ROWS, GRID, width), lambda j, s: (jnp.maximum(j - per_piece, 0), 0, 0))
        self.half_shape = jax.ShapeDtypeStruct((2 * quarter, GRID, half), F32)
        self.row_shape = jax.ShapeDtypeStruct((2 * quarter, GRID, width), F32)
        self.wide_shape = jax.ShapeDtypeStruct((2 * quarter, GRID, hidden), F32)
        self.piece_shape = jax.ShapeDtypeStruct((quarter, GRID, width), F32)

    def norm(self, layer):
        return pl.BlockSpec((None, 2, self.width), lambda j, s: (layer, 0, 0))

    def matrix(self, layer, rows, columns):
        return pl.BlockSpec((None, rows, columns), lambda j, s: (layer, 0, 0))

    def whole(self, shape):
        return pl.BlockSpec(shape, lambda j, s: (0,) * len(shape))


def first_norm(plan, info, a, b, gains, biases):
    return call(
        functools.partial(first_norm_kernel, plan.steps),
        plan.steps,
        [plan.first, plan.second, plan.norm(0), plan.norm(0)],
        [plan.half_row, plan.half_row],
        [plan.half_shape, plan.half_shape],
        [],
        0,
        4 * 2**20 * 2,
        "first_norm",
    )(info, a, b, gains, biases)


def spectral_specs(layer, width):
    block = width // BLOCKS
    cells = pl.BlockSpec((GRID // 2, GRID, block), lambda b, s: (0, 0, b))
    weight = pl.BlockSpec((None, 2, 2, None, block, block), lambda b, s: (layer, 0, 0, 2 * s[0] + b, 0, 0))
    offset = pl.BlockSpec((None, 2, 2, BLOCKS, block), lambda b, s: (layer, 0, 0, 0, 0))
    table = pl.BlockSpec((GRID, 4 * GRID), lambda b, s: (0, 0))
    modes = pl.BlockSpec((None, MODES * MODES, 2 * block), lambda b, s: (b, 0, 0))
    modes_shape = jax.ShapeDtypeStruct((2, MODES * MODES, 2 * block), F32)
    planes = pltpu.VMEM((MODES // 2 + 1, GRID, 2 * block), F32)
    flowing = pltpu.VMEM((MODES * MODES, 2 * block), F32)
    stacked = pltpu.VMEM((2, 2 * block, 2 * block), F32)
    return block, cells, weight, offset, table, modes, modes_shape, planes, flowing, stacked


def spectral_forward(plan, layer, info, own, recv, weight_all, offset_all, tables):
    block, cells, weight, offset, table, modes, modes_shape, planes, flowing, stacked = spectral_specs(layer, plan.width)
    return call(
        spectral_forward_kernel,
        2,
        [cells, cells, weight, offset, table, table],
        [cells, cells, modes, modes, modes],
        [plan.half_shape, plan.half_shape, modes_shape, modes_shape, modes_shape],
        [planes, flowing, stacked],
        3 * 2e9,
        14 * 2**20,
        f"spectral_forward_{layer}",
    )(info, own, recv, weight_all, offset_all, tables[0], tables[3])


def spectral_backward(plan, layer, info, own, recv, weight_all, saved, tables):
    block, cells, weight, offset, table, modes, modes_shape, planes, flowing, stacked = spectral_specs(layer, plan.width)
    return call(
        spectral_backward_kernel,
        2,
        [cells, cells, weight, modes, modes, modes, table, table],
        [
            cells,
            cells,
            pl.BlockSpec((2, 2, None, block, block), lambda b, s: (0, 0, b, 0, 0)),
            pl.BlockSpec((2, 2, None, 1, block), lambda b, s: (0, 0, b, 0, 0)),
        ],
        [
            plan.half_shape,
            plan.half_shape,
            jax.ShapeDtypeStruct((2, 2, 2, block, block), F32),
            jax.ShapeDtypeStruct((2, 2, 2, 1, block), F32),
        ],
        [planes, flowing, stacked, pltpu.VMEM((2, 2 * block, 2 * block), F32)],
        3 * 4e9,
        14 * 2**20,
        f"spectral_backward_{layer}",
    )(info, own, recv, weight_all, *saved, tables[1], tables[2])


def ffn_forward(plan, layer, more, info, x, kept, taken, gains, biases, up, up_offset, down, down_offset):
    width, hidden = plan.width, plan.hidden
    specs = [plan.first, plan.second] if len(x) == 2 else [plan.row]
    specs += [plan.half_row, plan.half_row, plan.norm(layer), plan.norm(layer)]
    specs += [plan.matrix(layer, width, hidden), plan.whole(up_offset.shape)]
    specs += [plan.matrix(layer, hidden, width), plan.whole(down_offset.shape)]
    args = [*x, kept, taken, gains, biases, up, up_offset, down, down_offset]
    out_specs = [plan.row, plan.wide_row]
    out_shapes = [plan.row_shape, plan.wide_shape]
    if more:
        specs += [plan.norm(layer + 1), plan.norm(layer + 1)]
        args += [gains, biases]
        out_specs += [plan.row, plan.half_row, plan.half_row]
        out_shapes += [plan.row_shape, plan.half_shape, plan.half_shape]
    else:
        out_specs += [plan.first, plan.second]
        out_shapes += [plan.piece_shape, plan.piece_shape]
    return call(
        functools.partial(ffn_forward_kernel, plan.steps, layer, len(x), more),
        plan.steps,
        specs,
        out_specs,
        out_shapes,
        [],
        3 * 4 * 2048 * width * hidden,
        24 * 2**20,
        f"ffn_forward_{layer}",
    )(info, *args)


def ffn_backward(plan, layer, info, mixed, before, gains, biases, up, down, grads):
    width, hidden = plan.width, plan.hidden
    fused = len(grads) == 5
    packed = (width // 128, hidden + 8, 128)
    packed = [packed, packed] if layer == 0 else [(2, *packed)]
    specs = [plan.row, plan.wide_row, plan.norm(layer), plan.norm(layer)]
    specs += [plan.matrix(layer, width, hidden), plan.matrix(layer, hidden, width)]
    args = [mixed, before, gains, biases, up, down, *grads]
    if fused:
        specs += [plan.row] + [plan.half_row] * 4 + [plan.norm(layer + 1)]
        args += [gains]
    else:
        specs += [plan.first, plan.second]
    return call(
        functools.partial(ffn_backward_kernel, plan.steps, fused, layer == 0),
        plan.steps,
        specs,
        [
            plan.half_row,
            plan.half_row,
            *[plan.whole(shape) for shape in packed],
        ],
        [
            plan.half_shape,
            plan.half_shape,
            *[jax.ShapeDtypeStruct(shape, F32) for shape in packed],
        ],
        [pltpu.VMEM(shape, F32) for shape in ((width, hidden), (hidden, width), (8, width))],
        3 * 8 * 2048 * width * hidden,
        24 * 2**20,
        f"ffn_backward_{layer}",
    )(info, *args)


def input_gradient(plan, info, a, b, du, dh, gains):
    return call(
        functools.partial(input_grad_kernel, plan.steps),
        plan.steps,
        [plan.first, plan.second] + [plan.half_row] * 4 + [plan.norm(0)],
        [plan.first, plan.second, plan.whole((8, plan.width))],
        [plan.piece_shape, plan.piece_shape, jax.ShapeDtypeStruct((8, plan.width), F32)],
        [],
        0,
        16 * 2**20,
        "input_gradient",
    )(info, a, b, *du, *dh, gains)


def item_routes(wide, section):
    routes = []
    for flip in range(2):
        pairs = []
        for w in range(wide):
            c = w % 2
            for z in range(section):
                pairs.append((w * section + z, (w - c + z // 2) * section + 2 * c + (z % 2 ^ flip)))
        routes.append(pairs)
    return routes


def copy_kernel(info, source, *refs):
    refs[-1][...] = source[...]


def pick(info, shard, flip, after=()):
    items, rows, *cell = shard.shape
    anywhere = pl.BlockSpec(memory_space=pl.ANY)
    return call(
        copy_kernel,
        rows // ROWS,
        [pl.BlockSpec((None, ROWS, *cell), lambda j, s: (s[1] ^ flip, j, 0, 0))] + [anywhere] * len(after),
        pl.BlockSpec((ROWS, *cell), lambda j, s: (j, 0, 0)),
        jax.ShapeDtypeStruct((rows, *cell), F32),
        [],
        0,
        0,
        "pick",
        16,
    )(info, shard, *after)


def pass_kernel(count, *refs):
    pass


def passed(values, after):
    anywhere = pl.BlockSpec(memory_space=pl.ANY)
    return pl.pallas_call(
        functools.partial(pass_kernel, len(values)),
        in_specs=[anywhere] * (len(values) + len(after)),
        out_specs=[anywhere] * len(values),
        out_shape=[jax.ShapeDtypeStruct(v.shape, v.dtype) for v in values],
        input_output_aliases={i: i for i in range(len(values))},
        name="passed",
    )(*values, *after)


def send_piece(piece, route):
    return lax.ppermute(piece, BOTH, route)


def join_kernel(steps, info, first, second, *refs):
    step = pl.program_id(0)
    from_first = (step // steps) == info[1]
    refs[-1][...] = jnp.where(from_first, first[...], second[...])


def join(info, first, second, after=()):
    rows, *cell = first.shape
    steps = rows // ROWS
    anywhere = pl.BlockSpec(memory_space=pl.ANY)

    def piece(flip):
        def place(j, s):
            return (jnp.where(j // steps == s[1] ^ flip, j % steps, (1 - j // steps) * (steps - 1)), 0, 0)

        return pl.BlockSpec((ROWS, *cell), place)

    return call(
        functools.partial(join_kernel, steps),
        2 * steps,
        [piece(0), piece(1)] + [anywhere] * len(after),
        pl.BlockSpec((None, ROWS, *cell), lambda j, s: (j // steps, j % steps, 0, 0)),
        jax.ShapeDtypeStruct((2, rows, *cell), F32),
        [],
        0,
        0,
        "join",
        16,
    )(info, first, second, *after)


def as_one(function, *args):
    def empty(*args):
        return jax.tree.map(lambda leaf: jnp.zeros(leaf.shape, leaf.dtype), jax.eval_shape(function, *args))

    return lax.cond(lax.axis_index("wide") < lax.axis_size("wide"), function, empty, *args)


def swap(values):
    return lax.ppermute(values, "wide", [(i, i ^ 1) for i in range(lax.axis_size("wide"))])


def digits(size, low, most):
    found = []
    while 1 << low < size:
        radix = most if most << low <= size else 2
        found.append((low, radix))
        low += radix.bit_length() - 1
    return found


def partners(axis, bit, offset):
    return [(i, i ^ offset << bit) for i in range(lax.axis_size(axis))]


def sum_spread(values, axis, bit, radix):
    me = (lax.axis_index(axis) >> bit) % radix
    parts = values.reshape((radix, -1) + values.shape[1:])
    total = lax.dynamic_index_in_dim(parts, me, 0, keepdims=False)
    for offset in range(1, radix):
        part = lax.dynamic_index_in_dim(parts, me ^ offset, 0, keepdims=False)
        total = total + lax.ppermute(part, axis, partners(axis, bit, offset))
    return total


def collect(values, axis, bit, radix):
    me = (lax.axis_index(axis) >> bit) % radix
    out = jnp.zeros((radix,) + values.shape, F32)
    for offset in range(radix):
        got = lax.ppermute(values, axis, partners(axis, bit, offset)) if offset else values
        out = lax.dynamic_update_index_in_dim(out, got, me ^ offset, 0)
    return out.reshape((-1,) + values.shape[1:])


def spread_steps(axis, low, most):
    return [(axis, *digit) for digit in digits(lax.axis_size(axis), low, most)]


def sum_spread_all(values, steps):
    for step in steps:
        values = sum_spread(values, *step)
    return values


def collect_all(values, steps):
    for step in steps[::-1]:
        values = collect(values, *step)
    return values


def packed_rows(parts, unit):
    rows = [part.reshape(-1, 128) for part in parts]
    missing = -sum(row.shape[0] for row in rows) % unit
    return jnp.concatenate(rows + [jnp.zeros((missing, 128), F32)])


def unpack_kernel(cuts, info, mine, other, second, *outs):
    gain_out, bias_out, mix_out, offset_out, up_out, up_offset_out, down_out, down_offset_out = outs
    core = info[0]
    low = jnp.where(core == 0, mine[...], other[...])
    high = jnp.where(core == 0, other[...], mine[...])
    width = up_out.shape[1]
    rows, lanes = width + 8, width // 128
    down_at, mix_at = lanes * rows, 2 * lanes * rows
    for index in range(lanes):
        at = pl.ds(index * 128, 128)
        begin = index * rows
        up_out[0, :, at] = low[begin : begin + width]
        down_out[0, :, at] = high[begin : begin + width]
        up_out[1, :, at] = second[begin : begin + width]
        down_out[1, :, at] = second[down_at + begin : down_at + begin + width]
        small = low[begin + width : begin + rows]
        late = second[begin + width : begin + rows]
        inner = [low[row : row + 1] + high[row : row + 1] for row in (cuts[3] + index, cuts[3] + lanes + index)]
        gain_out[0, 0:1, at] = inner[0]
        bias_out[0, 0:1, at] = inner[1]
        gain_out[0, 1:2, at] = small[0:1]
        bias_out[0, 1:2, at] = small[1:2]
        gain_out[1, 0:1, at] = small[4:5]
        bias_out[1, 0:1, at] = small[5:6]
        gain_out[1, 1:2, at] = late[0:1]
        bias_out[1, 1:2, at] = late[1:2]
        up_offset_out[0:1, at] = small[2:3]
        up_offset_out[1:2, at] = late[2:3]
        down_offset_out[0:1, at] = small[3:4]
        down_offset_out[1:2, at] = late[3:4]
    mix_rows = mix_out[1].size // 128
    mix_out[1] = second[mix_at : mix_at + mix_rows].reshape(mix_out.shape[1:])
    for j in range(2):
        for part in range(2):
            begin = mix_at + mix_rows + (2 * j + part) * BLOCKS
            offset_out[1, j, part] = second[begin : begin + BLOCKS]
            for block in range(2):
                index = (2 * j + part) * 2 + block
                begin = cuts[1] + index * 128
                mix_out[0, j, part, block] = low[begin : begin + 128]
                mix_out[0, j, part, 2 + block] = high[begin : begin + 128]
                begin = cuts[2] + index
                offset_out[0, j, part, block : block + 1] = low[begin : begin + 1]
                offset_out[0, j, part, 2 + block : 3 + block] = high[begin : begin + 1]


def unpack(info, cuts, args, shapes):
    def whole(shape):
        return pl.BlockSpec(shape, lambda j, s: (0,) * len(shape))

    return call(
        functools.partial(unpack_kernel, cuts),
        1,
        [whole(arg.shape) for arg in args],
        [whole(shape) for shape in shapes],
        [jax.ShapeDtypeStruct(shape, F32) for shape in shapes],
        [],
        0,
        0,
        "unpack",
        40,
    )(info, *args)


def whole_blocks(core, part):
    empty = jnp.zeros_like(part)
    return jnp.where(core == 0, jnp.concatenate([part, empty], 2), jnp.concatenate([empty, part], 2))


def on_device(
    inputs,
    norm_gain,
    norm_bias,
    mix_weight,
    mix_bias,
    up_weight,
    up_bias,
    down_weight,
    down_bias,
    out_grad,
):
    width, hidden = up_weight.shape[1:]
    plan = Plan(inputs.shape[1], width, hidden)
    routes = item_routes(lax.axis_size("wide"), lax.axis_size("section"))
    core = lax.axis_index("wide") % 2
    parity = lax.axis_index("section") % 2
    info = jnp.stack([core, parity]).astype(jnp.int32)
    plain, weighted = column_tables()
    tables = [jnp.asarray(split_table(t)) for t in (plain, weighted, plain.T, weighted.T)]

    back_routes = [[(b, a) for a, b in route] for route in routes]
    ffn_args = (norm_gain, norm_bias, up_weight, up_bias, down_weight, down_bias)
    back_args = (norm_gain, norm_bias, up_weight, down_weight)

    def forward(xa, xb):
        keep, send = first_norm(plan, info, xa, xb, norm_gain, norm_bias)
        keep, send, *saved0 = spectral_forward(plan, 0, info, keep, swap(send), mix_weight, mix_bias, tables)
        u0, a0, x1, keep, send = ffn_forward(plan, 0, True, info, (xa, xb), keep, swap(send), *ffn_args)
        keep, send, *saved1 = spectral_forward(plan, 1, info, keep, swap(send), mix_weight, mix_bias, tables)
        u1, a1, va, vb = ffn_forward(plan, 1, False, info, (x1,), keep, swap(send), *ffn_args)
        return (va, vb), (saved0, u0, a0, x1, saved1, u1, a1)

    def backward(xa, xb, ga, gb, saved):
        saved0, u0, a0, x1, saved1, u1, a1 = saved
        keep, send, matrices = ffn_backward(plan, 1, info, u1, a1, *back_args, (ga, gb))
        dh_keep, dh_send, mix, offsets = spectral_backward(plan, 1, info, keep, swap(send), mix_weight, saved1, tables)
        late = (x1, keep, send, dh_keep, swap(dh_send))
        mixing = [whole_blocks(core, part).reshape(-1, 128) for part in (mix, offsets)]
        second = packed_rows([matrices, *mixing], lax.axis_size("wide") * lax.axis_size("section") * 8)
        second = lax.psum_scatter(second, "wide", scatter_dimension=0, tiled=True)
        return *as_one(backward_first, xa, xb, late, (saved0, u0, a0)), second

    def backward_first(xa, xb, late, saved):
        saved0, u0, a0 = saved
        keep, send, *matrices = ffn_backward(plan, 0, info, u0, a0, *back_args, late)
        dh_keep, dh_send, mix, offsets = spectral_backward(plan, 0, info, keep, swap(send), mix_weight, saved0, tables)
        last = ((keep, send), (dh_keep, swap(dh_send)))
        dxa, dxb, inner = input_gradient(plan, info, xa, xb, *last, norm_gain)
        return (dxa, dxb), (matrices, mix, offsets, inner)

    members = spread_steps("wide", 1, 4)
    sections = spread_steps("section", 0, 2)

    def reduce_gradients(matrices, mix, offsets, inner, second):
        mine = matrices[0] + swap(matrices[1])
        parts = [mine, mix, offsets, inner.reshape(8, -1, 128)]
        unit = lax.axis_size("wide") // 2 * lax.axis_size("section") * 8
        first = sum_spread_all(packed_rows(parts, unit), members)
        both = sum_spread_all(jnp.stack([first, second], axis=1).reshape(-1, 2, 128), sections)
        both = collect_all(both, sections)
        return both[:, 0], both[:, 1]

    def share_first(first, outputs):
        summed = collect_all(first, members)
        return join(info, *outputs), summed, swap(summed)

    def share_gradients(first, second, outputs):
        second = lax.all_gather(second, "wide", axis=0, tiled=True)
        return *as_one(share_first, first, outputs), second

    xa = send_piece(pick(info, inputs, 0), routes[0])
    xb = send_piece(pick(info, inputs, 1), routes[1])
    picked_grads = pick(info, out_grad, 0), pick(info, out_grad, 1)
    ga, gb = [send_piece(piece, route) for piece, route in zip(passed(picked_grads, (xa, xb)), routes)]
    results, saved = as_one(forward, xa, xb)
    outputs = [send_piece(piece, route) for piece, route in zip(passed(results, (ga, gb)), back_routes)]
    (dxa, dxb), local, second = as_one(backward, xa, xb, ga, gb, saved)
    dxa = send_piece(*passed([dxa], outputs), back_routes[0])
    first, second = as_one(reduce_gradients, *local, second)
    dxb = send_piece(*passed([dxb], [dxa, first]), back_routes[1])
    outputs, mine, other, second = as_one(share_gradients, first, second, outputs)

    sizes = [part.size // 128 for part in (local[0][0], local[1], local[2])]
    cuts = [0, sizes[0], sizes[0] + sizes[1], sum(sizes)]
    args = [mine, other, second]
    shapes = [a.shape for a in (norm_gain, norm_bias, mix_weight, mix_bias, up_weight, up_bias, down_weight, down_bias)]
    gradients = unpack(info, cuts, args, shapes)
    return (outputs, join(info, dxa, dxb, gradients[:1]), *gradients)


def solution(mesh):
    cells = P("wide", "section", None, None)
    return jax.shard_map(
        on_device,
        mesh=mesh,
        in_specs=(cells, P(), P(), P(), P(), P(), P(), P(), P(), cells),
        out_specs=(cells, cells, P(), P(), P(), P(), P(), P(), P(), P()),
        check_vma=False,
    )
```

```python
import functools
import math

import jax
import jax.numpy as jnp
import numpy as np
from jax import lax
from jax.experimental import pallas as pl
from jax.experimental.pallas import tpu as pltpu
from jax.sharding import PartitionSpec as P

BLOCKS = 4
GRID = 64
MODES = 32
EPSILON = 1e-05
THRESHOLD = 0.05
ROWS = 8
SMALL_ROWS = 32
F32 = jnp.float32
BF16 = jnp.bfloat16
BOTH = ("wide", "section")


def split_table(table):
    table = table.astype(np.float32)
    high = table.astype(jnp.bfloat16)
    low = (table - high.astype(np.float32)).astype(jnp.bfloat16)
    return np.concatenate([high, high, low, low], axis=1)


def column_tables():
    columns = np.arange(MODES)
    angles = 2.0 * math.pi * (columns[:, None] * np.arange(GRID)[None, :] % GRID) / GRID
    plain = np.concatenate([np.cos(angles), np.sin(angles)], axis=0) / GRID
    factor = np.where(columns == 0, 1.0, 2.0)
    weighted = plain * np.concatenate([factor, factor])[:, None]
    return plain, weighted


def twiddle(index, length):
    angle = 2.0 * math.pi * index / length
    return math.cos(angle), math.sin(angle)


def half_spectrum(planes, pruned=False):
    length = len(planes)
    if length == 2:
        return [(planes[0] + planes[1], None), (planes[0] - planes[1], None)]
    even = half_spectrum(planes[0::2])
    odd = half_spectrum(planes[1::2])
    quarter = length // 4
    first, second = [], []
    for k in range(quarter + 1):
        (er, ei), (dr, di) = even[k], odd[k]
        if k == 0:
            first.append((er + dr, None))
            second.append((er - dr, None))
            continue
        if k == quarter:
            first.append((er, -dr))
            continue
        c, s = twiddle(k, length)
        if 2 * k == quarter:
            tr, ti = (dr + di) * c, (di - dr) * c
        else:
            tr, ti = dr * c + di * s, di * c - dr * s
        first.append((er + tr, ei + ti))
        second.append((er - tr, ti - ei))
    if pruned:
        return first
    return first + second[::-1]


def half_synthesis(spectrum, length, pruned=False):
    if length == 2:
        (a, _), (b, _) = spectrum
        return [a + b, a - b]
    quarter = length // 4
    even, odd = [], []
    for k in range(quarter + 1):
        ar, ai = spectrum[k]
        if k == quarter:
            even.append((ar, None))
            odd.append((-ai, None))
            continue
        if k == 0:
            if pruned:
                even.append((ar, None))
                odd.append((ar, None))
            else:
                br = spectrum[length // 2][0]
                even.append((ar + br, None))
                odd.append((ar - br, None))
            continue
        if pruned:
            sr, si, tr, ti = ar, ai, ar, ai
        else:
            br, bi = spectrum[length // 2 - k]
            sr, si, tr, ti = ar + br, ai - bi, ar - br, ai + bi
        even.append((sr, si))
        c, s = twiddle(k, length)
        if 2 * k == quarter:
            odd.append(((tr - ti) * c, (ti + tr) * c))
        else:
            odd.append((tr * c - ti * s, ti * c + tr * s))
    even_planes = half_synthesis(even, length // 2)
    odd_planes = half_synthesis(odd, length // 2)
    planes = []
    for e, o in zip(even_planes, odd_planes):
        planes += [e, o]
    return planes


def exact_dot(left, right, left_dim, right_dim):
    return lax.dot_general(
        left,
        right,
        (((left_dim,), (right_dim,)), ((), ())),
        precision=lax.Precision.HIGH,
        preferred_element_type=F32,
    )


def split(values):
    high = values.astype(BF16)
    low = (values - high.astype(F32)).astype(BF16)
    return high, low


def table_dot(table, values):
    high, low = split(values)
    stacked = jnp.concatenate([high, low, high, low], axis=0)
    return jnp.dot(table, stacked, preferred_element_type=F32)


def gelu(values):
    return 0.5 * values * (1.0 + lax.erf(values * math.sqrt(0.5)))


def gelu_and_slope(values):
    cumulative = 0.5 * (1.0 + lax.erf(values * math.sqrt(0.5)))
    density = jnp.exp(-0.5 * values * values) * (1.0 / math.sqrt(2.0 * math.pi))
    return values * cumulative, cumulative + values * density


def normalise(values):
    average = jnp.mean(values, axis=-1, keepdims=True)
    centered = values - average
    variance = jnp.mean(centered * centered, axis=-1, keepdims=True)
    scale = lax.rsqrt(variance + EPSILON)
    return centered * scale, scale


def norm_backward(grad, unit, scale, gains):
    inner = grad * gains
    mean_inner = jnp.mean(inner, axis=-1, keepdims=True)
    mean_unit = jnp.mean(inner * unit, axis=-1, keepdims=True)
    return scale * (inner - mean_inner - unit * mean_unit)


def column_sum(values):
    return jnp.sum(values, axis=0, keepdims=True)


def joined(core, kept, other):
    shape = (kept.shape[0] * kept.shape[1], kept.shape[2])
    kept, other = kept[...].reshape(shape), other[...].reshape(shape)
    first = jnp.where(core == 0, kept, other)
    second = jnp.where(core == 0, other, kept)
    return jnp.concatenate([first, second], axis=1)


def parted(core, values, kept, other):
    half = values.shape[1] // 2
    first, second = values[:, :half], values[:, half:]
    kept[...] = jnp.where(core == 0, first, second).reshape(kept.shape)
    other[...] = jnp.where(core == 0, second, first).reshape(other.shape)


def flat(ref):
    return ref[...].reshape(-1, ref.shape[-1])


def picked(info, step, steps, refs):
    if len(refs) == 1:
        return flat(refs[0])
    own, first, second = refs
    first = jnp.where(info[2] == 1, flat(own), flat(first))
    return jnp.where(step < steps // 2, first, flat(second))


def put_pieces(step, steps, refs, values):
    if len(refs) == 1:
        refs[0][...] = values.reshape(refs[0].shape)
        return

    @pl.when(step < steps // 2)
    def _():
        refs[0][...] = values.reshape(refs[0].shape)

    @pl.when(step >= steps // 2)
    def _():
        refs[1][...] = values.reshape(refs[1].shape)


def analyse(own, recv, table, sign, planes, modes):
    def rows(index, _):
        at = pl.ds(pl.multiple_of(index * 8, 8), 8)
        loaded = [own[p, at, :] for p in range(GRID // 2)] + [recv[p, at, :] for p in range(GRID // 2)]
        for k, (re, im) in enumerate(half_spectrum(loaded, pruned=True)):
            im = jnp.zeros_like(re) if im is None else im
            if k % 2:
                re, im = re * sign, im * sign
            planes[k, at, :] = jnp.concatenate([re, im], axis=1)
        return 0

    lax.fori_loop(0, GRID // 8, rows, 0)
    for k in range(MODES // 2 + 1):
        found = table_dot(table[...], planes[k])
        lanes = found.shape[1] // 2
        cr, ci = found[:MODES, :lanes], found[:MODES, lanes:]
        sr, si = found[MODES:, :lanes], found[MODES:, lanes:]
        if k < MODES // 2:
            modes[k * MODES : (k + 1) * MODES, :] = jnp.concatenate([cr + si, ci - sr], axis=1)
        if k > 0:
            place = MODES - k
            modes[place * MODES : (place + 1) * MODES, :] = jnp.concatenate([cr - si, -ci - sr], axis=1)


def synthesise(modes, table, sign, planes, keep, send):
    lanes = modes.shape[1] // 2
    for k in range(MODES // 2 + 1):
        place = MODES - k
        if k == 0:
            above, below = modes[0:MODES, :], None
            total, apart = above, above
        elif k == MODES // 2:
            below = modes[place * MODES : (place + 1) * MODES, :]
            total, apart = below, -below
        else:
            above = modes[k * MODES : (k + 1) * MODES, :]
            below = modes[place * MODES : (place + 1) * MODES, :]
            total, apart = above + below, above - below
        upper = jnp.concatenate([total[:, :lanes], apart[:, lanes:]], axis=1)
        lower = jnp.concatenate([-total[:, lanes:], apart[:, :lanes]], axis=1)
        planes[k] = table_dot(table[...], jnp.concatenate([upper, lower], axis=0))

    def rows(index, _):
        at = pl.ds(pl.multiple_of(index * 8, 8), 8)
        spectrum = []
        for k in range(MODES // 2 + 1):
            both = planes[k, at, :]
            if k % 2:
                both = both * sign
            spectrum.append((both[:, :lanes], both[:, lanes:]))
        cells = half_synthesis(spectrum, GRID, pruned=True)
        for p in range(GRID // 2):
            keep[p, at, :] = cells[p]
            send[p, at, :] = cells[GRID // 2 + p]
        return 0

    lax.fori_loop(0, GRID // 8, rows, 0)


def place_weights(weight, stacked):
    lanes = weight.shape[-1]
    for j in range(2):
        real, imag = weight[j, 0], weight[j, 1]
        stacked[j, :lanes, :lanes] = real
        stacked[j, :lanes, lanes:] = imag
        stacked[j, lanes:, :lanes] = -imag
        stacked[j, lanes:, lanes:] = real


MIX_ROWS = 256


def mix_offsets(offset, block):
    at = pl.ds(block, 1)
    return [jnp.concatenate([offset[j, 0, at, :], offset[j, 1, at, :]], axis=1) for j in range(2)]


def spectral_forward_kernel(
    info, own, recv, weight, offset, table_in, table_out, keep, send, modes, before, after, planes, shrunk, stacked
):
    core = info[0]
    sign = jnp.where(core == 1, -1.0, 1.0).astype(F32)
    place_weights(weight, stacked)
    first_offset, second_offset = mix_offsets(offset, 2 * core + pl.program_id(0))
    analyse(own, recv, table_in, sign, planes, modes)

    def mix(index, _):
        at = pl.ds(pl.multiple_of(index * MIX_ROWS, MIX_ROWS), MIX_ROWS)
        first = exact_dot(modes[at, :], stacked[0], 1, 0) + first_offset
        before[at, :] = first
        second = exact_dot(gelu(first), stacked[1], 1, 0) + second_offset
        after[at, :] = second
        shrunk[at, :] = second - THRESHOLD * jnp.tanh(second * (1.0 / THRESHOLD))
        return 0

    lax.fori_loop(0, MODES * MODES // MIX_ROWS, mix, 0)
    synthesise(shrunk, table_out, sign, planes, keep, send)


def spectral_backward_kernel(
    start, info, own, recv, weight, modes, before, after, table_in, table_out, *refs
):
    if start is None:
        keep, send, weight_grad, offset_grad, planes, flowing, stacked, summed = refs
    else:
        _, keep, send, out, planes, flowing, stacked, summed, weight_grad, offset_grad, blank, sems = refs
    core = info[0]
    sign = jnp.where(core == 1, -1.0, 1.0).astype(F32)
    place_weights(weight, stacked)
    analyse(own, recv, table_in, sign, planes, flowing)
    summed[...] = jnp.zeros_like(summed)

    def mix(index, totals):
        at = pl.ds(pl.multiple_of(index * MIX_ROWS, MIX_ROWS), MIX_ROWS)
        ratio = jnp.tanh(after[at, :] * (1.0 / THRESHOLD))
        grad_second = flowing[at, :] * ratio * ratio
        hidden, slope = gelu_and_slope(before[at, :])
        summed[1] += exact_dot(hidden, grad_second, 0, 0)
        grad_first = exact_dot(grad_second, stacked[1], 1, 1) * slope
        summed[0] += exact_dot(modes[at, :], grad_first, 0, 0)
        flowing[at, :] = exact_dot(grad_first, stacked[0], 1, 1)
        return totals[0] + column_sum(grad_first), totals[1] + column_sum(grad_second)

    empty = jnp.zeros((1, flowing.shape[1]), F32)
    totals = lax.fori_loop(0, MODES * MODES // MIX_ROWS, mix, (empty, empty))
    lanes = flowing.shape[1] // 2
    offset_grad[...] = jnp.zeros_like(offset_grad)
    for j in range(2):
        offset_grad[2 * j : 2 * j + 1] = totals[j][:, :lanes]
        offset_grad[2 * j + 1 : 2 * j + 2] = totals[j][:, lanes:]
        weight_grad[j, 0] = summed[j, :lanes, :lanes] + summed[j, lanes:, lanes:]
        weight_grad[j, 1] = summed[j, :lanes, lanes:] - summed[j, lanes:, :lanes]
    if start is not None:
        block, other = 2 * core + pl.program_id(0), 2 * (1 - core) + pl.program_id(0)
        blank[...] = jnp.zeros_like(blank)
        copies = []
        for index in range(4):
            for source, place in ((weight_grad.at[index // 2, index % 2], block), (blank, other)):
                at = pl.ds(pl.multiple_of(start + (index * BLOCKS + place) * 128, 8), 128)
                copies.append(pltpu.make_async_copy(source, out.at[at], sems.at[len(copies)]))
        for source, place in ((offset_grad, block), (blank.at[pl.ds(0, 8)], other)):
            at = pl.ds(pl.multiple_of(start + 4 * BLOCKS * 128 + place * 8, 8), 8)
            copies.append(pltpu.make_async_copy(source, out.at[at], sems.at[len(copies)]))
        for copy in copies:
            copy.start()
    synthesise(flowing, table_out, sign, planes, keep, send)
    if start is not None:
        for copy in copies:
            copy.wait()


def first_norm_kernel(steps, info, own, a, b, gains, biases, keep, send):
    unit, _ = normalise(picked(info, pl.program_id(0), steps, (own, a, b)))
    parted(info[0], unit * gains[0:1] + biases[0:1], keep, send)


def ffn_forward_kernel(steps, layer, pieces, more, info, *refs):
    step = pl.program_id(0)
    refs = list(refs)
    x_refs, refs = refs[:pieces], refs[pieces:]
    kept, taken, gains, biases, up, up_offset, down, down_offset = refs[:8]
    refs = refs[8:]
    core = info[0]
    mixed = picked(info, step, steps, x_refs) + joined(core, kept, taken)
    unit, _ = normalise(mixed)
    normed = unit * gains[1:2] + biases[1:2]
    before = exact_dot(normed, up[...], 1, 0) + up_offset[layer : layer + 1]
    result = mixed + exact_dot(gelu(before), down[...], 1, 0) + down_offset[layer : layer + 1]
    if more:
        next_gains, next_biases, mixed_out, before_out, result_out, keep, send = refs
        put_pieces(step, steps, (result_out,), result)
        unit, _ = normalise(result)
        parted(core, unit * next_gains[0:1] + next_biases[0:1], keep, send)
    else:
        mixed_out, before_out, first_out, second_out = refs
        put_pieces(step, steps, (first_out, second_out), result)
    mixed_out[...] = mixed.reshape(mixed_out.shape)
    before_out[...] = before.reshape(before_out.shape)


def first_norm_backward(core, x, du_kept, du_sent, dh_kept, dh_taken, gains):
    grad = joined(core, dh_kept, dh_taken)
    unit, scale = normalise(x)
    result = joined(core, du_kept, du_sent) + norm_backward(grad, unit, scale, gains[0:1])
    return result, column_sum(grad * unit), column_sum(grad)


def lanes_first(values):
    return [values[:, at : at + 128] for at in range(0, values.shape[1], 128)]


def ffn_backward_kernel(steps, fused, info, *refs):
    step = pl.program_id(0)
    core = info[0]
    refs = list(refs)
    mixed, before, gains, biases, up, down = refs[:6]
    if fused:
        x, du_kept, du_sent, dh_kept, dh_taken, next_gains = refs[6:12]
        grad, late_gain, late_bias = first_norm_backward(core, flat(x), du_kept, du_sent, dh_kept, dh_taken, next_gains)
        refs = refs[12:]
    else:
        grad = picked(info, step, steps, refs[6:9])
        refs = refs[9:]
    keep, send, *packed, up_grad, down_grad, small = refs
    if not fused:
        out, lined, sem, up_grad, down_grad, small = packed + [up_grad, down_grad, small]
    kept_grads, sent_grads = packed if fused else (lined.at[0], lined.at[1])

    @pl.when(step == 0)
    def _():
        up_grad[...] = jnp.zeros_like(up_grad)
        down_grad[...] = jnp.zeros_like(down_grad)
        small[...] = jnp.zeros_like(small)

    unit, scale = normalise(flat(mixed))
    normed = unit * gains[1:2] + biases[1:2]
    hidden, slope = gelu_and_slope(flat(before))
    down_grad[...] += exact_dot(hidden, grad, 0, 0)
    inner = exact_dot(grad, down[...], 1, 1) * slope
    up_grad[...] += exact_dot(normed, inner, 0, 0)
    outer = exact_dot(inner, up[...], 1, 1)
    small[0:1] += column_sum(outer * unit)
    small[1:2] += column_sum(outer)
    small[2:3] += column_sum(inner)
    small[3:4] += column_sum(grad)
    if fused:
        small[4:5] += late_gain
        small[5:6] += late_bias
    parted(core, grad + norm_backward(outer, unit, scale, gains[1:2]), keep, send)

    @pl.when(step == steps - 1)
    def _():
        width = up_grad.shape[0]
        parts = zip(lanes_first(up_grad[...]), lanes_first(down_grad[...]), lanes_first(small[...]))
        for index, (a, b, c) in enumerate(parts):
            kept_grads[index, :width] = jnp.where(core == 0, a, b) if fused else a
            sent_grads[index, :width] = jnp.where(core == 0, b, a) if fused else b
            for grads in (kept_grads, sent_grads):
                grads[index, width : width + 8] = c
                grads[index, width + 8 :] = jnp.zeros((SMALL_ROWS - 8, 128), F32)
        if not fused:
            lines = out.at[pl.ds(0, lined.size // 128)].reshape(lined.shape)
            copy = pltpu.make_async_copy(lined, lines, sem)
            copy.start()
            copy.wait()


def input_grad_kernel(steps, info, own, a, b, du_kept, du_sent, dh_kept, dh_taken, gains, first_out, second_out, small):
    step = pl.program_id(0)
    x = picked(info, step, steps, (own, a, b))
    result, gain_sum, bias_sum = first_norm_backward(info[0], x, du_kept, du_sent, dh_kept, dh_taken, gains)

    @pl.when(step == 0)
    def _():
        small[...] = jnp.zeros_like(small)

    small[0:1] += gain_sum
    small[1:2] += bias_sum
    put_pieces(step, steps, (first_out, second_out), result)


def call(kernel, grid, in_specs, out_specs, out_shapes, scratch, flops, moved, name, vmem=56, aliases=None):
    return pl.pallas_call(
        kernel,
        grid_spec=pltpu.PrefetchScalarGridSpec(
            num_scalar_prefetch=1,
            grid=(grid,),
            in_specs=in_specs,
            out_specs=out_specs,
            scratch_shapes=scratch,
        ),
        out_shape=out_shapes,
        input_output_aliases=aliases or {},
        compiler_params=pltpu.CompilerParams(vmem_limit_bytes=vmem * 2**20),
        cost_estimate=pl.CostEstimate(flops=int(flops), bytes_accessed=int(moved), transcendentals=0),
        name=name,
    )


class Plan:
    def __init__(self, quarter, width, hidden):
        self.quarter, self.width, self.hidden = quarter, width, hidden
        self.steps = 2 * quarter // ROWS
        per_piece = quarter // ROWS
        half = width // 2

        def local(j, s):
            return (j, 0, 0)

        def canonical(j, s):
            return (((j // per_piece) ^ s[1]) * per_piece + j % per_piece, 0, 0)

        self.row = pl.BlockSpec((ROWS, GRID, width), local)
        self.wide_row = pl.BlockSpec((ROWS, GRID, hidden), local)
        self.half_row = pl.BlockSpec((ROWS, GRID, half), canonical)
        self.first = pl.BlockSpec((ROWS, GRID, width), lambda j, s: (jnp.minimum(j, per_piece - 1), 0, 0))
        self.pieces = [
            pl.BlockSpec((None, ROWS, GRID, width), lambda j, s: (s[1], jnp.minimum(j, per_piece - 1) * s[2], 0, 0)),
            pl.BlockSpec((ROWS, GRID, width), lambda j, s: (jnp.minimum(j, per_piece - 1) * (1 - s[2]), 0, 0)),
            pl.BlockSpec((ROWS, GRID, width), lambda j, s: (jnp.maximum(j - per_piece, 0), 0, 0)),
        ]
        self.second = pl.BlockSpec((ROWS, GRID, width), lambda j, s: (jnp.maximum(j - per_piece, 0), 0, 0))
        self.half_shape = jax.ShapeDtypeStruct((2 * quarter, GRID, half), F32)
        self.row_shape = jax.ShapeDtypeStruct((2 * quarter, GRID, width), F32)
        self.wide_shape = jax.ShapeDtypeStruct((2 * quarter, GRID, hidden), F32)
        self.piece_shape = jax.ShapeDtypeStruct((quarter, GRID, width), F32)

    def norm(self, layer):
        return pl.BlockSpec((None, 2, self.width), lambda j, s: (layer, 0, 0))

    def matrix(self, layer, rows, columns):
        return pl.BlockSpec((None, rows, columns), lambda j, s: (layer, 0, 0))

    def whole(self, shape):
        return pl.BlockSpec(shape, lambda j, s: (0,) * len(shape))


def first_norm(plan, info, pieces, gains, biases):
    return call(
        functools.partial(first_norm_kernel, plan.steps),
        plan.steps,
        [*plan.pieces, plan.norm(0), plan.norm(0)],
        [plan.half_row, plan.half_row],
        [plan.half_shape, plan.half_shape],
        [],
        0,
        4 * 2**20 * 2,
        "first_norm",
    )(info, *pieces, gains, biases)


def spectral_specs(layer, width):
    block = width // BLOCKS
    cells = pl.BlockSpec((GRID // 2, GRID, block), lambda b, s: (0, 0, b))
    weight = pl.BlockSpec((None, 2, 2, None, block, block), lambda b, s: (layer, 0, 0, 2 * s[0] + b, 0, 0))
    offset = pl.BlockSpec((None, 2, 2, BLOCKS, block), lambda b, s: (layer, 0, 0, 0, 0))
    table = pl.BlockSpec((GRID, 4 * GRID), lambda b, s: (0, 0))
    modes = pl.BlockSpec((None, MODES * MODES, 2 * block), lambda b, s: (b, 0, 0))
    modes_shape = jax.ShapeDtypeStruct((2, MODES * MODES, 2 * block), F32)
    planes = pltpu.VMEM((MODES // 2 + 1, GRID, 2 * block), F32)
    flowing = pltpu.VMEM((MODES * MODES, 2 * block), F32)
    stacked = pltpu.VMEM((2, 2 * block, 2 * block), F32)
    return block, cells, weight, offset, table, modes, modes_shape, planes, flowing, stacked


def spectral_forward(plan, layer, info, own, recv, weight_all, offset_all, tables):
    block, cells, weight, offset, table, modes, modes_shape, planes, flowing, stacked = spectral_specs(layer, plan.width)
    return call(
        spectral_forward_kernel,
        2,
        [cells, cells, weight, offset, table, table],
        [cells, cells, modes, modes, modes],
        [plan.half_shape, plan.half_shape, modes_shape, modes_shape, modes_shape],
        [planes, flowing, stacked],
        3 * 2e9,
        14 * 2**20,
        f"spectral_forward_{layer}",
    )(info, own, recv, weight_all, offset_all, tables[0], tables[3])


def spectral_backward(plan, layer, info, own, recv, weight_all, saved, tables, packed=None, start=None):
    block, cells, weight, offset, table, modes, modes_shape, planes, flowing, stacked = spectral_specs(layer, plan.width)
    specs = [cells, cells, weight, modes, modes, modes, table, table]
    out_specs, out_shapes = [cells, cells], [plan.half_shape, plan.half_shape]
    scratch = [planes, flowing, stacked, pltpu.VMEM((2, 2 * block, 2 * block), F32)]
    args = [info, own, recv, weight_all, *saved, tables[1], tables[2]]
    aliases = {}
    if start is None:
        out_specs += [
            pl.BlockSpec((2, 2, None, block, block), lambda b, s: (0, 0, b, 0, 0)),
            pl.BlockSpec((None, 8, block), lambda b, s: (b, 0, 0)),
        ]
        out_shapes += [
            jax.ShapeDtypeStruct((2, 2, 2, block, block), F32),
            jax.ShapeDtypeStruct((2, 8, block), F32),
        ]
    else:
        specs.append(pl.BlockSpec(memory_space=pl.ANY))
        out_specs.append(pl.BlockSpec(memory_space=pl.ANY))
        out_shapes.append(jax.ShapeDtypeStruct(packed.shape, F32))
        aliases = {len(args): 2}
        args.append(packed)
        scratch += [pltpu.VMEM((2, 2, block, block), F32), pltpu.VMEM((8, block), F32), pltpu.VMEM((block, block), F32)]
        scratch += [pltpu.SemaphoreType.DMA((10,))]
    return call(
        functools.partial(spectral_backward_kernel, start),
        2,
        specs,
        out_specs,
        out_shapes,
        scratch,
        0,
        0,
        f"spectral_backward_{layer}",
        56,
        aliases,
    )(*args)


def ffn_forward(plan, layer, more, info, x, kept, taken, gains, biases, up, up_offset, down, down_offset):
    width, hidden = plan.width, plan.hidden
    specs = list(plan.pieces) if len(x) == 3 else [plan.row]
    specs += [plan.half_row, plan.half_row, plan.norm(layer), plan.norm(layer)]
    specs += [plan.matrix(layer, width, hidden), plan.whole(up_offset.shape)]
    specs += [plan.matrix(layer, hidden, width), plan.whole(down_offset.shape)]
    args = [*x, kept, taken, gains, biases, up, up_offset, down, down_offset]
    out_specs = [plan.row, plan.wide_row]
    out_shapes = [plan.row_shape, plan.wide_shape]
    if more:
        specs += [plan.norm(layer + 1), plan.norm(layer + 1)]
        args += [gains, biases]
        out_specs += [plan.row, plan.half_row, plan.half_row]
        out_shapes += [plan.row_shape, plan.half_shape, plan.half_shape]
    else:
        out_specs += [plan.first, plan.second]
        out_shapes += [plan.piece_shape, plan.piece_shape]
    return call(
        functools.partial(ffn_forward_kernel, plan.steps, layer, len(x), more),
        plan.steps,
        specs,
        out_specs,
        out_shapes,
        [],
        3 * 4 * 2048 * width * hidden,
        24 * 2**20,
        f"ffn_forward_{layer}",
    )(info, *args)


def ffn_backward(plan, layer, info, mixed, before, gains, biases, up, down, grads, rows=None):
    width, hidden = plan.width, plan.hidden
    fused = len(grads) == 5
    lined = (width // 128, hidden + SMALL_ROWS, 128)
    scratch = [pltpu.VMEM(shape, F32) for shape in ((width, hidden), (hidden, width), (8, width))]
    if fused:
        packed, packed_specs = [lined, lined], [plan.whole(lined)] * 2
    else:
        packed, packed_specs = [(rows, 128)], [pl.BlockSpec(memory_space=pl.ANY)]
        scratch = [pltpu.VMEM((2, *lined), F32), pltpu.SemaphoreType.DMA] + scratch
    specs = [plan.row, plan.wide_row, plan.norm(layer), plan.norm(layer)]
    specs += [plan.matrix(layer, width, hidden), plan.matrix(layer, hidden, width)]
    args = [mixed, before, gains, biases, up, down, *grads]
    if fused:
        specs += [plan.row] + [plan.half_row] * 4 + [plan.norm(layer + 1)]
        args += [gains]
    else:
        specs += plan.pieces
    return call(
        functools.partial(ffn_backward_kernel, plan.steps, fused),
        plan.steps,
        specs,
        [
            plan.half_row,
            plan.half_row,
            *packed_specs,
        ],
        [
            plan.half_shape,
            plan.half_shape,
            *[jax.ShapeDtypeStruct(shape, F32) for shape in packed],
        ],
        scratch,
        3 * 8 * 2048 * width * hidden,
        24 * 2**20,
        f"ffn_backward_{layer}",
    )(info, *args)


def input_gradient(plan, info, pieces, du, dh, gains):
    return call(
        functools.partial(input_grad_kernel, plan.steps),
        plan.steps,
        plan.pieces + [plan.half_row] * 4 + [plan.norm(0)],
        [plan.first, plan.second, plan.whole((8, plan.width))],
        [plan.piece_shape, plan.piece_shape, jax.ShapeDtypeStruct((8, plan.width), F32)],
        [],
        0,
        16 * 2**20,
        "input_gradient",
    )(info, *pieces, *du, *dh, gains)


def item_routes(wide, section):
    routes = []
    for flip in range(2):
        pairs = []
        for w in range(wide):
            c = w % 2
            for z in range(section):
                target = (w - c + z // 2) * section + 2 * c + (z % 2 ^ flip)
                if target != w * section + z:
                    pairs.append((w * section + z, target))
        routes.append(pairs)
    return routes


def copy_kernel(info, source, *refs):
    refs[-1][...] = source[...]


def pick(info, shard, flip, after=()):
    items, rows, *cell = shard.shape
    anywhere = pl.BlockSpec(memory_space=pl.ANY)
    return call(
        copy_kernel,
        rows // ROWS,
        [pl.BlockSpec((None, ROWS, *cell), lambda j, s: (s[1] ^ flip, j, 0, 0))] + [anywhere] * len(after),
        pl.BlockSpec((ROWS, *cell), lambda j, s: (j, 0, 0)),
        jax.ShapeDtypeStruct((rows, *cell), F32),
        [],
        0,
        0,
        "pick",
        16,
    )(info, shard, *after)


def pass_kernel(count, *refs):
    pass


def passed(values, after):
    anywhere = pl.BlockSpec(memory_space=pl.ANY)
    return pl.pallas_call(
        functools.partial(pass_kernel, len(values)),
        in_specs=[anywhere] * (len(values) + len(after)),
        out_specs=[anywhere] * len(values),
        out_shape=[jax.ShapeDtypeStruct(v.shape, v.dtype) for v in values],
        input_output_aliases={i: i for i in range(len(values))},
        name="passed",
    )(*values, *after)


def send_piece(piece, route):
    return lax.ppermute(piece, BOTH, route)


def join_kernel(sources, info, *refs):
    values = refs[0][...]
    if sources == 2:
        values = jnp.where(info[2] == 1, values, refs[1][...])
    refs[-1][...] = values


def join(info, own, first, second, after=()):
    rows, *cell = first.shape
    anywhere = pl.BlockSpec(memory_space=pl.ANY)
    shape = jax.ShapeDtypeStruct((2, rows, *cell), F32)

    def part(flip, sources, specs, others):
        return call(
            functools.partial(join_kernel, len(sources)),
            rows // ROWS,
            specs + [anywhere] * len(others),
            pl.BlockSpec((None, ROWS, *cell), lambda j, s: (s[1] ^ flip, j, 0, 0)),
            shape,
            [],
            0,
            0,
            f"join_{flip}",
            16,
            {1 + len(sources): 0} if flip else None,
        )(info, *sources, *others)

    mine = pl.BlockSpec((ROWS, *cell), lambda j, s: (j * s[2], 0, 0))
    sent = pl.BlockSpec((ROWS, *cell), lambda j, s: (j * (1 - s[2]), 0, 0))
    row = pl.BlockSpec((ROWS, *cell), lambda j, s: (j, 0, 0))
    half = part(0, [own, first], [mine, sent], list(after))
    return part(1, [second], [row], [half])


def as_one(function, *args):
    def empty(*args):
        return jax.tree.map(lambda leaf: jnp.zeros(leaf.shape, leaf.dtype), jax.eval_shape(function, *args))

    return lax.cond(lax.axis_index("wide") < lax.axis_size("wide"), function, empty, *args)


def swap(values):
    return lax.ppermute(values, "wide", [(i, i ^ 1) for i in range(lax.axis_size("wide"))])


def digits(size, low, most):
    found = []
    while 1 << low < size:
        radix = most if most << low <= size else 2
        found.append((low, radix))
        low += radix.bit_length() - 1
    return found


def partners(axis, bit, offset):
    return [(i, i ^ offset << bit) for i in range(lax.axis_size(axis))]


def sum_spread(values, axis, bit, radix):
    me = (lax.axis_index(axis) >> bit) % radix
    parts = values.reshape((radix, -1) + values.shape[1:])
    total = lax.dynamic_index_in_dim(parts, me, 0, keepdims=False)
    for offset in range(1, radix):
        part = lax.dynamic_index_in_dim(parts, me ^ offset, 0, keepdims=False)
        total = total + lax.ppermute(part, axis, partners(axis, bit, offset))
    return total


def collect(values, axis, bit, radix):
    me = (lax.axis_index(axis) >> bit) % radix
    out = jnp.zeros((radix,) + values.shape, F32)
    for offset in range(radix):
        got = lax.ppermute(values, axis, partners(axis, bit, offset)) if offset else values
        out = lax.dynamic_update_index_in_dim(out, got, me ^ offset, 0)
    return out.reshape((-1,) + values.shape[1:])


def spread_steps(axis, low, most):
    return [(axis, *digit) for digit in digits(lax.axis_size(axis), low, most)]


def sum_spread_all(values, steps):
    for step in steps:
        values = sum_spread(values, *step)
    return values


def collect_all(values, steps):
    for step in steps[::-1]:
        values = collect(values, *step)
    return values


def turned(steps):
    return steps, steps[1:] + steps[:1]


def sum_spread_halves(values, steps):
    halves = jnp.split(values, 2)
    for pair in zip(*turned(steps)):
        halves = [sum_spread(half, *step) for half, step in zip(halves, pair)]
    return jnp.concatenate(halves)


def collect_halves(values, steps):
    halves = jnp.split(values, 2)
    for pair in list(zip(*turned(steps)))[::-1]:
        halves = [collect(half, *step) for half, step in zip(halves, pair)]
    return jnp.concatenate(halves)


def packed_rows(parts, unit):
    rows = [part.reshape(-1, 128) for part in parts]
    missing = -sum(row.shape[0] for row in rows) % unit
    return jnp.concatenate(rows + [jnp.zeros((missing, 128), F32)])


def unpack_kernel(info, mine, other, second, *outs):
    gain_out, bias_out, mix_out, offset_out, up_out, up_offset_out, down_out, down_offset_out = outs
    core = info[0]

    def low_high(start, count):
        a, b = mine[start : start + count], other[start : start + count]
        return jnp.where(core == 0, a, b), jnp.where(core == 0, b, a)

    width = up_out.shape[1]
    rows, lanes = width + SMALL_ROWS, width // 128
    down_at, mix_at = lanes * rows, 2 * lanes * rows
    first_mix = lanes * rows
    inner_at = first_mix + 8 * 128 + 16
    for index in range(lanes):
        at = pl.ds(index * 128, 128)
        begin = index * rows
        up_out[0, :, at], down_out[0, :, at] = low_high(begin, width)
        up_out[1, :, at] = second[begin : begin + width]
        down_out[1, :, at] = second[down_at + begin : down_at + begin + width]
        small = low_high(begin + width, 8)[0]
        late = second[begin + width : begin + width + 8]
        low, high = low_high(inner_at + 8 * index, 8)
        inner = low + high
        gain_out[0, 0:1, at] = inner[0:1]
        bias_out[0, 0:1, at] = inner[1:2]
        gain_out[0, 1:2, at] = small[0:1]
        bias_out[0, 1:2, at] = small[1:2]
        gain_out[1, 0:1, at] = small[4:5]
        bias_out[1, 0:1, at] = small[5:6]
        gain_out[1, 1:2, at] = late[0:1]
        bias_out[1, 1:2, at] = late[1:2]
        up_offset_out[0:1, at] = small[2:3]
        up_offset_out[1:2, at] = late[2:3]
        down_offset_out[0:1, at] = small[3:4]
        down_offset_out[1:2, at] = late[3:4]
    for block in range(BLOCKS):
        late = second[mix_at + (4 * BLOCKS) * 128 + 8 * block : mix_at + (4 * BLOCKS) * 128 + 8 * block + 8]
        for j in range(2):
            for part in range(2):
                begin = mix_at + ((2 * j + part) * BLOCKS + block) * 128
                mix_out[1, j, part, block] = second[begin : begin + 128]
                offset_out[1, j, part, block : block + 1] = late[2 * j + part : 2 * j + part + 1]
    for block in range(2):
        offsets = low_high(first_mix + 8 * 128 + 8 * block, 8)
        for j in range(2):
            for part in range(2):
                weights = low_high(first_mix + ((2 * j + part) * 2 + block) * 128, 128)
                for half in range(2):
                    at = 2 * half + block
                    mix_out[0, j, part, at] = weights[half]
                    offset_out[0, j, part, at : at + 1] = offsets[half][2 * j + part : 2 * j + part + 1]


def unpack(info, args, shapes):
    def whole(shape):
        return pl.BlockSpec(shape, lambda j, s: (0,) * len(shape))

    return call(
        unpack_kernel,
        1,
        [whole(arg.shape) for arg in args],
        [whole(shape) for shape in shapes],
        [jax.ShapeDtypeStruct(shape, F32) for shape in shapes],
        [],
        0,
        0,
        "unpack",
        40,
    )(info, *args)


def on_device(
    inputs,
    norm_gain,
    norm_bias,
    mix_weight,
    mix_bias,
    up_weight,
    up_bias,
    down_weight,
    down_bias,
    out_grad,
):
    width, hidden = up_weight.shape[1:]
    plan = Plan(inputs.shape[1], width, hidden)
    routes = item_routes(lax.axis_size("wide"), lax.axis_size("section"))
    core = lax.axis_index("wide") % 2
    section = lax.axis_index("section")
    info = jnp.stack([core, section % 2, section // 2 == core]).astype(jnp.int32)
    plain, weighted = column_tables()
    tables = [jnp.asarray(split_table(t)) for t in (plain, weighted, plain.T, weighted.T)]

    back_routes = [[(b, a) for a, b in route] for route in routes]
    ffn_args = (norm_gain, norm_bias, up_weight, up_bias, down_weight, down_bias)
    back_args = (norm_gain, norm_bias, up_weight, down_weight)

    devices = lax.axis_size("wide") * lax.axis_size("section")
    members = spread_steps("wide", 1, 2)
    sections = spread_steps("section", 0, 2)
    matrix_rows = 2 * (width // 128) * (hidden + SMALL_ROWS)
    second_rows = matrix_rows + 4 * BLOCKS * 128 + 8 * BLOCKS
    second_rows += -second_rows % (8 * devices)

    def forward(x):
        keep, send = first_norm(plan, info, x, norm_gain, norm_bias)
        keep, send, *saved0 = spectral_forward(plan, 0, info, keep, swap(send), mix_weight, mix_bias, tables)
        u0, a0, x1, keep, send = ffn_forward(plan, 0, True, info, x, keep, swap(send), *ffn_args)
        keep, send, *saved1 = spectral_forward(plan, 1, info, keep, swap(send), mix_weight, mix_bias, tables)
        u1, a1, va, vb = ffn_forward(plan, 1, False, info, (x1,), keep, swap(send), *ffn_args)
        return (va, vb), (saved0, u0, a0, x1, saved1, u1, a1)

    def backward(x, grads, saved):
        saved0, u0, a0, x1, saved1, u1, a1 = saved
        keep, send, packed = ffn_backward(plan, 1, info, u1, a1, *back_args, grads, second_rows)
        dh_keep, dh_send, packed = spectral_backward(
            plan, 1, info, keep, swap(send), mix_weight, saved1, tables, packed, matrix_rows
        )
        late = (x1, keep, send, dh_keep, swap(dh_send))
        second = lax.psum_scatter(packed, "wide", scatter_dimension=0, tiled=True)
        return *as_one(backward_first, x, late, (saved0, u0, a0)), second

    def backward_first(x, late, saved):
        saved0, u0, a0 = saved
        keep, send, kept, sent = ffn_backward(plan, 0, info, u0, a0, *back_args, late)
        dh_keep, dh_send, mix, offsets = spectral_backward(plan, 0, info, keep, swap(send), mix_weight, saved0, tables)
        last = ((keep, send), (dh_keep, swap(dh_send)))
        dxa, dxb, inner = input_gradient(plan, info, x, *last, norm_gain)
        return (dxa, dxb), (kept, sent, mix, offsets, inner)

    def reduce_first(kept, sent, mix, offsets, inner, outputs):
        inner = inner.reshape(8, -1, 128).transpose(1, 0, 2)
        first = packed_rows([kept + swap(sent), mix, offsets, inner], 8 * devices)
        first = sum_spread_all(sum_spread_halves(first, members), sections[:1])
        outputs = join(info, *outputs)
        [first] = passed([first], [outputs])
        first = sum_spread_all(first, sections[1:])
        return collect_all(first, sections), outputs

    def reduce_gradients(local, second, outputs):
        second = lax.psum(second, "section")
        return *as_one(reduce_first, *local, outputs), second

    def share_first(first):
        summed = collect_halves(first, members)
        return summed, swap(summed)

    def share_gradients(first, second):
        second = lax.all_gather(second, "wide", axis=0, tiled=True)
        return *as_one(share_first, first), second

    def send_both(pieces, routes):
        return [send_piece(piece, route) for piece, route in zip(pieces, routes)]

    x = (inputs, *send_both((pick(info, inputs, 0), pick(info, inputs, 1)), routes))
    picked_grads = pick(info, out_grad, 0), pick(info, out_grad, 1)
    grads = (out_grad, *send_both(passed(picked_grads, x[1:]), routes))
    results, saved = as_one(forward, x)
    results = passed(results, grads[1:])
    outputs = (results[0], *send_both(results, back_routes))
    (dxa, dxb), local, second = as_one(backward, x, grads, saved)
    [dxa] = passed([dxa], outputs[1:])
    returned = send_piece(dxa, back_routes[0])
    first, outputs, second = as_one(reduce_gradients, local, second, outputs)
    dxb = send_piece(*passed([dxb], [returned, first]), back_routes[1])
    mine, other, second = as_one(share_gradients, first, second)
    shapes = [a.shape for a in (norm_gain, norm_bias, mix_weight, mix_bias, up_weight, up_bias, down_weight, down_bias)]
    gradients = unpack(info, [mine, other, second], shapes)
    return (outputs, join(info, dxa, returned, dxb), *gradients)


def solution(mesh):
    cells = P("wide", "section", None, None)
    return jax.shard_map(
        on_device,
        mesh=mesh,
        in_specs=(cells, P(), P(), P(), P(), P(), P(), P(), P(), cells),
        out_specs=(cells, cells, P(), P(), P(), P(), P(), P(), P(), P()),
        check_vma=False,
    )
```

```python
import functools
import math

import jax
import jax.numpy as jnp
import numpy as np
from jax import lax
from jax.experimental import pallas as pl
from jax.experimental.pallas import tpu as pltpu
from jax.sharding import PartitionSpec as P

BLOCKS = 4
GRID = 64
MODES = 32
EPSILON = 1e-05
THRESHOLD = 0.05
ROWS = 8
SMALL_ROWS = 32
F32 = jnp.float32
BF16 = jnp.bfloat16
BOTH = ("wide", "section")


def split_table(table):
    table = table.astype(np.float32)
    high = table.astype(jnp.bfloat16)
    low = (table - high.astype(np.float32)).astype(jnp.bfloat16)
    return np.concatenate([high, high, low, low], axis=1)


def column_tables():
    columns = np.arange(MODES)
    angles = 2.0 * math.pi * (columns[:, None] * np.arange(GRID)[None, :] % GRID) / GRID
    plain = np.concatenate([np.cos(angles), np.sin(angles)], axis=0) / GRID
    factor = np.where(columns == 0, 1.0, 2.0)
    weighted = plain * np.concatenate([factor, factor])[:, None]
    return plain, weighted


def twiddle(index, length):
    angle = 2.0 * math.pi * index / length
    return math.cos(angle), math.sin(angle)


def half_spectrum(planes, pruned=False):
    length = len(planes)
    if length == 2:
        return [(planes[0] + planes[1], None), (planes[0] - planes[1], None)]
    even = half_spectrum(planes[0::2])
    odd = half_spectrum(planes[1::2])
    quarter = length // 4
    first, second = [], []
    for k in range(quarter + 1):
        (er, ei), (dr, di) = even[k], odd[k]
        if k == 0:
            first.append((er + dr, None))
            second.append((er - dr, None))
            continue
        if k == quarter:
            first.append((er, -dr))
            continue
        c, s = twiddle(k, length)
        if 2 * k == quarter:
            tr, ti = (dr + di) * c, (di - dr) * c
        else:
            tr, ti = dr * c + di * s, di * c - dr * s
        first.append((er + tr, ei + ti))
        second.append((er - tr, ti - ei))
    if pruned:
        return first
    return first + second[::-1]


def half_synthesis(spectrum, length, pruned=False):
    if length == 2:
        (a, _), (b, _) = spectrum
        return [a + b, a - b]
    quarter = length // 4
    even, odd = [], []
    for k in range(quarter + 1):
        ar, ai = spectrum[k]
        if k == quarter:
            even.append((ar, None))
            odd.append((-ai, None))
            continue
        if k == 0:
            if pruned:
                even.append((ar, None))
                odd.append((ar, None))
            else:
                br = spectrum[length // 2][0]
                even.append((ar + br, None))
                odd.append((ar - br, None))
            continue
        if pruned:
            sr, si, tr, ti = ar, ai, ar, ai
        else:
            br, bi = spectrum[length // 2 - k]
            sr, si, tr, ti = ar + br, ai - bi, ar - br, ai + bi
        even.append((sr, si))
        c, s = twiddle(k, length)
        if 2 * k == quarter:
            odd.append(((tr - ti) * c, (ti + tr) * c))
        else:
            odd.append((tr * c - ti * s, ti * c + tr * s))
    even_planes = half_synthesis(even, length // 2)
    odd_planes = half_synthesis(odd, length // 2)
    planes = []
    for e, o in zip(even_planes, odd_planes):
        planes += [e, o]
    return planes


def exact_dot(left, right, left_dim, right_dim):
    return lax.dot_general(
        left,
        right,
        (((left_dim,), (right_dim,)), ((), ())),
        precision=lax.Precision.HIGH,
        preferred_element_type=F32,
    )


def split(values):
    high = values.astype(BF16)
    low = (values - high.astype(F32)).astype(BF16)
    return high, low


def table_dot(table, values):
    high, low = split(values)
    stacked = jnp.concatenate([high, low, high, low], axis=0)
    return jnp.dot(table, stacked, preferred_element_type=F32)


def gelu(values):
    return 0.5 * values * (1.0 + lax.erf(values * math.sqrt(0.5)))


def gelu_and_slope(values):
    cumulative = 0.5 * (1.0 + lax.erf(values * math.sqrt(0.5)))
    density = jnp.exp(-0.5 * values * values) * (1.0 / math.sqrt(2.0 * math.pi))
    return values * cumulative, cumulative + values * density


def normalise(values):
    average = jnp.mean(values, axis=-1, keepdims=True)
    centered = values - average
    variance = jnp.mean(centered * centered, axis=-1, keepdims=True)
    scale = lax.rsqrt(variance + EPSILON)
    return centered * scale, scale


def norm_backward(grad, unit, scale, gains):
    inner = grad * gains
    mean_inner = jnp.mean(inner, axis=-1, keepdims=True)
    mean_unit = jnp.mean(inner * unit, axis=-1, keepdims=True)
    return scale * (inner - mean_inner - unit * mean_unit)


def column_sum(values):
    return jnp.sum(values, axis=0, keepdims=True)


def joined(core, kept, other):
    shape = (kept.shape[0] * kept.shape[1], kept.shape[2])
    kept, other = kept[...].reshape(shape), other[...].reshape(shape)
    first = jnp.where(core == 0, kept, other)
    second = jnp.where(core == 0, other, kept)
    return jnp.concatenate([first, second], axis=1)


def parted(core, values, kept, other):
    half = values.shape[1] // 2
    first, second = values[:, :half], values[:, half:]
    kept[...] = jnp.where(core == 0, first, second).reshape(kept.shape)
    other[...] = jnp.where(core == 0, second, first).reshape(other.shape)


def flat(ref):
    return ref[...].reshape(-1, ref.shape[-1])


def picked(info, step, steps, refs):
    if len(refs) == 1:
        return flat(refs[0])
    own, first, second = refs
    first = jnp.where(info[2] == 1, flat(own), flat(first))
    return jnp.where(step < steps // 2, first, flat(second))


def put_pieces(step, steps, refs, values):
    if len(refs) == 1:
        refs[0][...] = values.reshape(refs[0].shape)
        return

    @pl.when(step < steps // 2)
    def _():
        refs[0][...] = values.reshape(refs[0].shape)

    @pl.when(step >= steps // 2)
    def _():
        refs[1][...] = values.reshape(refs[1].shape)


def analyse(own, recv, table, sign, planes, modes):
    def rows(index, _):
        at = pl.ds(pl.multiple_of(index * 8, 8), 8)
        loaded = [own[p, at, :] for p in range(GRID // 2)] + [recv[p, at, :] for p in range(GRID // 2)]
        for k, (re, im) in enumerate(half_spectrum(loaded, pruned=True)):
            im = jnp.zeros_like(re) if im is None else im
            if k % 2:
                re, im = re * sign, im * sign
            planes[k, at, :] = jnp.concatenate([re, im], axis=1)
        return 0

    lax.fori_loop(0, GRID // 8, rows, 0)
    for k in range(MODES // 2 + 1):
        found = table_dot(table[...], planes[k])
        lanes = found.shape[1] // 2
        cr, ci = found[:MODES, :lanes], found[:MODES, lanes:]
        sr, si = found[MODES:, :lanes], found[MODES:, lanes:]
        if k < MODES // 2:
            modes[k * MODES : (k + 1) * MODES, :] = jnp.concatenate([cr + si, ci - sr], axis=1)
        if k > 0:
            place = MODES - k
            modes[place * MODES : (place + 1) * MODES, :] = jnp.concatenate([cr - si, -ci - sr], axis=1)


def synthesise(modes, table, sign, planes, keep, send):
    lanes = modes.shape[1] // 2
    for k in range(MODES // 2 + 1):
        place = MODES - k
        if k == 0:
            above, below = modes[0:MODES, :], None
            total, apart = above, above
        elif k == MODES // 2:
            below = modes[place * MODES : (place + 1) * MODES, :]
            total, apart = below, -below
        else:
            above = modes[k * MODES : (k + 1) * MODES, :]
            below = modes[place * MODES : (place + 1) * MODES, :]
            total, apart = above + below, above - below
        upper = jnp.concatenate([total[:, :lanes], apart[:, lanes:]], axis=1)
        lower = jnp.concatenate([-total[:, lanes:], apart[:, :lanes]], axis=1)
        planes[k] = table_dot(table[...], jnp.concatenate([upper, lower], axis=0))

    def rows(index, _):
        at = pl.ds(pl.multiple_of(index * 8, 8), 8)
        spectrum = []
        for k in range(MODES // 2 + 1):
            both = planes[k, at, :]
            if k % 2:
                both = both * sign
            spectrum.append((both[:, :lanes], both[:, lanes:]))
        cells = half_synthesis(spectrum, GRID, pruned=True)
        for p in range(GRID // 2):
            keep[p, at, :] = cells[p]
            send[p, at, :] = cells[GRID // 2 + p]
        return 0

    lax.fori_loop(0, GRID // 8, rows, 0)


def place_weights(weight, stacked):
    lanes = weight.shape[-1]
    for j in range(2):
        real, imag = weight[j, 0], weight[j, 1]
        stacked[j, :lanes, :lanes] = real
        stacked[j, :lanes, lanes:] = imag
        stacked[j, lanes:, :lanes] = -imag
        stacked[j, lanes:, lanes:] = real


MIX_ROWS = 256


def mix_offsets(offset, block):
    at = pl.ds(block, 1)
    return [jnp.concatenate([offset[j, 0, at, :], offset[j, 1, at, :]], axis=1) for j in range(2)]


def spectral_forward_kernel(
    info, own, recv, weight, offset, table_in, table_out, keep, send, modes, before, after, planes, shrunk, stacked
):
    core = info[0]
    sign = jnp.where(core == 1, -1.0, 1.0).astype(F32)
    place_weights(weight, stacked)
    first_offset, second_offset = mix_offsets(offset, 2 * core + pl.program_id(0))
    analyse(own, recv, table_in, sign, planes, modes)

    def mix(index, _):
        at = pl.ds(pl.multiple_of(index * MIX_ROWS, MIX_ROWS), MIX_ROWS)
        first = exact_dot(modes[at, :], stacked[0], 1, 0) + first_offset
        before[at, :] = first
        second = exact_dot(gelu(first), stacked[1], 1, 0) + second_offset
        after[at, :] = second
        shrunk[at, :] = second - THRESHOLD * jnp.tanh(second * (1.0 / THRESHOLD))
        return 0

    lax.fori_loop(0, MODES * MODES // MIX_ROWS, mix, 0)
    synthesise(shrunk, table_out, sign, planes, keep, send)


def spectral_backward_kernel(
    start, info, own, recv, weight, modes, before, after, table_in, table_out, *refs
):
    if start is None:
        keep, send, weight_grad, offset_grad, planes, flowing, stacked, summed = refs
    else:
        _, keep, send, out, planes, flowing, stacked, summed, weight_grad, offset_grad, blank, sems = refs
    core = info[0]
    sign = jnp.where(core == 1, -1.0, 1.0).astype(F32)
    place_weights(weight, stacked)
    analyse(own, recv, table_in, sign, planes, flowing)
    summed[...] = jnp.zeros_like(summed)

    def mix(index, totals):
        at = pl.ds(pl.multiple_of(index * MIX_ROWS, MIX_ROWS), MIX_ROWS)
        ratio = jnp.tanh(after[at, :] * (1.0 / THRESHOLD))
        grad_second = flowing[at, :] * ratio * ratio
        hidden, slope = gelu_and_slope(before[at, :])
        summed[1] += exact_dot(hidden, grad_second, 0, 0)
        grad_first = exact_dot(grad_second, stacked[1], 1, 1) * slope
        summed[0] += exact_dot(modes[at, :], grad_first, 0, 0)
        flowing[at, :] = exact_dot(grad_first, stacked[0], 1, 1)
        return totals[0] + column_sum(grad_first), totals[1] + column_sum(grad_second)

    empty = jnp.zeros((1, flowing.shape[1]), F32)
    totals = lax.fori_loop(0, MODES * MODES // MIX_ROWS, mix, (empty, empty))
    lanes = flowing.shape[1] // 2
    offset_grad[...] = jnp.zeros_like(offset_grad)
    for j in range(2):
        offset_grad[2 * j : 2 * j + 1] = totals[j][:, :lanes]
        offset_grad[2 * j + 1 : 2 * j + 2] = totals[j][:, lanes:]
        weight_grad[j, 0] = summed[j, :lanes, :lanes] + summed[j, lanes:, lanes:]
        weight_grad[j, 1] = summed[j, :lanes, lanes:] - summed[j, lanes:, :lanes]
    if start is not None:
        block, other = 2 * core + pl.program_id(0), 2 * (1 - core) + pl.program_id(0)
        blank[...] = jnp.zeros_like(blank)
        copies = []
        for index in range(4):
            for source, place in ((weight_grad.at[index // 2, index % 2], block), (blank, other)):
                at = pl.ds(pl.multiple_of(start + (index * BLOCKS + place) * 128, 8), 128)
                copies.append(pltpu.make_async_copy(source, out.at[at], sems.at[len(copies)]))
        for source, place in ((offset_grad, block), (blank.at[pl.ds(0, 8)], other)):
            at = pl.ds(pl.multiple_of(start + 4 * BLOCKS * 128 + place * 8, 8), 8)
            copies.append(pltpu.make_async_copy(source, out.at[at], sems.at[len(copies)]))
        for copy in copies:
            copy.start()
    synthesise(flowing, table_out, sign, planes, keep, send)
    if start is not None:
        for copy in copies:
            copy.wait()


def first_norm_kernel(steps, info, own, a, b, gains, biases, keep, send):
    unit, _ = normalise(picked(info, pl.program_id(0), steps, (own, a, b)))
    parted(info[0], unit * gains[0:1] + biases[0:1], keep, send)


def ffn_forward_kernel(steps, layer, pieces, more, info, *refs):
    step = pl.program_id(0)
    refs = list(refs)
    x_refs, refs = refs[:pieces], refs[pieces:]
    kept, taken, gains, biases, up, up_offset, down, down_offset = refs[:8]
    refs = refs[8:]
    core = info[0]
    mixed = picked(info, step, steps, x_refs) + joined(core, kept, taken)
    unit, _ = normalise(mixed)
    normed = unit * gains[1:2] + biases[1:2]
    before = exact_dot(normed, up[...], 1, 0) + up_offset[layer : layer + 1]
    result = mixed + exact_dot(gelu(before), down[...], 1, 0) + down_offset[layer : layer + 1]
    if more:
        next_gains, next_biases, mixed_out, before_out, result_out, keep, send = refs
        put_pieces(step, steps, (result_out,), result)
        unit, _ = normalise(result)
        parted(core, unit * next_gains[0:1] + next_biases[0:1], keep, send)
    else:
        mixed_out, before_out, first_out, second_out = refs
        put_pieces(step, steps, (first_out, second_out), result)
    mixed_out[...] = mixed.reshape(mixed_out.shape)
    before_out[...] = before.reshape(before_out.shape)


def first_norm_backward(core, x, du_kept, du_sent, dh_kept, dh_taken, gains):
    grad = joined(core, dh_kept, dh_taken)
    unit, scale = normalise(x)
    result = joined(core, du_kept, du_sent) + norm_backward(grad, unit, scale, gains[0:1])
    return result, column_sum(grad * unit), column_sum(grad)


def lanes_first(values):
    return [values[:, at : at + 128] for at in range(0, values.shape[1], 128)]


def ffn_backward_kernel(steps, fused, part, info, *refs):
    step = pl.program_id(0)
    core = info[0]
    refs = list(refs)
    mixed, before, gains, biases, up, down = refs[:6]
    if fused:
        x, du_kept, du_sent, dh_kept, dh_taken, next_gains = refs[6:12]
        grad, late_gain, late_bias = first_norm_backward(core, flat(x), du_kept, du_sent, dh_kept, dh_taken, next_gains)
        refs = refs[12:]
    else:
        grad = flat(refs[6]) if part else jnp.where(info[2] == 1, flat(refs[6]), flat(refs[7]))
        refs = refs[7:] if part else refs[8:]
    if fused:
        keep, send, kept_grads, sent_grads, up_grad, down_grad, small = refs
    elif part == 0:
        keep, send, up_grad, down_grad, small = refs
    else:
        *started, _, _, keep, send, out, lined, sem, up_grad, down_grad, small = refs
        kept_grads, sent_grads = lined.at[0], lined.at[1]

    @pl.when(step == 0)
    def _():
        for index, total in enumerate((up_grad, down_grad, small)):
            total[...] = started[index][...] if part else jnp.zeros_like(total)

    unit, scale = normalise(flat(mixed))
    normed = unit * gains[1:2] + biases[1:2]
    hidden, slope = gelu_and_slope(flat(before))
    down_grad[...] += exact_dot(hidden, grad, 0, 0)
    inner = exact_dot(grad, down[...], 1, 1) * slope
    up_grad[...] += exact_dot(normed, inner, 0, 0)
    outer = exact_dot(inner, up[...], 1, 1)
    small[0:1] += column_sum(outer * unit)
    small[1:2] += column_sum(outer)
    small[2:3] += column_sum(inner)
    small[3:4] += column_sum(grad)
    if fused:
        small[4:5] += late_gain
        small[5:6] += late_bias
    parted(core, grad + norm_backward(outer, unit, scale, gains[1:2]), keep, send)
    if part == 0 and not fused:
        return

    @pl.when(step == steps - 1)
    def _():
        width = up_grad.shape[0]
        parts = zip(lanes_first(up_grad[...]), lanes_first(down_grad[...]), lanes_first(small[...]))
        for index, (a, b, c) in enumerate(parts):
            kept_grads[index, :width] = jnp.where(core == 0, a, b) if fused else a
            sent_grads[index, :width] = jnp.where(core == 0, b, a) if fused else b
            for grads in (kept_grads, sent_grads):
                grads[index, width : width + 8] = c
                grads[index, width + 8 :] = jnp.zeros((SMALL_ROWS - 8, 128), F32)
        if not fused:
            lines = out.at[pl.ds(0, lined.size // 128)].reshape(lined.shape)
            copy = pltpu.make_async_copy(lined, lines, sem)
            copy.start()
            copy.wait()


def input_grad_kernel(steps, info, own, a, b, du_kept, du_sent, dh_kept, dh_taken, gains, first_out, second_out, small):
    step = pl.program_id(0)
    x = picked(info, step, steps, (own, a, b))
    result, gain_sum, bias_sum = first_norm_backward(info[0], x, du_kept, du_sent, dh_kept, dh_taken, gains)

    @pl.when(step == 0)
    def _():
        small[...] = jnp.zeros_like(small)

    small[0:1] += gain_sum
    small[1:2] += bias_sum
    put_pieces(step, steps, (first_out, second_out), result)


def call(kernel, grid, in_specs, out_specs, out_shapes, scratch, flops, moved, name, vmem=30, aliases=None):
    return pl.pallas_call(
        kernel,
        grid_spec=pltpu.PrefetchScalarGridSpec(
            num_scalar_prefetch=1,
            grid=(grid,),
            in_specs=in_specs,
            out_specs=out_specs,
            scratch_shapes=scratch,
        ),
        out_shape=out_shapes,
        input_output_aliases=aliases or {},
        compiler_params=pltpu.CompilerParams(vmem_limit_bytes=vmem * 2**20),
        cost_estimate=pl.CostEstimate(flops=int(flops), bytes_accessed=int(moved), transcendentals=0),
        name=name,
    )


class Plan:
    def __init__(self, quarter, width, hidden):
        self.quarter, self.width, self.hidden = quarter, width, hidden
        self.steps = 2 * quarter // ROWS
        per_piece = quarter // ROWS
        half = width // 2

        def local(j, s):
            return (j, 0, 0)

        def canonical(j, s):
            return (((j // per_piece) ^ s[1]) * per_piece + j % per_piece, 0, 0)

        self.row = pl.BlockSpec((ROWS, GRID, width), local)
        self.wide_row = pl.BlockSpec((ROWS, GRID, hidden), local)
        self.half_row = pl.BlockSpec((ROWS, GRID, half), canonical)
        self.first = pl.BlockSpec((ROWS, GRID, width), lambda j, s: (jnp.minimum(j, per_piece - 1), 0, 0))
        self.pieces = [
            pl.BlockSpec((None, ROWS, GRID, width), lambda j, s: (s[1], jnp.minimum(j, per_piece - 1) * s[2], 0, 0)),
            pl.BlockSpec((ROWS, GRID, width), lambda j, s: (jnp.minimum(j, per_piece - 1) * (1 - s[2]), 0, 0)),
            pl.BlockSpec((ROWS, GRID, width), lambda j, s: (jnp.maximum(j - per_piece, 0), 0, 0)),
        ]
        self.second = pl.BlockSpec((ROWS, GRID, width), lambda j, s: (jnp.maximum(j - per_piece, 0), 0, 0))
        self.half_shape = jax.ShapeDtypeStruct((2 * quarter, GRID, half), F32)
        self.row_shape = jax.ShapeDtypeStruct((2 * quarter, GRID, width), F32)
        self.wide_shape = jax.ShapeDtypeStruct((2 * quarter, GRID, hidden), F32)
        self.piece_shape = jax.ShapeDtypeStruct((quarter, GRID, width), F32)

    def norm(self, layer):
        return pl.BlockSpec((None, 2, self.width), lambda j, s: (layer, 0, 0))

    def matrix(self, layer, rows, columns):
        return pl.BlockSpec((None, rows, columns), lambda j, s: (layer, 0, 0))

    def whole(self, shape):
        return pl.BlockSpec(shape, lambda j, s: (0,) * len(shape))


def first_norm(plan, info, pieces, gains, biases):
    return call(
        functools.partial(first_norm_kernel, plan.steps),
        plan.steps,
        [*plan.pieces, plan.norm(0), plan.norm(0)],
        [plan.half_row, plan.half_row],
        [plan.half_shape, plan.half_shape],
        [],
        0,
        4 * 2**20 * 2,
        "first_norm",
    )(info, *pieces, gains, biases)


def spectral_specs(layer, width):
    block = width // BLOCKS
    cells = pl.BlockSpec((GRID // 2, GRID, block), lambda b, s: (0, 0, b))
    weight = pl.BlockSpec((None, 2, 2, None, block, block), lambda b, s: (layer, 0, 0, 2 * s[0] + b, 0, 0))
    offset = pl.BlockSpec((None, 2, 2, BLOCKS, block), lambda b, s: (layer, 0, 0, 0, 0))
    table = pl.BlockSpec((GRID, 4 * GRID), lambda b, s: (0, 0))
    modes = pl.BlockSpec((None, MODES * MODES, 2 * block), lambda b, s: (b, 0, 0))
    modes_shape = jax.ShapeDtypeStruct((2, MODES * MODES, 2 * block), F32)
    planes = pltpu.VMEM((MODES // 2 + 1, GRID, 2 * block), F32)
    flowing = pltpu.VMEM((MODES * MODES, 2 * block), F32)
    stacked = pltpu.VMEM((2, 2 * block, 2 * block), F32)
    return block, cells, weight, offset, table, modes, modes_shape, planes, flowing, stacked


def spectral_forward(plan, layer, info, own, recv, weight_all, offset_all, tables):
    block, cells, weight, offset, table, modes, modes_shape, planes, flowing, stacked = spectral_specs(layer, plan.width)
    return call(
        spectral_forward_kernel,
        2,
        [cells, cells, weight, offset, table, table],
        [cells, cells, modes, modes, modes],
        [plan.half_shape, plan.half_shape, modes_shape, modes_shape, modes_shape],
        [planes, flowing, stacked],
        3 * 2e9,
        14 * 2**20,
        f"spectral_forward_{layer}",
    )(info, own, recv, weight_all, offset_all, tables[0], tables[3])


def spectral_backward(plan, layer, info, own, recv, weight_all, saved, tables, packed=None, start=None):
    block, cells, weight, offset, table, modes, modes_shape, planes, flowing, stacked = spectral_specs(layer, plan.width)
    specs = [cells, cells, weight, modes, modes, modes, table, table]
    out_specs, out_shapes = [cells, cells], [plan.half_shape, plan.half_shape]
    scratch = [planes, flowing, stacked, pltpu.VMEM((2, 2 * block, 2 * block), F32)]
    args = [info, own, recv, weight_all, *saved, tables[1], tables[2]]
    aliases = {}
    if start is None:
        out_specs += [
            pl.BlockSpec((2, 2, None, block, block), lambda b, s: (0, 0, b, 0, 0)),
            pl.BlockSpec((None, 8, block), lambda b, s: (b, 0, 0)),
        ]
        out_shapes += [
            jax.ShapeDtypeStruct((2, 2, 2, block, block), F32),
            jax.ShapeDtypeStruct((2, 8, block), F32),
        ]
    else:
        specs.append(pl.BlockSpec(memory_space=pl.ANY))
        out_specs.append(pl.BlockSpec(memory_space=pl.ANY))
        out_shapes.append(jax.ShapeDtypeStruct(packed.shape, F32))
        aliases = {len(args): 2}
        args.append(packed)
        scratch += [pltpu.VMEM((2, 2, block, block), F32), pltpu.VMEM((8, block), F32), pltpu.VMEM((block, block), F32)]
        scratch += [pltpu.SemaphoreType.DMA((10,))]
    return call(
        functools.partial(spectral_backward_kernel, start),
        2,
        specs,
        out_specs,
        out_shapes,
        scratch,
        0,
        0,
        f"spectral_backward_{layer}",
        30,
        aliases,
    )(*args)


def ffn_forward(plan, layer, more, info, x, kept, taken, gains, biases, up, up_offset, down, down_offset):
    width, hidden = plan.width, plan.hidden
    specs = list(plan.pieces) if len(x) == 3 else [plan.row]
    specs += [plan.half_row, plan.half_row, plan.norm(layer), plan.norm(layer)]
    specs += [plan.matrix(layer, width, hidden), plan.whole(up_offset.shape)]
    specs += [plan.matrix(layer, hidden, width), plan.whole(down_offset.shape)]
    args = [*x, kept, taken, gains, biases, up, up_offset, down, down_offset]
    out_specs = [plan.row, plan.wide_row]
    out_shapes = [plan.row_shape, plan.wide_shape]
    if more:
        specs += [plan.norm(layer + 1), plan.norm(layer + 1)]
        args += [gains, biases]
        out_specs += [plan.row, plan.half_row, plan.half_row]
        out_shapes += [plan.row_shape, plan.half_shape, plan.half_shape]
    else:
        out_specs += [plan.first, plan.second]
        out_shapes += [plan.piece_shape, plan.piece_shape]
    return call(
        functools.partial(ffn_forward_kernel, plan.steps, layer, len(x), more),
        plan.steps,
        specs,
        out_specs,
        out_shapes,
        [],
        3 * 4 * 2048 * width * hidden,
        24 * 2**20,
        f"ffn_forward_{layer}",
    )(info, *args)


def ffn_backward(plan, layer, info, mixed, before, gains, biases, up, down, grads, part=0, started=(), rows=None):
    width, hidden = plan.width, plan.hidden
    fused = layer == 0
    steps = plan.steps if fused else plan.steps // 2
    start = part * steps
    anywhere = pl.BlockSpec(memory_space=pl.ANY)

    def shifted_rows(spec, lanes):
        return pl.BlockSpec((ROWS, GRID, lanes), lambda j, s: spec.index_map(j + start, s))

    specs = [shifted_rows(plan.row, width), shifted_rows(plan.wide_row, hidden), plan.norm(layer), plan.norm(layer)]
    specs += [plan.matrix(layer, width, hidden), plan.matrix(layer, hidden, width)]
    args = [info, mixed, before, gains, biases, up, down, *grads]
    if fused:
        specs += [plan.row] + [plan.half_row] * 4 + [plan.norm(layer + 1)]
        args += [gains]
    else:
        specs += [plan.row] if part else plan.pieces[:2]
    lined = (width // 128, hidden + SMALL_ROWS, 128)
    totals = ((width, hidden), (hidden, width), (8, width))
    scratch = [pltpu.VMEM(shape, F32) for shape in totals]
    aliases = None
    if fused:
        packed, packed_specs = [lined, lined], [plan.whole(lined)] * 2
    elif part == 0:
        packed, packed_specs, scratch = totals, [plan.whole(shape) for shape in totals], []
    else:
        packed, packed_specs = [(rows, 128)], [anywhere]
        scratch = [pltpu.VMEM((2, *lined), F32), pltpu.SemaphoreType.DMA] + scratch
        keep, send, *begun = started
        specs += [plan.whole(shape) for shape in totals] + [anywhere] * 2
        args += [*begun, keep, send]
        aliases = {len(args) - 2: 0, len(args) - 1: 1}
    return call(
        functools.partial(ffn_backward_kernel, steps, fused, part),
        steps,
        specs,
        [shifted_rows(plan.half_row, width // 2)] * 2 + packed_specs,
        [plan.half_shape, plan.half_shape] + [jax.ShapeDtypeStruct(shape, F32) for shape in packed],
        scratch,
        3 * 8 * 2048 * width * hidden,
        24 * 2**20,
        f"ffn_backward_{layer}_{part}",
        30,
        aliases,
    )(*args)


def input_gradient(plan, info, pieces, du, dh, gains):
    return call(
        functools.partial(input_grad_kernel, plan.steps),
        plan.steps,
        plan.pieces + [plan.half_row] * 4 + [plan.norm(0)],
        [plan.first, plan.second, plan.whole((8, plan.width))],
        [plan.piece_shape, plan.piece_shape, jax.ShapeDtypeStruct((8, plan.width), F32)],
        [],
        0,
        16 * 2**20,
        "input_gradient",
    )(info, *pieces, *du, *dh, gains)


def item_routes(wide, section):
    routes = []
    for flip in range(2):
        pairs = []
        for w in range(wide):
            c = w % 2
            for z in range(section):
                target = (w - c + z // 2) * section + 2 * c + (z % 2 ^ flip)
                if target != w * section + z:
                    pairs.append((w * section + z, target))
        routes.append(pairs)
    return routes


def copy_kernel(info, source, *refs):
    refs[-1][...] = source[...]


def pick(info, shard, flip, after=()):
    items, rows, *cell = shard.shape
    anywhere = pl.BlockSpec(memory_space=pl.ANY)
    return call(
        copy_kernel,
        rows // ROWS,
        [pl.BlockSpec((None, ROWS, *cell), lambda j, s: (s[1] ^ flip, j, 0, 0))] + [anywhere] * len(after),
        pl.BlockSpec((ROWS, *cell), lambda j, s: (j, 0, 0)),
        jax.ShapeDtypeStruct((rows, *cell), F32),
        [],
        0,
        0,
        "pick",
        16,
    )(info, shard, *after)


def pass_kernel(count, *refs):
    pass


def passed(values, after):
    anywhere = pl.BlockSpec(memory_space=pl.ANY)
    return pl.pallas_call(
        functools.partial(pass_kernel, len(values)),
        in_specs=[anywhere] * (len(values) + len(after)),
        out_specs=[anywhere] * len(values),
        out_shape=[jax.ShapeDtypeStruct(v.shape, v.dtype) for v in values],
        input_output_aliases={i: i for i in range(len(values))},
        name="passed",
    )(*values, *after)


def send_piece(piece, route):
    return lax.ppermute(piece, BOTH, route)


def join_kernel(sources, info, *refs):
    values = refs[0][...]
    if sources == 2:
        values = jnp.where(info[2] == 1, values, refs[1][...])
    refs[-1][...] = values


def join(info, own, first, second, after=()):
    rows, *cell = first.shape
    anywhere = pl.BlockSpec(memory_space=pl.ANY)
    shape = jax.ShapeDtypeStruct((2, rows, *cell), F32)

    def part(flip, sources, specs, others):
        return call(
            functools.partial(join_kernel, len(sources)),
            rows // ROWS,
            specs + [anywhere] * len(others),
            pl.BlockSpec((None, ROWS, *cell), lambda j, s: (s[1] ^ flip, j, 0, 0)),
            shape,
            [],
            0,
            0,
            f"join_{flip}",
            16,
            {1 + len(sources): 0} if flip else None,
        )(info, *sources, *others)

    mine = pl.BlockSpec((ROWS, *cell), lambda j, s: (j * s[2], 0, 0))
    sent = pl.BlockSpec((ROWS, *cell), lambda j, s: (j * (1 - s[2]), 0, 0))
    row = pl.BlockSpec((ROWS, *cell), lambda j, s: (j, 0, 0))
    half = part(0, [own, first], [mine, sent], list(after))
    return part(1, [second], [row], [half])


def as_one(function, *args):
    def empty(*args):
        return jax.tree.map(lambda leaf: jnp.zeros(leaf.shape, leaf.dtype), jax.eval_shape(function, *args))

    return lax.cond(lax.axis_index("wide") < lax.axis_size("wide"), function, empty, *args)


def swap(values):
    return lax.ppermute(values, "wide", [(i, i ^ 1) for i in range(lax.axis_size("wide"))])


def digits(size, low, most):
    found = []
    while 1 << low < size:
        radix = most if most << low <= size else 2
        found.append((low, radix))
        low += radix.bit_length() - 1
    return found


def partners(axis, bit, offset):
    return [(i, i ^ offset << bit) for i in range(lax.axis_size(axis))]


def sum_spread(values, axis, bit, radix):
    me = (lax.axis_index(axis) >> bit) % radix
    parts = values.reshape((radix, -1) + values.shape[1:])
    total = lax.dynamic_index_in_dim(parts, me, 0, keepdims=False)
    for offset in range(1, radix):
        part = lax.dynamic_index_in_dim(parts, me ^ offset, 0, keepdims=False)
        total = total + lax.ppermute(part, axis, partners(axis, bit, offset))
    return total


def collect(values, axis, bit, radix):
    me = (lax.axis_index(axis) >> bit) % radix
    out = jnp.zeros((radix,) + values.shape, F32)
    for offset in range(radix):
        got = lax.ppermute(values, axis, partners(axis, bit, offset)) if offset else values
        out = lax.dynamic_update_index_in_dim(out, got, me ^ offset, 0)
    return out.reshape((-1,) + values.shape[1:])


def spread_steps(axis, low, most):
    return [(axis, *digit) for digit in digits(lax.axis_size(axis), low, most)]


def sum_spread_all(values, steps):
    for step in steps:
        values = sum_spread(values, *step)
    return values


def collect_all(values, steps):
    for step in steps[::-1]:
        values = collect(values, *step)
    return values


def turned(steps):
    return steps, steps[1:] + steps[:1]


def sum_spread_halves(values, steps):
    halves = jnp.split(values, 2)
    for pair in zip(*turned(steps)):
        halves = [sum_spread(half, *step) for half, step in zip(halves, pair)]
    return jnp.concatenate(halves)


def collect_halves(values, steps):
    halves = jnp.split(values, 2)
    for pair in list(zip(*turned(steps)))[::-1]:
        halves = [collect(half, *step) for half, step in zip(halves, pair)]
    return jnp.concatenate(halves)


def packed_rows(parts, unit):
    rows = [part.reshape(-1, 128) for part in parts]
    missing = -sum(row.shape[0] for row in rows) % unit
    return jnp.concatenate(rows + [jnp.zeros((missing, 128), F32)])


def unpack_kernel(info, mine, other, second, *outs):
    gain_out, bias_out, mix_out, offset_out, up_out, up_offset_out, down_out, down_offset_out = outs
    core = info[0]

    def low_high(start, count):
        a, b = mine[start : start + count], other[start : start + count]
        return jnp.where(core == 0, a, b), jnp.where(core == 0, b, a)

    width = up_out.shape[1]
    rows, lanes = width + SMALL_ROWS, width // 128
    down_at, mix_at = lanes * rows, 2 * lanes * rows
    first_mix = lanes * rows
    inner_at = first_mix + 8 * 128 + 16
    for index in range(lanes):
        at = pl.ds(index * 128, 128)
        begin = index * rows
        up_out[0, :, at], down_out[0, :, at] = low_high(begin, width)
        up_out[1, :, at] = second[begin : begin + width]
        down_out[1, :, at] = second[down_at + begin : down_at + begin + width]
        small = low_high(begin + width, 8)[0]
        late = second[begin + width : begin + width + 8]
        low, high = low_high(inner_at + 8 * index, 8)
        inner = low + high
        gain_out[0, 0:1, at] = inner[0:1]
        bias_out[0, 0:1, at] = inner[1:2]
        gain_out[0, 1:2, at] = small[0:1]
        bias_out[0, 1:2, at] = small[1:2]
        gain_out[1, 0:1, at] = small[4:5]
        bias_out[1, 0:1, at] = small[5:6]
        gain_out[1, 1:2, at] = late[0:1]
        bias_out[1, 1:2, at] = late[1:2]
        up_offset_out[0:1, at] = small[2:3]
        up_offset_out[1:2, at] = late[2:3]
        down_offset_out[0:1, at] = small[3:4]
        down_offset_out[1:2, at] = late[3:4]
    for block in range(BLOCKS):
        late = second[mix_at + (4 * BLOCKS) * 128 + 8 * block : mix_at + (4 * BLOCKS) * 128 + 8 * block + 8]
        for j in range(2):
            for part in range(2):
                begin = mix_at + ((2 * j + part) * BLOCKS + block) * 128
                mix_out[1, j, part, block] = second[begin : begin + 128]
                offset_out[1, j, part, block : block + 1] = late[2 * j + part : 2 * j + part + 1]
    for block in range(2):
        offsets = low_high(first_mix + 8 * 128 + 8 * block, 8)
        for j in range(2):
            for part in range(2):
                weights = low_high(first_mix + ((2 * j + part) * 2 + block) * 128, 128)
                for half in range(2):
                    at = 2 * half + block
                    mix_out[0, j, part, at] = weights[half]
                    offset_out[0, j, part, at : at + 1] = offsets[half][2 * j + part : 2 * j + part + 1]


def unpack(info, args, shapes):
    def whole(shape):
        return pl.BlockSpec(shape, lambda j, s: (0,) * len(shape))

    return call(
        unpack_kernel,
        1,
        [whole(arg.shape) for arg in args],
        [whole(shape) for shape in shapes],
        [jax.ShapeDtypeStruct(shape, F32) for shape in shapes],
        [],
        0,
        0,
        "unpack",
        40,
    )(info, *args)


def on_device(
    inputs,
    norm_gain,
    norm_bias,
    mix_weight,
    mix_bias,
    up_weight,
    up_bias,
    down_weight,
    down_bias,
    out_grad,
):
    width, hidden = up_weight.shape[1:]
    plan = Plan(inputs.shape[1], width, hidden)
    routes = item_routes(lax.axis_size("wide"), lax.axis_size("section"))
    core = lax.axis_index("wide") % 2
    section = lax.axis_index("section")
    info = jnp.stack([core, section % 2, section // 2 == core]).astype(jnp.int32)
    plain, weighted = column_tables()
    tables = [jnp.asarray(split_table(t)) for t in (plain, weighted, plain.T, weighted.T)]

    back_routes = [[(b, a) for a, b in route] for route in routes]
    ffn_args = (norm_gain, norm_bias, up_weight, up_bias, down_weight, down_bias)
    back_args = (norm_gain, norm_bias, up_weight, down_weight)

    devices = lax.axis_size("wide") * lax.axis_size("section")
    members = spread_steps("wide", 1, 2)
    sections = spread_steps("section", 0, 2)
    matrix_rows = 2 * (width // 128) * (hidden + SMALL_ROWS)
    second_rows = matrix_rows + 4 * BLOCKS * 128 + 8 * BLOCKS
    second_rows += -second_rows % (8 * devices)

    def forward(x):
        keep, send = first_norm(plan, info, x, norm_gain, norm_bias)
        keep, send, *saved0 = spectral_forward(plan, 0, info, keep, swap(send), mix_weight, mix_bias, tables)
        u0, a0, x1, keep, send = ffn_forward(plan, 0, True, info, x, keep, swap(send), *ffn_args)
        keep, send, *saved1 = spectral_forward(plan, 1, info, keep, swap(send), mix_weight, mix_bias, tables)
        u1, a1, va, vb = ffn_forward(plan, 1, False, info, (x1,), keep, swap(send), *ffn_args)
        return (va, vb), (saved0, u0, a0, x1, saved1, u1, a1)

    def backward(x, grads, started, saved):
        saved0, u0, a0, x1, saved1, u1, a1 = saved
        keep, send, packed = ffn_backward(plan, 1, info, u1, a1, *back_args, grads, 1, started, second_rows)
        dh_keep, dh_send, packed = spectral_backward(
            plan, 1, info, keep, swap(send), mix_weight, saved1, tables, packed, matrix_rows
        )
        late = (x1, keep, send, dh_keep, swap(dh_send))
        second = lax.psum_scatter(packed, "wide", scatter_dimension=0, tiled=True)
        return *as_one(backward_first, x, late, (saved0, u0, a0)), second

    def backward_first(x, late, saved):
        saved0, u0, a0 = saved
        keep, send, kept, sent = ffn_backward(plan, 0, info, u0, a0, *back_args, late)
        dh_keep, dh_send, mix, offsets = spectral_backward(plan, 0, info, keep, swap(send), mix_weight, saved0, tables)
        last = ((keep, send), (dh_keep, swap(dh_send)))
        dxa, dxb, inner = input_gradient(plan, info, x, *last, norm_gain)
        return (dxa, dxb), (kept, sent, mix, offsets, inner)

    def reduce_first(kept, sent, mix, offsets, inner, outputs):
        inner = inner.reshape(8, -1, 128).transpose(1, 0, 2)
        first = packed_rows([kept + swap(sent), mix, offsets, inner], 8 * devices)
        first = sum_spread_all(sum_spread_halves(first, members), sections[:1])
        outputs = join(info, *outputs)
        [first] = passed([first], [outputs])
        first = sum_spread_all(first, sections[1:])
        return collect_all(first, sections), outputs

    def reduce_gradients(local, second, outputs):
        second = lax.psum(second, "section")
        return *as_one(reduce_first, *local, outputs), second

    def share_first(first):
        summed = collect_halves(first, members)
        return summed, swap(summed)

    def share_gradients(first, second):
        second = lax.all_gather(second, "wide", axis=0, tiled=True)
        return *as_one(share_first, first), second

    def send_both(pieces, routes):
        return [send_piece(piece, route) for piece, route in zip(pieces, routes)]

    x = (inputs, *send_both((pick(info, inputs, 0), pick(info, inputs, 1)), routes))
    picked_grads = pick(info, out_grad, 0), pick(info, out_grad, 1)
    grads = (out_grad, *send_both(passed(picked_grads, x[1:]), routes))
    results, saved = as_one(forward, x)
    started = ffn_backward(plan, 1, info, *saved[-2:], *back_args, grads[:2])
    results = passed(results, [grads[2], started[-1]])
    outputs = (results[0], *send_both(results, back_routes))
    (dxa, dxb), local, second = as_one(backward, x, grads[2:], started, saved)
    [dxa] = passed([dxa], outputs[1:])
    returned = send_piece(dxa, back_routes[0])
    first, outputs, second = as_one(reduce_gradients, local, second, outputs)
    dxb = send_piece(*passed([dxb], [returned, first]), back_routes[1])
    mine, other, second = as_one(share_gradients, first, second)
    shapes = [a.shape for a in (norm_gain, norm_bias, mix_weight, mix_bias, up_weight, up_bias, down_weight, down_bias)]
    gradients = unpack(info, [mine, other, second], shapes)
    return (outputs, join(info, dxa, returned, dxb), *gradients)


def solution(mesh):
    cells = P("wide", "section", None, None)
    return jax.shard_map(
        on_device,
        mesh=mesh,
        in_specs=(cells, P(), P(), P(), P(), P(), P(), P(), P(), cells),
        out_specs=(cells, cells, P(), P(), P(), P(), P(), P(), P(), P()),
        check_vma=False,
    )
```

```python
import functools
import math

import jax
import jax.numpy as jnp
import numpy as np
from jax import lax
from jax.experimental import pallas as pl
from jax.experimental.pallas import tpu as pltpu
from jax.sharding import PartitionSpec as P

BLOCKS = 4
GRID = 64
MODES = 32
EPSILON = 1e-05
THRESHOLD = 0.05
ROWS = 8
SMALL_ROWS = 32
F32 = jnp.float32
BF16 = jnp.bfloat16
BOTH = ("wide", "section")


def split_table(table):
    table = table.astype(np.float32)
    high = table.astype(jnp.bfloat16)
    low = (table - high.astype(np.float32)).astype(jnp.bfloat16)
    return np.concatenate([high, high, low, low], axis=1)


def column_tables():
    columns = np.arange(MODES)
    angles = 2.0 * math.pi * (columns[:, None] * np.arange(GRID)[None, :] % GRID) / GRID
    plain = np.concatenate([np.cos(angles), np.sin(angles)], axis=0) / GRID
    factor = np.where(columns == 0, 1.0, 2.0)
    weighted = plain * np.concatenate([factor, factor])[:, None]
    return plain, weighted


def twiddle(index, length):
    angle = 2.0 * math.pi * index / length
    return math.cos(angle), math.sin(angle)


def half_spectrum(planes, pruned=False):
    length = len(planes)
    if length == 2:
        return [(planes[0] + planes[1], None), (planes[0] - planes[1], None)]
    even = half_spectrum(planes[0::2])
    odd = half_spectrum(planes[1::2])
    quarter = length // 4
    first, second = [], []
    for k in range(quarter + 1):
        (er, ei), (dr, di) = even[k], odd[k]
        if k == 0:
            first.append((er + dr, None))
            second.append((er - dr, None))
            continue
        if k == quarter:
            first.append((er, -dr))
            continue
        c, s = twiddle(k, length)
        if 2 * k == quarter:
            tr, ti = (dr + di) * c, (di - dr) * c
        else:
            tr, ti = dr * c + di * s, di * c - dr * s
        first.append((er + tr, ei + ti))
        second.append((er - tr, ti - ei))
    if pruned:
        return first
    return first + second[::-1]


def half_synthesis(spectrum, length, pruned=False):
    if length == 2:
        (a, _), (b, _) = spectrum
        return [a + b, a - b]
    quarter = length // 4
    even, odd = [], []
    for k in range(quarter + 1):
        ar, ai = spectrum[k]
        if k == quarter:
            even.append((ar, None))
            odd.append((-ai, None))
            continue
        if k == 0:
            if pruned:
                even.append((ar, None))
                odd.append((ar, None))
            else:
                br = spectrum[length // 2][0]
                even.append((ar + br, None))
                odd.append((ar - br, None))
            continue
        if pruned:
            sr, si, tr, ti = ar, ai, ar, ai
        else:
            br, bi = spectrum[length // 2 - k]
            sr, si, tr, ti = ar + br, ai - bi, ar - br, ai + bi
        even.append((sr, si))
        c, s = twiddle(k, length)
        if 2 * k == quarter:
            odd.append(((tr - ti) * c, (ti + tr) * c))
        else:
            odd.append((tr * c - ti * s, ti * c + tr * s))
    even_planes = half_synthesis(even, length // 2)
    odd_planes = half_synthesis(odd, length // 2)
    planes = []
    for e, o in zip(even_planes, odd_planes):
        planes += [e, o]
    return planes


def exact_dot(left, right, left_dim, right_dim):
    return lax.dot_general(
        left,
        right,
        (((left_dim,), (right_dim,)), ((), ())),
        precision=lax.Precision.HIGH,
        preferred_element_type=F32,
    )


def split(values):
    high = values.astype(BF16)
    low = (values - high.astype(F32)).astype(BF16)
    return high, low


def table_dot(table, values):
    high, low = split(values)
    stacked = jnp.concatenate([high, low, high, low], axis=0)
    return jnp.dot(table, stacked, preferred_element_type=F32)


def gelu(values):
    return 0.5 * values * (1.0 + lax.erf(values * math.sqrt(0.5)))


def gelu_and_slope(values):
    cumulative = 0.5 * (1.0 + lax.erf(values * math.sqrt(0.5)))
    density = jnp.exp(-0.5 * values * values) * (1.0 / math.sqrt(2.0 * math.pi))
    return values * cumulative, cumulative + values * density


def normalise(values):
    average = jnp.mean(values, axis=-1, keepdims=True)
    centered = values - average
    variance = jnp.mean(centered * centered, axis=-1, keepdims=True)
    scale = lax.rsqrt(variance + EPSILON)
    return centered * scale, scale


def norm_backward(grad, unit, scale, gains):
    inner = grad * gains
    mean_inner = jnp.mean(inner, axis=-1, keepdims=True)
    mean_unit = jnp.mean(inner * unit, axis=-1, keepdims=True)
    return scale * (inner - mean_inner - unit * mean_unit)


def column_sum(values):
    return jnp.sum(values, axis=0, keepdims=True)


def joined(core, kept, other):
    shape = (kept.shape[0] * kept.shape[1], kept.shape[2])
    kept, other = kept[...].reshape(shape), other[...].reshape(shape)
    first = jnp.where(core == 0, kept, other)
    second = jnp.where(core == 0, other, kept)
    return jnp.concatenate([first, second], axis=1)


def parted(core, values, kept, other):
    half = values.shape[1] // 2
    first, second = values[:, :half], values[:, half:]
    kept[...] = jnp.where(core == 0, first, second).reshape(kept.shape)
    other[...] = jnp.where(core == 0, second, first).reshape(other.shape)


def flat(ref):
    return ref[...].reshape(-1, ref.shape[-1])


def picked(info, step, steps, refs):
    if len(refs) == 1:
        return flat(refs[0])
    own, first, second = refs
    first = jnp.where(info[2] == 1, flat(own), flat(first))
    return jnp.where(step < steps // 2, first, flat(second))


def put_pieces(step, steps, refs, values):
    if len(refs) == 1:
        refs[0][...] = values.reshape(refs[0].shape)
        return

    @pl.when(step < steps // 2)
    def _():
        refs[0][...] = values.reshape(refs[0].shape)

    @pl.when(step >= steps // 2)
    def _():
        refs[1][...] = values.reshape(refs[1].shape)


def analyse(own, recv, table, sign, planes, modes):
    def rows(index, _):
        at = pl.ds(pl.multiple_of(index * 8, 8), 8)
        loaded = [own[p, at, :] for p in range(GRID // 2)] + [recv[p, at, :] for p in range(GRID // 2)]
        for k, (re, im) in enumerate(half_spectrum(loaded, pruned=True)):
            im = jnp.zeros_like(re) if im is None else im
            if k % 2:
                re, im = re * sign, im * sign
            planes[k, at, :] = jnp.concatenate([re, im], axis=1)
        return 0

    lax.fori_loop(0, GRID // 8, rows, 0)
    for k in range(MODES // 2 + 1):
        found = table_dot(table[...], planes[k])
        lanes = found.shape[1] // 2
        cr, ci = found[:MODES, :lanes], found[:MODES, lanes:]
        sr, si = found[MODES:, :lanes], found[MODES:, lanes:]
        if k < MODES // 2:
            modes[k * MODES : (k + 1) * MODES, :] = jnp.concatenate([cr + si, ci - sr], axis=1)
        if k > 0:
            place = MODES - k
            modes[place * MODES : (place + 1) * MODES, :] = jnp.concatenate([cr - si, -ci - sr], axis=1)


def synthesise(modes, table, sign, planes, keep, send):
    lanes = modes.shape[1] // 2
    for k in range(MODES // 2 + 1):
        place = MODES - k
        if k == 0:
            above, below = modes[0:MODES, :], None
            total, apart = above, above
        elif k == MODES // 2:
            below = modes[place * MODES : (place + 1) * MODES, :]
            total, apart = below, -below
        else:
            above = modes[k * MODES : (k + 1) * MODES, :]
            below = modes[place * MODES : (place + 1) * MODES, :]
            total, apart = above + below, above - below
        upper = jnp.concatenate([total[:, :lanes], apart[:, lanes:]], axis=1)
        lower = jnp.concatenate([-total[:, lanes:], apart[:, :lanes]], axis=1)
        planes[k] = table_dot(table[...], jnp.concatenate([upper, lower], axis=0))

    def rows(index, _):
        at = pl.ds(pl.multiple_of(index * 8, 8), 8)
        spectrum = []
        for k in range(MODES // 2 + 1):
            both = planes[k, at, :]
            if k % 2:
                both = both * sign
            spectrum.append((both[:, :lanes], both[:, lanes:]))
        cells = half_synthesis(spectrum, GRID, pruned=True)
        for p in range(GRID // 2):
            keep[p, at, :] = cells[p]
            send[p, at, :] = cells[GRID // 2 + p]
        return 0

    lax.fori_loop(0, GRID // 8, rows, 0)


def place_weights(weight, stacked):
    lanes = weight.shape[-1]
    for j in range(2):
        real, imag = weight[j, 0], weight[j, 1]
        stacked[j, :lanes, :lanes] = real
        stacked[j, :lanes, lanes:] = imag
        stacked[j, lanes:, :lanes] = -imag
        stacked[j, lanes:, lanes:] = real


MIX_ROWS = 256


def mix_offsets(offset, block):
    at = pl.ds(block, 1)
    return [jnp.concatenate([offset[j, 0, at, :], offset[j, 1, at, :]], axis=1) for j in range(2)]


def spectral_forward_kernel(
    info, own, recv, weight, offset, table_in, table_out, keep, send, modes, before, after, planes, shrunk, stacked
):
    core = info[0]
    sign = jnp.where(core == 1, -1.0, 1.0).astype(F32)
    place_weights(weight, stacked)
    first_offset, second_offset = mix_offsets(offset, 2 * core + pl.program_id(0))
    analyse(own, recv, table_in, sign, planes, modes)

    def mix(index, _):
        at = pl.ds(pl.multiple_of(index * MIX_ROWS, MIX_ROWS), MIX_ROWS)
        first = exact_dot(modes[at, :], stacked[0], 1, 0) + first_offset
        before[at, :] = first
        second = exact_dot(gelu(first), stacked[1], 1, 0) + second_offset
        after[at, :] = second
        shrunk[at, :] = second - THRESHOLD * jnp.tanh(second * (1.0 / THRESHOLD))
        return 0

    lax.fori_loop(0, MODES * MODES // MIX_ROWS, mix, 0)
    synthesise(shrunk, table_out, sign, planes, keep, send)


def spectral_backward_kernel(
    start, info, own, recv, weight, modes, before, after, table_in, table_out, *refs
):
    if start is None:
        keep, send, weight_grad, offset_grad, planes, flowing, stacked, summed = refs
    else:
        _, keep, send, out, planes, flowing, stacked, summed, weight_grad, offset_grad, blank, sems = refs
    core = info[0]
    sign = jnp.where(core == 1, -1.0, 1.0).astype(F32)
    place_weights(weight, stacked)
    analyse(own, recv, table_in, sign, planes, flowing)
    summed[...] = jnp.zeros_like(summed)

    def mix(index, totals):
        at = pl.ds(pl.multiple_of(index * MIX_ROWS, MIX_ROWS), MIX_ROWS)
        ratio = jnp.tanh(after[at, :] * (1.0 / THRESHOLD))
        grad_second = flowing[at, :] * ratio * ratio
        hidden, slope = gelu_and_slope(before[at, :])
        summed[1] += exact_dot(hidden, grad_second, 0, 0)
        grad_first = exact_dot(grad_second, stacked[1], 1, 1) * slope
        summed[0] += exact_dot(modes[at, :], grad_first, 0, 0)
        flowing[at, :] = exact_dot(grad_first, stacked[0], 1, 1)
        return totals[0] + column_sum(grad_first), totals[1] + column_sum(grad_second)

    empty = jnp.zeros((1, flowing.shape[1]), F32)
    totals = lax.fori_loop(0, MODES * MODES // MIX_ROWS, mix, (empty, empty))
    lanes = flowing.shape[1] // 2
    offset_grad[...] = jnp.zeros_like(offset_grad)
    for j in range(2):
        offset_grad[2 * j : 2 * j + 1] = totals[j][:, :lanes]
        offset_grad[2 * j + 1 : 2 * j + 2] = totals[j][:, lanes:]
        weight_grad[j, 0] = summed[j, :lanes, :lanes] + summed[j, lanes:, lanes:]
        weight_grad[j, 1] = summed[j, :lanes, lanes:] - summed[j, lanes:, :lanes]
    if start is not None:
        block, other = 2 * core + pl.program_id(0), 2 * (1 - core) + pl.program_id(0)
        blank[...] = jnp.zeros_like(blank)
        copies = []
        for index in range(4):
            for source, place in ((weight_grad.at[index // 2, index % 2], block), (blank, other)):
                at = pl.ds(pl.multiple_of(start + (index * BLOCKS + place) * 128, 8), 128)
                copies.append(pltpu.make_async_copy(source, out.at[at], sems.at[len(copies)]))
        for source, place in ((offset_grad, block), (blank.at[pl.ds(0, 8)], other)):
            at = pl.ds(pl.multiple_of(start + 4 * BLOCKS * 128 + place * 8, 8), 8)
            copies.append(pltpu.make_async_copy(source, out.at[at], sems.at[len(copies)]))
        for copy in copies:
            copy.start()
    synthesise(flowing, table_out, sign, planes, keep, send)
    if start is not None:
        for copy in copies:
            copy.wait()


def first_norm_kernel(steps, info, own, a, b, gains, biases, keep, send):
    unit, _ = normalise(picked(info, pl.program_id(0), steps, (own, a, b)))
    parted(info[0], unit * gains[0:1] + biases[0:1], keep, send)


def ffn_forward_kernel(steps, layer, pieces, more, info, *refs):
    step = pl.program_id(0)
    refs = list(refs)
    x_refs, refs = refs[:pieces], refs[pieces:]
    kept, taken, gains, biases, up, up_offset, down, down_offset = refs[:8]
    refs = refs[8:]
    core = info[0]
    mixed = picked(info, step, steps, x_refs) + joined(core, kept, taken)
    unit, _ = normalise(mixed)
    normed = unit * gains[1:2] + biases[1:2]
    before = exact_dot(normed, up[...], 1, 0) + up_offset[layer : layer + 1]
    result = mixed + exact_dot(gelu(before), down[...], 1, 0) + down_offset[layer : layer + 1]
    if more:
        next_gains, next_biases, mixed_out, before_out, result_out, keep, send = refs
        put_pieces(step, steps, (result_out,), result)
        unit, _ = normalise(result)
        parted(core, unit * next_gains[0:1] + next_biases[0:1], keep, send)
    else:
        mixed_out, before_out, first_out, second_out = refs
        put_pieces(step, steps, (first_out, second_out), result)
    mixed_out[...] = mixed.reshape(mixed_out.shape)
    before_out[...] = before.reshape(before_out.shape)


def first_norm_backward(core, x, du_kept, du_sent, dh_kept, dh_taken, gains):
    grad = joined(core, dh_kept, dh_taken)
    unit, scale = normalise(x)
    result = joined(core, du_kept, du_sent) + norm_backward(grad, unit, scale, gains[0:1])
    return result, column_sum(grad * unit), column_sum(grad)


def lanes_first(values):
    return [values[:, at : at + 128] for at in range(0, values.shape[1], 128)]


def ffn_backward_kernel(steps, fused, part, info, *refs):
    step = pl.program_id(0)
    core = info[0]
    refs = list(refs)
    mixed, before, gains, biases, up, down = refs[:6]
    if fused:
        x, du_kept, du_sent, dh_kept, dh_taken, next_gains = refs[6:12]
        grad, late_gain, late_bias = first_norm_backward(core, flat(x), du_kept, du_sent, dh_kept, dh_taken, next_gains)
        refs = refs[12:]
    else:
        grad = flat(refs[6]) if part else jnp.where(info[2] == 1, flat(refs[6]), flat(refs[7]))
        refs = refs[7:] if part else refs[8:]
    if fused:
        keep, send, kept_grads, sent_grads, up_grad, down_grad, small = refs
    elif part == 0:
        keep, send, up_grad, down_grad, small = refs
    else:
        *started, _, _, keep, send, out, lined, sem, up_grad, down_grad, small = refs
        kept_grads, sent_grads = lined.at[0], lined.at[1]

    @pl.when(step == 0)
    def _():
        for index, total in enumerate((up_grad, down_grad, small)):
            total[...] = started[index][...] if part else jnp.zeros_like(total)

    unit, scale = normalise(flat(mixed))
    normed = unit * gains[1:2] + biases[1:2]
    hidden, slope = gelu_and_slope(flat(before))
    down_grad[...] += exact_dot(hidden, grad, 0, 0)
    inner = exact_dot(grad, down[...], 1, 1) * slope
    up_grad[...] += exact_dot(normed, inner, 0, 0)
    outer = exact_dot(inner, up[...], 1, 1)
    small[0:1] += column_sum(outer * unit)
    small[1:2] += column_sum(outer)
    small[2:3] += column_sum(inner)
    small[3:4] += column_sum(grad)
    if fused:
        small[4:5] += late_gain
        small[5:6] += late_bias
    parted(core, grad + norm_backward(outer, unit, scale, gains[1:2]), keep, send)
    if part == 0 and not fused:
        return

    @pl.when(step == steps - 1)
    def _():
        width = up_grad.shape[0]
        parts = zip(lanes_first(up_grad[...]), lanes_first(down_grad[...]), lanes_first(small[...]))
        for index, (a, b, c) in enumerate(parts):
            kept_grads[index, :width] = jnp.where(core == 0, a, b) if fused else a
            sent_grads[index, :width] = jnp.where(core == 0, b, a) if fused else b
            for grads in (kept_grads, sent_grads):
                grads[index, width : width + 8] = c
                grads[index, width + 8 :] = jnp.zeros((SMALL_ROWS - 8, 128), F32)
        if not fused:
            lines = out.at[pl.ds(0, lined.size // 128)].reshape(lined.shape)
            copy = pltpu.make_async_copy(lined, lines, sem)
            copy.start()
            copy.wait()


def input_grad_kernel(steps, info, own, a, b, du_kept, du_sent, dh_kept, dh_taken, gains, first_out, second_out, small):
    step = pl.program_id(0)
    x = picked(info, step, steps, (own, a, b))
    result, gain_sum, bias_sum = first_norm_backward(info[0], x, du_kept, du_sent, dh_kept, dh_taken, gains)

    @pl.when(step == 0)
    def _():
        small[...] = jnp.zeros_like(small)

    small[0:1] += gain_sum
    small[1:2] += bias_sum
    put_pieces(step, steps, (first_out, second_out), result)


def call(kernel, grid, in_specs, out_specs, out_shapes, scratch, flops, moved, name, vmem=30, aliases=None):
    return pl.pallas_call(
        kernel,
        grid_spec=pltpu.PrefetchScalarGridSpec(
            num_scalar_prefetch=1,
            grid=(grid,),
            in_specs=in_specs,
            out_specs=out_specs,
            scratch_shapes=scratch,
        ),
        out_shape=out_shapes,
        input_output_aliases=aliases or {},
        compiler_params=pltpu.CompilerParams(vmem_limit_bytes=vmem * 2**20),
        cost_estimate=pl.CostEstimate(flops=int(flops), bytes_accessed=int(moved), transcendentals=0),
        name=name,
    )


class Plan:
    def __init__(self, quarter, width, hidden):
        self.quarter, self.width, self.hidden = quarter, width, hidden
        self.steps = 2 * quarter // ROWS
        per_piece = quarter // ROWS
        half = width // 2

        def local(j, s):
            return (j, 0, 0)

        def canonical(j, s):
            return (((j // per_piece) ^ s[1]) * per_piece + j % per_piece, 0, 0)

        self.row = pl.BlockSpec((ROWS, GRID, width), local)
        self.wide_row = pl.BlockSpec((ROWS, GRID, hidden), local)
        self.half_row = pl.BlockSpec((ROWS, GRID, half), canonical)
        self.first = pl.BlockSpec((ROWS, GRID, width), lambda j, s: (jnp.minimum(j, per_piece - 1), 0, 0))
        self.pieces = [
            pl.BlockSpec((None, ROWS, GRID, width), lambda j, s: (s[1], jnp.minimum(j, per_piece - 1) * s[2], 0, 0)),
            pl.BlockSpec((ROWS, GRID, width), lambda j, s: (jnp.minimum(j, per_piece - 1) * (1 - s[2]), 0, 0)),
            pl.BlockSpec((ROWS, GRID, width), lambda j, s: (jnp.maximum(j - per_piece, 0), 0, 0)),
        ]
        self.second = pl.BlockSpec((ROWS, GRID, width), lambda j, s: (jnp.maximum(j - per_piece, 0), 0, 0))
        self.half_shape = jax.ShapeDtypeStruct((2 * quarter, GRID, half), F32)
        self.row_shape = jax.ShapeDtypeStruct((2 * quarter, GRID, width), F32)
        self.wide_shape = jax.ShapeDtypeStruct((2 * quarter, GRID, hidden), F32)
        self.piece_shape = jax.ShapeDtypeStruct((quarter, GRID, width), F32)

    def norm(self, layer):
        return pl.BlockSpec((None, 2, self.width), lambda j, s: (layer, 0, 0))

    def matrix(self, layer, rows, columns):
        return pl.BlockSpec((None, rows, columns), lambda j, s: (layer, 0, 0))

    def whole(self, shape):
        return pl.BlockSpec(shape, lambda j, s: (0,) * len(shape))


def first_norm(plan, info, pieces, gains, biases):
    return call(
        functools.partial(first_norm_kernel, plan.steps),
        plan.steps,
        [*plan.pieces, plan.norm(0), plan.norm(0)],
        [plan.half_row, plan.half_row],
        [plan.half_shape, plan.half_shape],
        [],
        0,
        4 * 2**20 * 2,
        "first_norm",
    )(info, *pieces, gains, biases)


def spectral_specs(layer, width):
    block = width // BLOCKS
    cells = pl.BlockSpec((GRID // 2, GRID, block), lambda b, s: (0, 0, b))
    weight = pl.BlockSpec((None, 2, 2, None, block, block), lambda b, s: (layer, 0, 0, 2 * s[0] + b, 0, 0))
    offset = pl.BlockSpec((None, 2, 2, BLOCKS, block), lambda b, s: (layer, 0, 0, 0, 0))
    table = pl.BlockSpec((GRID, 4 * GRID), lambda b, s: (0, 0))
    modes = pl.BlockSpec((None, MODES * MODES, 2 * block), lambda b, s: (b, 0, 0))
    modes_shape = jax.ShapeDtypeStruct((2, MODES * MODES, 2 * block), F32)
    planes = pltpu.VMEM((MODES // 2 + 1, GRID, 2 * block), F32)
    flowing = pltpu.VMEM((MODES * MODES, 2 * block), F32)
    stacked = pltpu.VMEM((2, 2 * block, 2 * block), F32)
    return block, cells, weight, offset, table, modes, modes_shape, planes, flowing, stacked


def spectral_forward(plan, layer, info, own, recv, weight_all, offset_all, tables):
    block, cells, weight, offset, table, modes, modes_shape, planes, flowing, stacked = spectral_specs(layer, plan.width)
    return call(
        spectral_forward_kernel,
        2,
        [cells, cells, weight, offset, table, table],
        [cells, cells, modes, modes, modes],
        [plan.half_shape, plan.half_shape, modes_shape, modes_shape, modes_shape],
        [planes, flowing, stacked],
        3 * 2e9,
        14 * 2**20,
        f"spectral_forward_{layer}",
    )(info, own, recv, weight_all, offset_all, tables[0], tables[3])


def spectral_backward(plan, layer, info, own, recv, weight_all, saved, tables, packed=None, start=None):
    block, cells, weight, offset, table, modes, modes_shape, planes, flowing, stacked = spectral_specs(layer, plan.width)
    specs = [cells, cells, weight, modes, modes, modes, table, table]
    out_specs, out_shapes = [cells, cells], [plan.half_shape, plan.half_shape]
    scratch = [planes, flowing, stacked, pltpu.VMEM((2, 2 * block, 2 * block), F32)]
    args = [info, own, recv, weight_all, *saved, tables[1], tables[2]]
    aliases = {}
    if start is None:
        out_specs += [
            pl.BlockSpec((2, 2, None, block, block), lambda b, s: (0, 0, b, 0, 0)),
            pl.BlockSpec((None, 8, block), lambda b, s: (b, 0, 0)),
        ]
        out_shapes += [
            jax.ShapeDtypeStruct((2, 2, 2, block, block), F32),
            jax.ShapeDtypeStruct((2, 8, block), F32),
        ]
    else:
        specs.append(pl.BlockSpec(memory_space=pl.ANY))
        out_specs.append(pl.BlockSpec(memory_space=pl.ANY))
        out_shapes.append(jax.ShapeDtypeStruct(packed.shape, F32))
        aliases = {len(args): 2}
        args.append(packed)
        scratch += [pltpu.VMEM((2, 2, block, block), F32), pltpu.VMEM((8, block), F32), pltpu.VMEM((block, block), F32)]
        scratch += [pltpu.SemaphoreType.DMA((10,))]
    return call(
        functools.partial(spectral_backward_kernel, start),
        2,
        specs,
        out_specs,
        out_shapes,
        scratch,
        0,
        0,
        f"spectral_backward_{layer}",
        30,
        aliases,
    )(*args)


def ffn_forward(plan, layer, more, info, x, kept, taken, gains, biases, up, up_offset, down, down_offset):
    width, hidden = plan.width, plan.hidden
    specs = list(plan.pieces) if len(x) == 3 else [plan.row]
    specs += [plan.half_row, plan.half_row, plan.norm(layer), plan.norm(layer)]
    specs += [plan.matrix(layer, width, hidden), plan.whole(up_offset.shape)]
    specs += [plan.matrix(layer, hidden, width), plan.whole(down_offset.shape)]
    args = [*x, kept, taken, gains, biases, up, up_offset, down, down_offset]
    out_specs = [plan.row, plan.wide_row]
    out_shapes = [plan.row_shape, plan.wide_shape]
    if more:
        specs += [plan.norm(layer + 1), plan.norm(layer + 1)]
        args += [gains, biases]
        out_specs += [plan.row, plan.half_row, plan.half_row]
        out_shapes += [plan.row_shape, plan.half_shape, plan.half_shape]
    else:
        out_specs += [plan.first, plan.second]
        out_shapes += [plan.piece_shape, plan.piece_shape]
    return call(
        functools.partial(ffn_forward_kernel, plan.steps, layer, len(x), more),
        plan.steps,
        specs,
        out_specs,
        out_shapes,
        [],
        3 * 4 * 2048 * width * hidden,
        24 * 2**20,
        f"ffn_forward_{layer}",
    )(info, *args)


def ffn_backward(plan, layer, info, mixed, before, gains, biases, up, down, grads, part=0, started=(), rows=None):
    width, hidden = plan.width, plan.hidden
    fused = layer == 0
    steps = plan.steps if fused else plan.steps // 2
    start = part * steps
    anywhere = pl.BlockSpec(memory_space=pl.ANY)

    def shifted_rows(spec, lanes):
        return pl.BlockSpec((ROWS, GRID, lanes), lambda j, s: spec.index_map(j + start, s))

    specs = [shifted_rows(plan.row, width), shifted_rows(plan.wide_row, hidden), plan.norm(layer), plan.norm(layer)]
    specs += [plan.matrix(layer, width, hidden), plan.matrix(layer, hidden, width)]
    args = [info, mixed, before, gains, biases, up, down, *grads]
    if fused:
        specs += [plan.row] + [plan.half_row] * 4 + [plan.norm(layer + 1)]
        args += [gains]
    else:
        specs += [plan.row] if part else plan.pieces[:2]
    lined = (width // 128, hidden + SMALL_ROWS, 128)
    totals = ((width, hidden), (hidden, width), (8, width))
    scratch = [pltpu.VMEM(shape, F32) for shape in totals]
    aliases = None
    if fused:
        packed, packed_specs = [lined, lined], [plan.whole(lined)] * 2
    elif part == 0:
        packed, packed_specs, scratch = totals, [plan.whole(shape) for shape in totals], []
    else:
        packed, packed_specs = [(rows, 128)], [anywhere]
        scratch = [pltpu.VMEM((2, *lined), F32), pltpu.SemaphoreType.DMA] + scratch
        keep, send, *begun = started
        specs += [plan.whole(shape) for shape in totals] + [anywhere] * 2
        args += [*begun, keep, send]
        aliases = {len(args) - 2: 0, len(args) - 1: 1}
    return call(
        functools.partial(ffn_backward_kernel, steps, fused, part),
        steps,
        specs,
        [shifted_rows(plan.half_row, width // 2)] * 2 + packed_specs,
        [plan.half_shape, plan.half_shape] + [jax.ShapeDtypeStruct(shape, F32) for shape in packed],
        scratch,
        3 * 8 * 2048 * width * hidden,
        24 * 2**20,
        f"ffn_backward_{layer}_{part}",
        30,
        aliases,
    )(*args)


def input_gradient(plan, info, pieces, du, dh, gains):
    return call(
        functools.partial(input_grad_kernel, plan.steps),
        plan.steps,
        plan.pieces + [plan.half_row] * 4 + [plan.norm(0)],
        [plan.first, plan.second, plan.whole((8, plan.width))],
        [plan.piece_shape, plan.piece_shape, jax.ShapeDtypeStruct((8, plan.width), F32)],
        [],
        0,
        16 * 2**20,
        "input_gradient",
    )(info, *pieces, *du, *dh, gains)


def item_routes(wide, section):
    routes = []
    for flip in range(2):
        pairs = []
        for w in range(wide):
            c = w % 2
            for z in range(section):
                target = (w - c + z // 2) * section + 2 * c + (z % 2 ^ flip)
                if target != w * section + z:
                    pairs.append((w * section + z, target))
        routes.append(pairs)
    return routes


def copy_kernel(info, source, *refs):
    refs[-1][...] = source[...]


def pick(info, shard, flip, after=()):
    items, rows, *cell = shard.shape
    anywhere = pl.BlockSpec(memory_space=pl.ANY)
    return call(
        copy_kernel,
        rows // ROWS,
        [pl.BlockSpec((None, ROWS, *cell), lambda j, s: (s[1] ^ flip, j, 0, 0))] + [anywhere] * len(after),
        pl.BlockSpec((ROWS, *cell), lambda j, s: (j, 0, 0)),
        jax.ShapeDtypeStruct((rows, *cell), F32),
        [],
        0,
        0,
        "pick",
        16,
    )(info, shard, *after)


def pass_kernel(count, *refs):
    pass


def passed(values, after):
    anywhere = pl.BlockSpec(memory_space=pl.ANY)
    return pl.pallas_call(
        functools.partial(pass_kernel, len(values)),
        in_specs=[anywhere] * (len(values) + len(after)),
        out_specs=[anywhere] * len(values),
        out_shape=[jax.ShapeDtypeStruct(v.shape, v.dtype) for v in values],
        input_output_aliases={i: i for i in range(len(values))},
        name="passed",
    )(*values, *after)


def send_piece(piece, route):
    return lax.ppermute(piece, BOTH, route)


def join_kernel(sources, info, *refs):
    values = refs[0][...]
    if sources == 2:
        values = jnp.where(info[2] == 1, values, refs[1][...])
    refs[-1][...] = values


def join_part(info, flip, sources, others):
    rows, *cell = sources[0].shape
    anywhere = pl.BlockSpec(memory_space=pl.ANY)
    mine = pl.BlockSpec((ROWS, *cell), lambda j, s: (j * s[2], 0, 0))
    sent = pl.BlockSpec((ROWS, *cell), lambda j, s: (j * (1 - s[2]), 0, 0))
    row = pl.BlockSpec((ROWS, *cell), lambda j, s: (j, 0, 0))
    return call(
        functools.partial(join_kernel, len(sources)),
        rows // ROWS,
        ([row] if flip else [mine, sent]) + [anywhere] * len(others),
        pl.BlockSpec((None, ROWS, *cell), lambda j, s: (s[1] ^ flip, j, 0, 0)),
        jax.ShapeDtypeStruct((2, rows, *cell), F32),
        [],
        0,
        0,
        f"join_{flip}",
        16,
        {1 + len(sources): 0} if flip else None,
    )(info, *sources, *others)


def join_first(info, own, first):
    return join_part(info, 0, [own, first], [])


def join_second(info, half, second):
    return join_part(info, 1, [second], [half])


def as_one(function, *args):
    def empty(*args):
        return jax.tree.map(lambda leaf: jnp.zeros(leaf.shape, leaf.dtype), jax.eval_shape(function, *args))

    return lax.cond(lax.axis_index("wide") < lax.axis_size("wide"), function, empty, *args)


def swap(values):
    return lax.ppermute(values, "wide", [(i, i ^ 1) for i in range(lax.axis_size("wide"))])


def digits(size, low, most):
    found = []
    while 1 << low < size:
        radix = most if most << low <= size else 2
        found.append((low, radix))
        low += radix.bit_length() - 1
    return found


def partners(axis, bit, offset):
    return [(i, i ^ offset << bit) for i in range(lax.axis_size(axis))]


def sum_spread(values, axis, bit, radix):
    me = (lax.axis_index(axis) >> bit) % radix
    parts = values.reshape((radix, -1) + values.shape[1:])
    total = lax.dynamic_index_in_dim(parts, me, 0, keepdims=False)
    for offset in range(1, radix):
        part = lax.dynamic_index_in_dim(parts, me ^ offset, 0, keepdims=False)
        total = total + lax.ppermute(part, axis, partners(axis, bit, offset))
    return total


def collect(values, axis, bit, radix):
    me = (lax.axis_index(axis) >> bit) % radix
    out = jnp.zeros((radix,) + values.shape, F32)
    for offset in range(radix):
        got = lax.ppermute(values, axis, partners(axis, bit, offset)) if offset else values
        out = lax.dynamic_update_index_in_dim(out, got, me ^ offset, 0)
    return out.reshape((-1,) + values.shape[1:])


def spread_steps(axis, low, most):
    return [(axis, *digit) for digit in digits(lax.axis_size(axis), low, most)]


def sum_spread_all(values, steps):
    for step in steps:
        values = sum_spread(values, *step)
    return values


def collect_all(values, steps):
    for step in steps[::-1]:
        values = collect(values, *step)
    return values


def turned(steps):
    return steps, steps[1:] + steps[:1]


def sum_spread_halves(values, steps):
    halves = jnp.split(values, 2)
    for pair in zip(*turned(steps)):
        halves = [sum_spread(half, *step) for half, step in zip(halves, pair)]
    return jnp.concatenate(halves)


def collect_halves(values, steps):
    halves = jnp.split(values, 2)
    for pair in list(zip(*turned(steps)))[::-1]:
        halves = [collect(half, *step) for half, step in zip(halves, pair)]
    return jnp.concatenate(halves)


def packed_rows(parts, unit):
    rows = [part.reshape(-1, 128) for part in parts]
    missing = -sum(row.shape[0] for row in rows) % unit
    return jnp.concatenate(rows + [jnp.zeros((missing, 128), F32)])


def unpack_kernel(info, mine, other, second, *outs):
    gain_out, bias_out, mix_out, offset_out, up_out, up_offset_out, down_out, down_offset_out = outs
    core = info[0]

    def low_high(start, count):
        a, b = mine[start : start + count], other[start : start + count]
        return jnp.where(core == 0, a, b), jnp.where(core == 0, b, a)

    width = up_out.shape[1]
    rows, lanes = width + SMALL_ROWS, width // 128
    down_at, mix_at = lanes * rows, 2 * lanes * rows
    first_mix = lanes * rows
    inner_at = first_mix + 8 * 128 + 16
    for index in range(lanes):
        at = pl.ds(index * 128, 128)
        begin = index * rows
        up_out[0, :, at], down_out[0, :, at] = low_high(begin, width)
        up_out[1, :, at] = second[begin : begin + width]
        down_out[1, :, at] = second[down_at + begin : down_at + begin + width]
        small = low_high(begin + width, 8)[0]
        late = second[begin + width : begin + width + 8]
        low, high = low_high(inner_at + 8 * index, 8)
        inner = low + high
        gain_out[0, 0:1, at] = inner[0:1]
        bias_out[0, 0:1, at] = inner[1:2]
        gain_out[0, 1:2, at] = small[0:1]
        bias_out[0, 1:2, at] = small[1:2]
        gain_out[1, 0:1, at] = small[4:5]
        bias_out[1, 0:1, at] = small[5:6]
        gain_out[1, 1:2, at] = late[0:1]
        bias_out[1, 1:2, at] = late[1:2]
        up_offset_out[0:1, at] = small[2:3]
        up_offset_out[1:2, at] = late[2:3]
        down_offset_out[0:1, at] = small[3:4]
        down_offset_out[1:2, at] = late[3:4]
    for block in range(BLOCKS):
        late = second[mix_at + (4 * BLOCKS) * 128 + 8 * block : mix_at + (4 * BLOCKS) * 128 + 8 * block + 8]
        for j in range(2):
            for part in range(2):
                begin = mix_at + ((2 * j + part) * BLOCKS + block) * 128
                mix_out[1, j, part, block] = second[begin : begin + 128]
                offset_out[1, j, part, block : block + 1] = late[2 * j + part : 2 * j + part + 1]
    for block in range(2):
        offsets = low_high(first_mix + 8 * 128 + 8 * block, 8)
        for j in range(2):
            for part in range(2):
                weights = low_high(first_mix + ((2 * j + part) * 2 + block) * 128, 128)
                for half in range(2):
                    at = 2 * half + block
                    mix_out[0, j, part, at] = weights[half]
                    offset_out[0, j, part, at : at + 1] = offsets[half][2 * j + part : 2 * j + part + 1]


def unpack(info, args, shapes):
    def whole(shape):
        return pl.BlockSpec(shape, lambda j, s: (0,) * len(shape))

    return call(
        unpack_kernel,
        1,
        [whole(arg.shape) for arg in args],
        [whole(shape) for shape in shapes],
        [jax.ShapeDtypeStruct(shape, F32) for shape in shapes],
        [],
        0,
        0,
        "unpack",
        40,
    )(info, *args)


def on_device(
    inputs,
    norm_gain,
    norm_bias,
    mix_weight,
    mix_bias,
    up_weight,
    up_bias,
    down_weight,
    down_bias,
    out_grad,
):
    width, hidden = up_weight.shape[1:]
    plan = Plan(inputs.shape[1], width, hidden)
    routes = item_routes(lax.axis_size("wide"), lax.axis_size("section"))
    core = lax.axis_index("wide") % 2
    section = lax.axis_index("section")
    info = jnp.stack([core, section % 2, section // 2 == core]).astype(jnp.int32)
    plain, weighted = column_tables()
    tables = [jnp.asarray(split_table(t)) for t in (plain, weighted, plain.T, weighted.T)]

    back_routes = [[(b, a) for a, b in route] for route in routes]
    ffn_args = (norm_gain, norm_bias, up_weight, up_bias, down_weight, down_bias)
    back_args = (norm_gain, norm_bias, up_weight, down_weight)

    devices = lax.axis_size("wide") * lax.axis_size("section")
    members = spread_steps("wide", 1, 2)
    sections = spread_steps("section", 0, 2)
    matrix_rows = 2 * (width // 128) * (hidden + SMALL_ROWS)
    second_rows = matrix_rows + 4 * BLOCKS * 128 + 8 * BLOCKS
    second_rows += -second_rows % (8 * devices)

    def forward(x):
        keep, send = first_norm(plan, info, x, norm_gain, norm_bias)
        keep, send, *saved0 = spectral_forward(plan, 0, info, keep, swap(send), mix_weight, mix_bias, tables)
        u0, a0, x1, keep, send = ffn_forward(plan, 0, True, info, x, keep, swap(send), *ffn_args)
        keep, send, *saved1 = spectral_forward(plan, 1, info, keep, swap(send), mix_weight, mix_bias, tables)
        u1, a1, va, vb = ffn_forward(plan, 1, False, info, (x1,), keep, swap(send), *ffn_args)
        return (va, vb), (saved0, u0, a0, x1, saved1, u1, a1)

    def backward(x, grads, started, saved):
        saved0, u0, a0, x1, saved1, u1, a1 = saved
        keep, send, packed = ffn_backward(plan, 1, info, u1, a1, *back_args, grads, 1, started, second_rows)
        dh_keep, dh_send, packed = spectral_backward(
            plan, 1, info, keep, swap(send), mix_weight, saved1, tables, packed, matrix_rows
        )
        late = (x1, keep, send, dh_keep, swap(dh_send))
        second = lax.psum_scatter(packed, "wide", scatter_dimension=0, tiled=True)
        return *as_one(backward_first, x, late, (saved0, u0, a0)), second

    def backward_first(x, late, saved):
        saved0, u0, a0 = saved
        keep, send, kept, sent = ffn_backward(plan, 0, info, u0, a0, *back_args, late)
        dh_keep, dh_send, mix, offsets = spectral_backward(plan, 0, info, keep, swap(send), mix_weight, saved0, tables)
        last = ((keep, send), (dh_keep, swap(dh_send)))
        dxa, dxb, inner = input_gradient(plan, info, x, *last, norm_gain)
        return (dxa, dxb), (kept, sent, mix, offsets, inner)

    def reduce_first(kept, sent, mix, offsets, inner, outputs):
        inner = inner.reshape(8, -1, 128).transpose(1, 0, 2)
        first = packed_rows([kept + swap(sent), mix, offsets, inner], 8 * devices)
        first = sum_spread_all(sum_spread_halves(first, members), sections[:1])
        outputs = join_second(info, join_first(info, *outputs[:2]), outputs[2])
        [first] = passed([first], [outputs])
        first = sum_spread_all(first, sections[1:])
        return collect_all(first, sections), outputs

    def reduce_gradients(local, second, outputs):
        second = lax.psum(second, "section")
        return *as_one(reduce_first, *local, outputs), second

    def share_first(first, own, returned):
        half = join_first(info, own, returned)
        summed = collect_halves(first, members)
        return summed, swap(summed), half

    def share_gradients(first, second, own, returned):
        second = lax.all_gather(second, "wide", axis=0, tiled=True)
        return *as_one(share_first, first, own, returned), second

    def send_both(pieces, routes):
        return [send_piece(piece, route) for piece, route in zip(pieces, routes)]

    x = (inputs, *send_both((pick(info, inputs, 0), pick(info, inputs, 1)), routes))
    picked_grads = pick(info, out_grad, 0), pick(info, out_grad, 1)
    grads = (out_grad, *send_both(passed(picked_grads, x[1:]), routes))
    results, saved = as_one(forward, x)
    started = ffn_backward(plan, 1, info, *saved[-2:], *back_args, grads[:2])
    results = passed(results, [grads[2], started[-1]])
    outputs = (results[0], *send_both(results, back_routes))
    (dxa, dxb), local, second = as_one(backward, x, grads[2:], started, saved)
    [dxa] = passed([dxa], outputs[1:])
    returned = send_piece(dxa, back_routes[0])
    first, outputs, second = as_one(reduce_gradients, local, second, outputs)
    dxb = send_piece(*passed([dxb], [returned, first]), back_routes[1])
    mine, other, half, second = as_one(share_gradients, first, second, dxa, returned)
    shapes = [a.shape for a in (norm_gain, norm_bias, mix_weight, mix_bias, up_weight, up_bias, down_weight, down_bias)]
    gradients = unpack(info, [mine, other, second], shapes)
    return (outputs, join_second(info, half, dxb), *gradients)


def solution(mesh):
    cells = P("wide", "section", None, None)
    return jax.shard_map(
        on_device,
        mesh=mesh,
        in_specs=(cells, P(), P(), P(), P(), P(), P(), P(), P(), cells),
        out_specs=(cells, cells, P(), P(), P(), P(), P(), P(), P(), P()),
        check_vma=False,
    )
```
